128 devices in a mesh: seq: 8 (over y, x_lo), tok: 16 (over x_hi, z, core).
Axes of the slice: x: 4 (x_hi: 2, x_lo: 2; x = x_hi * 2 + x_lo), y: 4, z: 4, core: 2. Of those that a mesh axis runs over, the one named last changes fastest.
Arguments:
- tokens: bfloat16 [24576, 1024], P(('seq', 'tok')), may hold values from -6 to 6
- cotangent: bfloat16 [24576, 1024], P(('seq', 'tok')), may hold values from -6 to 6
- doc_lengths: int32 [8, 4], P('seq'), may hold values from 1 to 3069, as said below
- pad_counts: int32 [8], P('seq'), may hold values from 0 to 96, as said below
- w_query: bfloat16 [1024, 1024], P(('seq', 'tok')), may hold values from -0.25 to 0.25
- b_query: bfloat16 [1024], P(('seq', 'tok')), may hold values from -3 to 3
- w_key: bfloat16 [1024, 1024], P(('seq', 'tok')), may hold values from -0.25 to 0.25
- w_value: bfloat16 [1024, 1024], P(('seq', 'tok')), may hold values from -0.1875 to 0.1875
- b_value: bfloat16 [1024], P(('seq', 'tok')), may hold values from -3 to 3
- w_out: bfloat16 [1024, 1024], P(('seq', 'tok')), may hold values from -0.375 to 0.375
- b_out: bfloat16 [1024], P(('seq', 'tok')), may hold values from -3 to 3
- gain_attn: bfloat16 [1024], P(('seq', 'tok')), may hold values from 0.5 to 1.5
- shift_attn: bfloat16 [1024], P(('seq', 'tok')), may hold values from -3 to 3
- w_in: bfloat16 [1024, 4096], P(('seq', 'tok')), may hold values from -0.1875 to 0.1875
- b_in: bfloat16 [4096], P(('seq', 'tok')), may hold values from -3 to 3
- w_back: bfloat16 [4096, 1024], P(('seq', 'tok')), may hold values from -0.09375 to 0.09375
- b_back: bfloat16 [1024], P(('seq', 'tok')), may hold values from -3 to 3
- gain_ffn: bfloat16 [1024], P(('seq', 'tok')), may hold values from 0.5 to 1.5
- shift_ffn: bfloat16 [1024], P(('seq', 'tok')), may hold values from -3 to 3
Outputs:
- output: bfloat16 [24576, 1024], P(('seq', 'tok'))
- tokens_grad: bfloat16 [24576, 1024], P(('seq', 'tok'))
- grad_w_query: float32 [1024, 1024], P(('seq', 'tok'))
- grad_b_query: float32 [1024], P(('seq', 'tok'))
- grad_w_key: float32 [1024, 1024], P(('seq', 'tok'))
- grad_w_value: float32 [1024, 1024], P(('seq', 'tok'))
- grad_b_value: float32 [1024], P(('seq', 'tok'))
- grad_w_out: float32 [1024, 1024], P(('seq', 'tok'))
- grad_b_out: float32 [1024], P(('seq', 'tok'))
- grad_gain_attn: float32 [1024], P(('seq', 'tok'))
- grad_shift_attn: float32 [1024], P(('seq', 'tok'))
- grad_w_in: float32 [1024, 4096], P(('seq', 'tok'))
- grad_b_in: float32 [4096], P(('seq', 'tok'))
- grad_w_back: float32 [4096, 1024], P(('seq', 'tok'))
- grad_b_back: float32 [1024], P(('seq', 'tok'))
- grad_gain_ffn: float32 [1024], P(('seq', 'tok'))
- grad_shift_ffn: float32 [1024], P(('seq', 'tok'))
The draws below stay inside these ranges and needn't reach their ends.
Inputs may be any that keep to these rules, and one draw needn't show every extreme that they name: `doc_lengths`: each row sums to 3072. Of each row one document starts within the first 192 positions and ends within the last 192; the other documents have at most 24 tokens. `pad_counts`: some sequence has 96 padding positions and another none.
All inputs are finite; a program needn't handle non-finite values.
Results may differ from the reference program's by a relative error of at most 0.03.
Values may be sent and summed in bfloat16 or wider, within the bound.
A program may use at most 256 MiB of HBM per device.

```python
import math
import jax
import jax.numpy as jnp
from jax import lax

D = 1024
HEADS = 16
FF = 4096
WINDOW = 1024
DOCS = 4
HEAD = 64
LENGTH = 3072
SEQS = 8
TOKENS = 24576
PAD_MOST = 96
SHORT_MOST = 24


def documents(key):
    splits = jax.random.split(key, 4)
    padding = jax.random.randint(splits[0], (SEQS,), 0, PAD_MOST + 1)
    chosen = jax.random.randint(splits[1], (), 0, SEQS)
    seq_index = jnp.arange(SEQS)
    padding = jnp.where(seq_index == chosen, PAD_MOST, padding)
    padding = jnp.where(seq_index == (chosen + 1) % SEQS, 0, padding)
    shorts = jax.random.randint(splits[2], (SEQS, DOCS - 1), 1, SHORT_MOST + 1)
    shorts = jnp.where(seq_index[:, None] == chosen, 1, shorts)
    long_at = jax.random.randint(splits[3], (SEQS, 1), 0, DOCS)
    doc_slot = jnp.arange(DOCS)[None, :]
    earlier = jnp.concatenate([shorts, shorts[:, :1]], axis=1)
    later_docs = jnp.concatenate([shorts[:, :1], shorts], axis=1)
    longest = LENGTH - jnp.sum(shorts, axis=1, keepdims=True)
    lengths = jnp.where(doc_slot < long_at, earlier, jnp.where(doc_slot == long_at, longest, later_docs))
    return (lengths.astype(jnp.int32), padding.astype(jnp.int32))


def draw_doc_lengths(key, part):
    return documents(key)[0]


def draw_pad_counts(key, part):
    return documents(key)[1]


def levels(rng, shape, shards, smallest, largest):
    def one(position, shards_of):
        draws = jax.random.uniform(jax.random.fold_in(jax.random.fold_in(rng, 6), position), (shards_of,), jnp.float32, smallest / len(shards), largest / len(shards))
        return jnp.repeat(jnp.exp(draws), shape[position] // shards_of).reshape((-1,) + (1,) * (len(shape) - position - 1))

    gain = one(*shards[0])
    for cut in shards[1:]:
        gain = gain * one(*cut)
    return gain


def noise(rng, extent, spread, reach, cuts=(), kind=jnp.bfloat16):
    values = spread * jax.random.normal(rng, extent, jnp.float32)
    if cuts:
        values = values * levels(rng, extent, cuts, -0.22, 0.18)
    return jnp.clip(values, -reach, reach).astype(kind)


def setup_inputs(seed: int = 0) -> dict:
    key_of = jax.random.split(jax.random.key(seed), 20)
    tokens = noise(key_of[0], (TOKENS, D), 1.0, 6.0, ((0, 128),))
    cotangent = noise(key_of[1], (TOKENS, D), 1.0, 6.0, ((0, 128),))
    doc_lengths = draw_doc_lengths(jax.random.fold_in(key_of[19], 71), 0)
    pad_counts = draw_pad_counts(jax.random.fold_in(key_of[19], 71), 0)
    w_query = noise(key_of[4], (D, D), (D // 2) ** -0.5, 0.25, ((0, 128),))
    b_query = noise(key_of[5], (D,), 0.5, 3.0, ((0, 128),))
    w_key = noise(key_of[6], (D, D), (D // 2) ** -0.5, 0.25, ((0, 128),))
    w_value = noise(key_of[7], (D, D), D ** -0.5, 0.1875, ((0, 128),))
    b_value = noise(key_of[8], (D,), 0.5, 3.0, ((0, 128),))
    w_out = noise(key_of[9], (D, D), (D // 4) ** -0.5, 0.375, ((0, 128),))
    b_out = noise(key_of[10], (D,), 0.5, 3.0, ((0, 128),))
    gain_attn = jnp.clip(1.0 + 0.1 * jax.random.normal(key_of[11], (D,), jnp.float32), 0.5, 1.5).astype(jnp.bfloat16)
    shift_attn = noise(key_of[12], (D,), 0.5, 3.0, ((0, 128),))
    w_in = noise(key_of[13], (D, FF), D ** -0.5, 0.1875, ((0, 128),))
    b_in = noise(key_of[14], (FF,), 0.5, 3.0, ((0, 128),))
    w_back = noise(key_of[15], (FF, D), FF ** -0.5, 0.09375, ((0, 128),))
    b_back = noise(key_of[16], (D,), 0.5, 3.0, ((0, 128),))
    gain_ffn = jnp.clip(1.0 + 0.1 * jax.random.normal(key_of[17], (D,), jnp.float32), 0.5, 1.5).astype(jnp.bfloat16)
    shift_ffn = noise(key_of[18], (D,), 0.5, 3.0, ((0, 128),))
    return dict(tokens=tokens, cotangent=cotangent, doc_lengths=doc_lengths, pad_counts=pad_counts, w_query=w_query, b_query=b_query, w_key=w_key, w_value=w_value, b_value=b_value, w_out=w_out, b_out=b_out, gain_attn=gain_attn, shift_attn=shift_attn, w_in=w_in, b_in=b_in, w_back=w_back, b_back=b_back, gain_ffn=gain_ffn, shift_ffn=shift_ffn)


@jax.custom_vjp
def low(v):
    return lax.optimization_barrier(v.astype(jnp.bfloat16)).astype(jnp.float32)

@jax.custom_vjp
def low_back(v):
    return v

def low_keep(v):
    return (low(v), None)

def low_pass(kept, grad):
    return (grad,)

def back_keep(v):
    return (v, None)

def back_low(kept, grad):
    return (low(grad),)
low.defvjp(low_keep, low_pass)
low_back.defvjp(back_keep, back_low)
EPSILON = 1e-05
MASKED = -1e+30

def product(former, latter):
    return jnp.dot(former, latter, precision=lax.Precision.HIGHEST)

def normalize(tensor, norm_gain, norm_shift):
    centred = tensor - lax.optimization_barrier(jnp.mean(tensor, axis=-1, keepdims=True))
    factor = lax.rsqrt(lax.optimization_barrier(jnp.mean(centred * centred, axis=-1, keepdims=True)) + EPSILON)
    return centred * factor * norm_gain + norm_shift

def segment_ids(length_row, pad_count):
    doc_ends = jnp.cumsum(length_row).astype(jnp.int32)
    places = jnp.arange(LENGTH, dtype=jnp.int32)
    inside = lax.optimization_barrier(jnp.sum((places[:, None] >= doc_ends[None, :]).astype(jnp.int32), axis=1))
    return jnp.where(places >= LENGTH - pad_count, DOCS, inside).astype(jnp.int32)

def attend(queries, keys, values, segment):
    block_rows = min(512, LENGTH)
    key_heads = keys.reshape(LENGTH, HEADS, HEAD)
    value_heads = values.reshape(LENGTH, HEADS, HEAD)
    places = jnp.arange(LENGTH, dtype=jnp.int32)

    def one_block(first_row):
        query_heads = lax.dynamic_slice_in_dim(queries, first_row, block_rows, 0).reshape(block_rows, HEADS, HEAD)
        row_segment = lax.dynamic_slice_in_dim(segment, first_row, block_rows, 0)
        row_places = first_row + jnp.arange(block_rows, dtype=jnp.int32)
        scores = jnp.einsum('qhd,khd->hqk', query_heads, key_heads, precision=lax.Precision.HIGHEST) * (1.0 / math.sqrt(HEAD))
        scores = low_back(scores)
        allowed = (row_segment[:, None] == segment[None, :]) & (jnp.abs(row_places[:, None] - places[None, :]) < WINDOW // 2)
        scores = jnp.where(allowed[None], scores, MASKED)
        weights = low(jax.nn.softmax(scores, axis=-1))
        mixed = jnp.einsum('hqk,khd->qhd', weights, value_heads, precision=lax.Precision.HIGHEST)
        return mixed.reshape(block_rows, D)
    starts = jnp.arange(0, LENGTH, block_rows, dtype=jnp.int32)
    return lax.map(jax.checkpoint(one_block), starts).reshape(LENGTH, D)

def layer(hidden, params, segment):
    w_query, b_query, w_key, w_value, b_value, w_out, b_out, gain_attn, shift_attn, w_in, b_in, w_back, b_back, gain_ffn, shift_ffn = params
    entry = low(hidden)
    queries = low(low_back(product(entry, w_query) + b_query))
    keys = low(low_back(product(entry, w_key)))
    values = low(low_back(product(entry, w_value) + b_value))
    mixed = low(low_back(attend(queries, keys, values, segment)))
    branch = low_back(product(mixed, w_out) + b_out)
    first = normalize(hidden + branch, gain_attn, shift_attn)
    before = low_back(product(low(first), w_in) + b_in)
    active = low(jax.nn.gelu(before, approximate=True))
    second = low_back(product(active, w_back) + b_back)
    return normalize(first + second, gain_ffn, shift_ffn)

def reference(tokens, cotangent, doc_lengths, pad_counts, w_query, b_query, w_key, w_value, b_value, w_out, b_out, gain_attn, shift_attn, w_in, b_in, w_back, b_back, gain_ffn, shift_ffn):
    params = tuple((item.astype(jnp.float32) for item in (w_query, b_query, w_key, w_value, b_value, w_out, b_out, gain_attn, shift_attn, w_in, b_in, w_back, b_back, gain_ffn, shift_ffn)))
    seq_tokens = tokens.astype(jnp.float32).reshape(SEQS, LENGTH, D)
    seq_grads = cotangent.astype(jnp.float32).reshape(SEQS, LENGTH, D)

    def one_sequence(totals, items):
        entry_rows, grad_rows, length_row, pad_count = items
        segment = segment_ids(length_row, pad_count)

        def forward(hidden, *weights):
            return layer(layer(hidden, weights, segment), weights, segment)
        result, pullback = jax.vjp(forward, entry_rows, *params)
        gradients = pullback(grad_rows)
        totals = tuple((older + newer for older, newer in zip(totals, gradients[1:])))
        return (totals, (result.astype(jnp.bfloat16), gradients[0].astype(jnp.bfloat16)))
    zeros = tuple((jnp.zeros(item.shape, jnp.float32) for item in params))
    totals, (results, entry_grads) = lax.scan(one_sequence, zeros, (seq_tokens, seq_grads, doc_lengths, pad_counts))
    return (results.reshape(TOKENS, D), entry_grads.reshape(TOKENS, D), totals[0], totals[1], totals[2], totals[3], totals[4], totals[5], totals[6], totals[7], totals[8], totals[9], totals[10], totals[11], totals[12], totals[13], totals[14])
```

```python
import functools
import math

import jax
import jax.numpy as jnp
from jax import lax
from jax.experimental import pallas as pl
from jax.experimental.pallas import tpu as pltpu
from jax.sharding import PartitionSpec as P

HEADS = 16
WINDOW = 1024
D = 1024
FF = 4096
HEAD = 64
CHIPS = 8
ROWS = 192
CHIP_ROWS = 2 * ROWS
LENGTH = CHIP_ROWS * CHIPS
HALF = 512
EPSILON = 1e-05
MASKED = -1e30
SCALE = 1.0 / math.sqrt(HEAD)
LOG2E = 1.4426950408889634
MESH = pl.DeviceIdType.MESH
BF = jnp.bfloat16
F32 = jnp.float32
CUBE = (4, 2, 2, 4)


def bfloat(tensor):
    return tensor.astype(BF)


def widen(tensor):
    return tensor.astype(F32)


def place():
    seq, tok = lax.axis_index("seq"), lax.axis_index("tok")
    x = (tok // 8) * 2 + seq % 2
    return {"x": x, "y": seq // 2, "z": (tok // 2) % 4, "core": tok % 2}


def device(x, y, z, core):
    return (y * 2 + x % 2, (x // 2) * 8 + z * 2 + core)


def moved(here, axis, steps):
    there = dict(here)
    there[axis] = lax.rem(here[axis] + steps + 4, 4)
    return device(**there)


def partner(here):
    return device(here["x"], here["y"], here["z"], 1 - here["core"])


def cube_index(here, whole, axis, value):
    index = []
    for name in ("y", "x", "z"):
        if name in whole:
            index += [slice(None)] * (2 if name == "x" else 1)
        else:
            at = value if name == axis else here[name]
            index += [at % 2, at // 2] if name == "x" else [at]
    return tuple(index)


def greet(targets):
    barrier = pltpu.get_barrier_semaphore()
    for target in targets:
        pl.semaphore_signal(barrier, inc=1, device_id=target, device_id_type=MESH)
    pl.semaphore_wait(barrier, len(targets))


def neighbours(here):
    return [moved(here, axis, step) for axis in ("x", "y", "z") for step in (1, -1)] + [
        partner(here)
    ]


def remote(source, target, sems, number, to):
    return pltpu.make_async_remote_copy(
        src_ref=source,
        dst_ref=target,
        send_sem=sems[0].at[number],
        recv_sem=sems[1].at[number],
        device_id=to,
        device_id_type=MESH,
    )


GATHER_ORDERS = (("x", "y", "z"), ("z", "x", "y"), ("y", "z", "x"), ("x", "y", "z"))


def gather_kernel(
    pack, small, ga, gb, gc, gs, wo, wb, theirs, small_theirs, stage, small_stage, send, recv, local
):
    here = place()
    core = here["core"]
    other = partner(here)
    sems = (send, recv)
    greet(neighbours(here))
    first = remote(pack.at[1 - core], theirs, sems, 0, other)
    second = remote(small, small_theirs, sems, 1, other)
    first.start()
    second.start()
    first.wait()
    second.wait()

    def build(low, high):
        low, high = widen(low), widen(high)
        for piece in range(8):
            rows = slice(8 * piece, 8 * piece + 8)
            both = bfloat(jnp.concatenate([low[rows], high[rows]], axis=0))
            stage[piece // 4, (piece % 4) * 16 : (piece % 4) * 16 + 16, :] = both
        stage[2, 0:32, :] = bfloat(low[64:96])
        stage[2, 32:64, :] = bfloat(high[64:96])

    @pl.when(core == 0)
    def _():
        build(pack[0], theirs[...])

    @pl.when(core == 1)
    def _():
        build(theirs[...], pack[1])

    small_stage[...] = small[...] + small_theirs[...]
    whole = (ga, gb, gc, gs)
    own = cube_index(here, (), None, None)
    kept = []
    for part in range(4):
        source = small_stage if part == 3 else stage.at[part]
        copy = pltpu.make_async_copy(source, whole[part].at[own], local.at[part])
        copy.start()
        kept.append(copy)

    number = 2
    sent = []
    for phase in range(3):
        one, two = [], []
        for part in range(4):
            axis = GATHER_ORDERS[part][phase]
            done = GATHER_ORDERS[part][:phase]
            index = cube_index(here, done, axis, here[axis])
            if phase == 0:
                source = small_stage if part == 3 else stage.at[part]
            else:
                source = whole[part].at[index]
            pair = []
            for step in (1, -1):
                copy = remote(source, whole[part].at[index], sems, number, moved(here, axis, step))
                number += 1
                copy.start()
                pair.append(copy)
            one.append(pair)
            sent += pair
        for part in range(4):
            axis = GATHER_ORDERS[part][phase]
            done = GATHER_ORDERS[part][:phase]
            for side, step in enumerate((1, -1)):
                one[part][side].wait_recv()
                if part == 3 and side == 1:
                    continue
                come = lax.rem(here[axis] - step + 4, 4)
                index = cube_index(here, done, axis, come)
                block = whole[part].at[index]
                if part < 3:
                    rows = pl.ds(32 * side, 32)
                    block = whole[part].at[index + (rows,)]
                copy = remote(block, block, sems, number, moved(here, axis, step))
                number += 1
                copy.start()
                two.append(copy)
        for copy in two:
            copy.wait_recv()
        sent += two
        if phase == 0:
            for copy in kept:
                copy.wait()

    mine, yours = pl.ds(2 * core, 2), pl.ds(2 * (1 - core), 2)
    out_rows = pl.ds(48, 16)
    every = slice(None)
    last = [
        remote(gc.at[yours], wb.at[core], sems, number, other),
        remote(ga.at[yours, every, every, every, out_rows], wo.at[core], sems, number + 1, other),
    ]
    for copy in last:
        copy.start()
    kept = [
        pltpu.make_async_copy(gc.at[mine], wb.at[core], local.at[4]),
        pltpu.make_async_copy(
            ga.at[mine, every, every, every, out_rows], wo.at[core], local.at[5]
        ),
    ]
    for copy in kept:
        copy.start()
    for copy in kept + last:
        copy.wait()
    for copy in sent:
        copy.wait_send()


GATHER_COPIES = 2 + 3 * (8 + 7) + 2


def gather_weights(pack, small):
    any_space = pl.BlockSpec(memory_space=pl.ANY)
    vmem = pl.BlockSpec(memory_space=pltpu.VMEM)
    big = jax.ShapeDtypeStruct(CUBE + (64, HALF), BF)
    return pl.pallas_call(
        gather_kernel,
        out_shape=(
            big,
            big,
            big,
            jax.ShapeDtypeStruct(CUBE + (16, 128), BF),
            jax.ShapeDtypeStruct((2, 2, 2, 2, 4, 16, HALF), BF),
            jax.ShapeDtypeStruct((2, 2, 2, 2, 4, 64, HALF), BF),
        ),
        in_specs=[vmem, vmem],
        out_specs=(any_space,) * 6,
        scratch_shapes=[
            pltpu.VMEM((96, HALF), BF),
            pltpu.VMEM((16, 128), BF),
            pltpu.VMEM((3, 64, HALF), BF),
            pltpu.VMEM((16, 128), BF),
            pltpu.SemaphoreType.DMA((GATHER_COPIES,)),
            pltpu.SemaphoreType.DMA((GATHER_COPIES,)),
            pltpu.SemaphoreType.DMA((6,)),
        ],
        name="gather_weights",
        compiler_params=pltpu.CompilerParams(collective_id=0, has_side_effects=True),
    )(pack, small)


SCATTER_ORDERS = (("z", "y", "x"), ("y", "x", "z"), ("x", "z", "y"), ("z", "y", "x"))
SIZES = {"y": (4,), "x": (2, 2), "z": (4,)}


def lengths_of(full):
    return tuple(n for name in ("y", "x", "z") if name in full for n in SIZES[name])


def digits_of(i, lengths):
    digits = []
    for length in reversed(lengths):
        digits.append(lax.rem(i, length))
        i = lax.div(i, length)
    return tuple(digits[::-1])


def one_chip(here, full, axis, value, digits):
    digits, index = list(digits), []
    for name in ("y", "x", "z"):
        if name in full:
            index += [digits.pop(0) for _ in SIZES[name]]
        else:
            at = value if name == axis else here[name]
            index += [at % 2, at // 2] if name == "x" else [at]
    return tuple(index)


def scatter_kernel(
    da, do, db, dc, ds,
    o_query, o_key, o_value, o_out, o_in, o_back, o_small,
    *scratch,
):
    whole, slots = scratch[:4], scratch[4:28]
    final, landed, small_out, send, recv, local = scratch[28:]
    wa, wb, wc, ws = whole
    here = place()
    core = here["core"]
    other = partner(here)
    sems = (send, recv)
    every = slice(None)
    mine = pl.ds(2 * core, 2)
    out_rows = pl.ds(48, 16)
    kept = [
        pltpu.make_async_copy(da, wa.at[every, every, every, every, pl.ds(0, 48)], local.at[0]),
        pltpu.make_async_copy(db, wb, local.at[1]),
        pltpu.make_async_copy(dc.at[core], wc.at[mine], local.at[2]),
        pltpu.make_async_copy(do.at[core], wa.at[mine, every, every, every, out_rows], local.at[3]),
        pltpu.make_async_copy(ds, ws, local.at[4]),
    ]
    for copy in kept:
        copy.start()
    greet(neighbours(here))
    swaps = [
        remote(do.at[1 - core], wa.at[mine, every, every, every, out_rows], sems, 0, other),
        remote(dc.at[1 - core], wc.at[mine], sems, 1, other),
    ]
    for copy in swaps:
        copy.start()
    for copy in kept:
        copy.wait()
    for copy in swaps:
        copy.wait()

    number = 2
    sent = []
    for phase in range(3):
        ahead, arriving = {}, {}
        for part in range(4):
            axis, full = SCATTER_ORDERS[part][phase], SCATTER_ORDERS[part][phase + 1 :]
            far = cube_index(here, full, axis, lax.rem(here[axis] + 2, 4))
            for side, step in enumerate((1, -1)):
                if part == 3 and side == 1:
                    continue
                rows = () if part == 3 else (pl.ds(32 * side, 32),)
                copy = ahead[part, side] = remote(
                    whole[part].at[far + rows],
                    slots[part * 6 + phase * 2].at[side],
                    sems,
                    number,
                    moved(here, axis, step),
                )
                number += 1
                copy.start()
                sent.append(copy)
        for part in range(4):
            axis, full = SCATTER_ORDERS[part][phase], SCATTER_ORDERS[part][phase + 1 :]
            lengths = lengths_of(full)
            half, whole_slot = slots[part * 6 + phase * 2 : part * 6 + phase * 2 + 2]
            for side, step in enumerate((1, -1)):
                value = lax.rem(here[axis] + step + 4, 4)
                if not (part == 3 and side == 1):
                    ahead[part, side].wait_recv()
                    rows = (every,) if part == 3 else (pl.ds(32 * side, 32),)

                    def add(i, _, part=part, side=side, half=half, value=value, rows=rows):
                        digits = digits_of(i, lengths_of(SCATTER_ORDERS[part][phase + 1 :]))
                        at = one_chip(
                            here,
                            SCATTER_ORDERS[part][phase + 1 :],
                            SCATTER_ORDERS[part][phase],
                            value,
                            digits,
                        )
                        ref = whole[part]
                        ref[at + rows] = bfloat(
                            widen(ref[at + rows]) + widen(half[(side,) + digits])
                        )
                        return 0

                    lax.fori_loop(0, math.prod(lengths), add, 0)
                copy = arriving[part, side] = remote(
                    whole[part].at[cube_index(here, full, axis, value)],
                    whole_slot.at[side],
                    sems,
                    number,
                    moved(here, axis, step),
                )
                number += 1
                copy.start()
                sent.append(copy)
        for part in range(4):
            axis, full = SCATTER_ORDERS[part][phase], SCATTER_ORDERS[part][phase + 1 :]
            lengths = lengths_of(full)
            whole_slot = slots[part * 6 + phase * 2 + 1]
            arriving[part, 0].wait_recv()
            arriving[part, 1].wait_recv()

            def total(i, _, part=part, whole_slot=whole_slot, axis=axis, full=full):
                digits = digits_of(i, lengths_of(full))
                at = one_chip(here, full, axis, here[axis], digits)
                ref = whole[part]
                value = (
                    widen(ref[at])
                    + widen(whole_slot[(0,) + digits])
                    + widen(whole_slot[(1,) + digits])
                )
                if phase < 2:
                    ref[at] = bfloat(value)
                elif part == 3:
                    small_out[...] = value
                else:
                    final[part] = value
                return 0

            lax.fori_loop(0, math.prod(lengths), total, 0)

    o_small[...] = small_out[...]

    def finish(own):
        rows = []
        for piece in range(8):
            part, low = piece // 4, (piece % 4) * 16 + 8 * own
            rows.append(final[part, low : low + 8, :])
        rows.append(final[2, 32 * own : 32 * own + 32, :])
        return jnp.concatenate(rows, axis=0)

    @pl.when(core == 0)
    def _():
        landed[2] = finish(1)
        landed[0] = finish(0)

    @pl.when(core == 1)
    def _():
        landed[2] = finish(0)
        landed[1] = finish(1)

    last = remote(landed.at[2], landed.at[core], sems, number, other)
    last.start()
    last.wait()
    for column in (0, 1):
        span = slice(column * HALF, column * HALF + HALF)
        for piece, ref in enumerate((o_query, o_key, o_value, o_out)):
            ref[:, span] = landed[column, 8 * piece : 8 * piece + 8, :]
        for chunk in range(4):
            low = column * 2048 + chunk * HALF
            o_in[:, low : low + HALF] = landed[column, 32 + 8 * chunk : 40 + 8 * chunk, :]
        o_back[:, span] = landed[column, 64:96, :]
    for copy in sent:
        copy.wait_send()


SCATTER_COPIES = 2 + 3 * (7 + 8) + 1


def scatter_gradients(da, do, db, dc, ds):
    any_space = pl.BlockSpec(memory_space=pl.ANY)
    vmem = pl.BlockSpec(memory_space=pltpu.VMEM)
    slots = []
    for part in range(4):
        for phase in range(3):
            dims = lengths_of(SCATTER_ORDERS[part][phase + 1 :])
            ends = ((16, 128), (16, 128)) if part == 3 else ((32, HALF), (64, HALF))
            slots += [pltpu.VMEM((2,) + dims + end, BF) for end in ends]
    return pl.pallas_call(
        scatter_kernel,
        out_shape=(
            jax.ShapeDtypeStruct((8, D), F32),
            jax.ShapeDtypeStruct((8, D), F32),
            jax.ShapeDtypeStruct((8, D), F32),
            jax.ShapeDtypeStruct((8, D), F32),
            jax.ShapeDtypeStruct((8, FF), F32),
            jax.ShapeDtypeStruct((32, D), F32),
            jax.ShapeDtypeStruct((16, 128), F32),
        ),
        in_specs=[any_space] * 5,
        out_specs=(vmem,) * 7,
        scratch_shapes=[
            pltpu.VMEM(CUBE + (64, HALF), BF),
            pltpu.VMEM(CUBE + (64, HALF), BF),
            pltpu.VMEM(CUBE + (64, HALF), BF),
            pltpu.VMEM(CUBE + (16, 128), BF),
        ]
        + slots
        + [
            pltpu.VMEM((3, 64, HALF), F32),
            pltpu.VMEM((3, 96, HALF), F32),
            pltpu.VMEM((16, 128), F32),
            pltpu.SemaphoreType.DMA((SCATTER_COPIES,)),
            pltpu.SemaphoreType.DMA((SCATTER_COPIES,)),
            pltpu.SemaphoreType.DMA((5,)),
        ],
        name="scatter_gradients",
        compiler_params=pltpu.CompilerParams(
            collective_id=1, has_side_effects=True, vmem_limit_bytes=60 * 2**20
        ),
    )(da, do, db, dc, ds)


def group_device(here, number):
    seq = lax.axis_index("seq")
    return (seq, (number // 4) * 8 + (number % 4) * 2 + here["core"])


def exchange_kernel(outward, value, result, send, recv, local):
    here = place()
    me = (here["x"] // 2) * 4 + here["z"]
    targets = [group_device(here, lax.rem(me + k, CHIPS)) for k in range(1, CHIPS)]
    greet(targets)

    def spot(ref, number, grouped):
        if grouped:
            return ref.at[:, number]
        start = pl.multiple_of(number * CHIP_ROWS, CHIP_ROWS)
        return ref.at[:, :, pl.ds(start, CHIP_ROWS)]

    copies = []
    for k in range(1, CHIPS):
        to = lax.rem(me + k, CHIPS)
        copies.append(
            remote(
                spot(value, to, outward),
                spot(result, me, not outward),
                (send, recv),
                k - 1,
                group_device(here, to),
            )
        )
    for copy in copies:
        copy.start()
    own = pltpu.make_async_copy(
        spot(value, me, outward), spot(result, me, not outward), local.at[0]
    )
    own.start()
    own.wait()
    for copy in copies:
        copy.wait()


def exchange(value, outward, number):
    count = value.shape[0]
    grouped, flat = (count, CHIPS, HEAD, CHIP_ROWS), (count, HEAD, LENGTH)
    vmem = pl.BlockSpec(memory_space=pltpu.VMEM)
    return pl.pallas_call(
        functools.partial(exchange_kernel, outward),
        out_shape=jax.ShapeDtypeStruct(flat if outward else grouped, BF),
        in_specs=[vmem],
        out_specs=vmem,
        scratch_shapes=[
            pltpu.SemaphoreType.DMA((CHIPS - 1,)),
            pltpu.SemaphoreType.DMA((CHIPS - 1,)),
            pltpu.SemaphoreType.DMA((1,)),
        ],
        name="exchange_%d" % number,
        compiler_params=pltpu.CompilerParams(
            collective_id=number, has_side_effects=True, vmem_limit_bytes=40 * 2**20
        ),
    )(value)


BLOCK = 256
SPAN = 1280
STEPS = LENGTH // BLOCK


def limits(bounds, first, count):
    places = first + lax.broadcasted_iota(jnp.int32, (1, count), 1)
    low = jnp.maximum(places - (WINDOW // 2 - 1), 0)
    high = jnp.minimum(places + WINDOW // 2, LENGTH)
    for k in range(4):
        bound = bounds[k]
        low = jnp.maximum(low, jnp.where(bound <= places, bound, 0))
        high = jnp.minimum(high, jnp.where(bound > places, bound, LENGTH))
    return low, high


def dot(former, latter):
    return jnp.dot(former, latter, preferred_element_type=F32)


def block_scores(bounds, qkv, kv, i):
    first = pl.multiple_of(i * BLOCK, BLOCK)
    start = pl.multiple_of(jnp.clip(first - 512, 0, LENGTH - SPAN), BLOCK)
    queries = qkv[0, :, pl.ds(first, BLOCK)]
    padded = jnp.concatenate([queries, jnp.zeros_like(queries)], axis=0)
    keys = kv[pl.ds(start, SPAN), :]
    scores = dot(keys, padded)
    low, high = limits(bounds, first, BLOCK)
    places = start + lax.broadcasted_iota(jnp.int32, (SPAN, BLOCK), 0)
    allowed = (places >= low) & (places < high)
    return first, start, queries, keys, jnp.where(allowed, scores, MASKED)


def attend_kernel(bounds, qkv, mixed, logsum, kv, kv_t):
    kv_t[...] = jnp.concatenate([qkv[1], qkv[2]], axis=0)
    kv[...] = kv_t[...].T

    def step(i, _):
        first, start, _, _, scores = block_scores(bounds, qkv, kv, i)
        highest = jnp.max(scores, axis=0, keepdims=True)
        chances = jnp.exp2((scores - highest) * (SCALE * LOG2E))
        totals = jnp.sum(chances, axis=0, keepdims=True)
        out = dot(kv_t[:, pl.ds(start, SPAN)], bfloat(chances))
        mixed[:, pl.ds(first, BLOCK)] = bfloat(out[HEAD:] / totals)
        logsum[:, pl.ds(first, BLOCK)] = highest * (SCALE * LOG2E) + jnp.log2(totals)
        return 0

    lax.fori_loop(0, STEPS, step, 0)


def attend(bounds, qkv):
    vmem = pl.BlockSpec(memory_space=pltpu.VMEM)
    return pl.pallas_call(
        attend_kernel,
        out_shape=(
            jax.ShapeDtypeStruct((HEAD, LENGTH), BF),
            jax.ShapeDtypeStruct((1, LENGTH), F32),
        ),
        in_specs=[pl.BlockSpec(memory_space=pltpu.SMEM), vmem],
        out_specs=(vmem, vmem),
        scratch_shapes=[
            pltpu.VMEM((LENGTH, 2 * HEAD), BF),
            pltpu.VMEM((2 * HEAD, LENGTH), BF),
        ],
        name="attend",
        compiler_params=pltpu.CompilerParams(vmem_limit_bytes=50 * 2**20),
    )(bounds, qkv)


def attend_back_kernel(bounds, qkv, logsum, grad_mixed, grads, kv, kv_t, total):
    kv_t[...] = jnp.concatenate([qkv[1], qkv[2]], axis=0)
    kv[...] = kv_t[...].T
    total[...] = jnp.zeros_like(total)
    left = lax.broadcasted_iota(jnp.int32, (BLOCK, 2 * HEAD), 1) < HEAD

    def step(i, _):
        first, start, queries, keys, scores = block_scores(bounds, qkv, kv, i)
        grad = grad_mixed[:, pl.ds(first, BLOCK)]
        chances = jnp.exp2(scores * (SCALE * LOG2E) - logsum[:, pl.ds(first, BLOCK)])
        grad_weights = dot(keys, jnp.concatenate([jnp.zeros_like(grad), grad], axis=0))
        inner = jnp.sum(chances * grad_weights, axis=0, keepdims=True)
        grad_scores = bfloat(chances * (grad_weights - inner))
        weights = bfloat(chances)
        grad_queries = dot(kv_t[:, pl.ds(start, SPAN)], grad_scores)
        grads[0, :, pl.ds(first, BLOCK)] = bfloat(grad_queries[:HEAD] * SCALE)
        both = jnp.concatenate([queries, grad], axis=0).T
        none = jnp.zeros_like(both)
        total[pl.ds(start, SPAN), :] += dot(weights, jnp.where(left, none, both)) + dot(
            grad_scores, jnp.where(left, both, none)
        )
        return 0

    lax.fori_loop(0, STEPS, step, 0)

    def last(i, _):
        first = pl.multiple_of(i * BLOCK, BLOCK)
        turned = total[pl.ds(first, BLOCK), :].T
        grads[1, :, pl.ds(first, BLOCK)] = bfloat(turned[:HEAD] * SCALE)
        grads[2, :, pl.ds(first, BLOCK)] = bfloat(turned[HEAD:])
        return 0

    lax.fori_loop(0, STEPS, last, 0)


def attend_back(bounds, qkv, logsum, grad_mixed):
    vmem = pl.BlockSpec(memory_space=pltpu.VMEM)
    return pl.pallas_call(
        attend_back_kernel,
        out_shape=jax.ShapeDtypeStruct((3, HEAD, LENGTH), BF),
        in_specs=[pl.BlockSpec(memory_space=pltpu.SMEM), vmem, vmem, vmem],
        out_specs=vmem,
        scratch_shapes=[
            pltpu.VMEM((LENGTH, 2 * HEAD), BF),
            pltpu.VMEM((2 * HEAD, LENGTH), BF),
            pltpu.VMEM((LENGTH, 2 * HEAD), F32),
        ],
        name="attend_back",
        compiler_params=pltpu.CompilerParams(vmem_limit_bytes=50 * 2**20),
    )(bounds, qkv, logsum, grad_mixed)


def product(former, latter):
    return jnp.dot(former, latter, preferred_element_type=F32)


def product_tn(former, latter):
    return lax.dot_general(former, latter, (((0,), (0,)), ((), ())), preferred_element_type=F32)


def product_nt(former, latter):
    return lax.dot_general(former, latter, (((1,), (1,)), ((), ())), preferred_element_type=F32)


def smooth(tensor):
    return jax.nn.gelu(tensor, approximate=True)


def swap(value):
    return lax.ppermute(value, "tok", [(t, t ^ 1) for t in range(16)])


def both_cores(core, value):
    other = swap(value)
    return jnp.where(
        core == 0,
        jnp.concatenate([value, other], axis=0),
        jnp.concatenate([other, value], axis=0),
    )


def own_rows(core, partial):
    mine = lax.dynamic_slice_in_dim(partial, core * ROWS, ROWS, 0)
    yours = lax.dynamic_slice_in_dim(partial, (1 - core) * ROWS, ROWS, 0)
    return mine + swap(yours)


def normalize(tensor, norm_gain, norm_shift):
    centred = tensor - jnp.mean(tensor, axis=-1, keepdims=True)
    factor = lax.rsqrt(jnp.mean(centred * centred, axis=-1, keepdims=True) + EPSILON)
    normed = centred * factor
    return (normed * norm_gain + norm_shift, normed, factor)


def normalize_back(grad_out, normed, factor, norm_gain):
    grad_normed = grad_out * norm_gain
    grad_input = factor * (
        grad_normed
        - jnp.mean(grad_normed, axis=-1, keepdims=True)
        - normed * jnp.mean(grad_normed * normed, axis=-1, keepdims=True)
    )
    return (grad_input, jnp.sum(grad_out * normed, axis=0), jnp.sum(grad_out, axis=0))


def layer_forward(hidden, w, core, bounds, number):
    entry = both_cores(core, bfloat(hidden))
    queries = bfloat(product(entry, w["query"]) + w["b_query"])
    keys = bfloat(product(entry, w["key"]))
    values = bfloat(product(entry, w["value"]) + w["b_value"])
    stacked = jnp.stack([queries.T, keys.T, values.T]).reshape(3, CHIPS, HEAD, CHIP_ROWS)
    qkv = exchange(stacked, True, number)
    mixed_head, logsum = attend(bounds, qkv)
    mixed = exchange(mixed_head[None], False, number + 1).reshape(HALF, CHIP_ROWS).T
    branch = own_rows(core, product(mixed, w["out"]))
    first, normed_one, factor_one = normalize(
        hidden + branch + w["b_out"], w["gain_attn"], w["shift_attn"]
    )
    entry_two = both_cores(core, bfloat(first))
    before = product(entry_two, w["in"]) + w["b_in"]
    active = bfloat(smooth(before))
    second = own_rows(core, product(active, w["back"]))
    result, normed_two, factor_two = normalize(
        first + second + w["b_back"], w["gain_ffn"], w["shift_ffn"]
    )
    saved = (
        entry, qkv, logsum, mixed, normed_one, factor_one, entry_two, before, active, normed_two,
        factor_two,
    )
    return result, saved


def layer_backward(grad_out, w, saved, core, bounds, number):
    (
        entry, qkv, logsum, mixed, normed_one, factor_one, entry_two, before, active, normed_two,
        factor_two,
    ) = saved
    d_second, g_gain_ffn, g_shift_ffn = normalize_back(
        grad_out, normed_two, factor_two, w["gain_ffn"]
    )
    d_branch = bfloat(d_second)
    g_b_back = jnp.sum(widen(d_branch), axis=0)
    d_branch = both_cores(core, d_branch)
    d_active = product_nt(d_branch, w["back"])
    d_before = bfloat(jax.vjp(smooth, before)[1](d_active)[0])
    g_b_in = jnp.sum(widen(d_before), axis=0)
    d_first = d_second + own_rows(core, product_nt(d_before, w["in"]))
    d_inner, g_gain_attn, g_shift_attn = normalize_back(
        d_first, normed_one, factor_one, w["gain_attn"]
    )
    d_attn = bfloat(d_inner)
    g_b_out = jnp.sum(widen(d_attn), axis=0)
    d_attn = both_cores(core, d_attn)
    d_mixed = bfloat(product_nt(d_attn, w["out"]))
    grad_head = exchange(d_mixed.T.reshape(1, CHIPS, HEAD, CHIP_ROWS), True, number)[0]
    d_qkv = exchange(attend_back(bounds, qkv, logsum, grad_head), False, number + 1)
    d_queries, d_keys, d_values = [d_qkv[k].reshape(HALF, CHIP_ROWS).T for k in range(3)]
    g_b_query = jnp.sum(widen(d_queries), axis=0)
    g_b_value = jnp.sum(widen(d_values), axis=0)
    d_hidden = d_inner + own_rows(
        core,
        product_nt(d_queries, w["query"])
        + product_nt(d_keys, w["key"])
        + product_nt(d_values, w["value"]),
    )
    vectors = (
        g_b_query, g_b_value, g_b_out, g_gain_attn, g_shift_attn, g_b_back, g_gain_ffn,
        g_shift_ffn, g_b_in,
    )
    pairs = (
        (entry, d_queries), (entry, d_keys), (entry, d_values), (mixed, d_attn),
        (entry_two, d_before), (active, d_branch),
    )
    return d_hidden, vectors, pairs


def on_device(
    tokens, cotangent, doc_lengths, pad_counts, w_query, b_query, w_key, w_value, b_value, w_out,
    b_out, gain_attn, shift_attn, w_in, b_in, w_back, b_back, gain_ffn, shift_ffn,
):
    tok = lax.axis_index("tok")
    core = tok % 2
    live = LENGTH - pad_counts[0]
    ends = jnp.cumsum(doc_lengths[0])
    bounds = jnp.minimum(ends, live).astype(jnp.int32)

    pack = jnp.stack(
        [
            jnp.concatenate(
                [w[:, HALF * half : HALF * half + HALF] for w in (w_query, w_key, w_value, w_out)]
                + [w_in[:, 2048 * half + HALF * k : 2048 * half + HALF * k + HALF] for k in range(4)]
                + [w_back[:, HALF * half : HALF * half + HALF]],
                axis=0,
            )
            for half in range(2)
        ]
    )
    eight = jnp.stack(
        [b_query, b_value, b_out, gain_attn, shift_attn, b_back, gain_ffn, shift_ffn]
    )
    small = lax.dynamic_update_slice(jnp.zeros((16, 128), BF), eight, (0, tok * 8))
    small = lax.dynamic_update_slice(small, b_in[None], (8 + tok // 4, (tok % 4) * 32))
    ga, gb, _, gs, wo, wb = gather_weights(pack, small)
    ga, gb = ga.reshape(64, 4, 16, HALF), gb.reshape(64, 4, 16, HALF)
    lines = jnp.sum(widen(gs.reshape(8, 8, 16, 128)), axis=1)
    vectors = [lines[:, k].reshape(D) for k in range(8)]

    def half_of(vector):
        return lax.dynamic_slice_in_dim(vector, core * (vector.shape[0] // 2), vector.shape[0] // 2)

    w = {
        "query": ga[:, 0].reshape(D, HALF),
        "key": ga[:, 1].reshape(D, HALF),
        "value": ga[:, 2].reshape(D, HALF),
        "out": jnp.concatenate([wo[0].reshape(HALF, HALF), wo[1].reshape(HALF, HALF)], axis=1),
        "in": jnp.concatenate([gb[:, k].reshape(D, HALF) for k in range(4)], axis=1),
        "back": jnp.concatenate([wb[0].reshape(2048, HALF), wb[1].reshape(2048, HALF)], axis=1),
        "b_query": half_of(vectors[0]),
        "b_value": half_of(vectors[1]),
        "b_out": vectors[2],
        "gain_attn": vectors[3],
        "shift_attn": vectors[4],
        "b_back": vectors[5],
        "gain_ffn": vectors[6],
        "shift_ffn": vectors[7],
        "b_in": half_of(lines[:, 8:12].reshape(FF)),
    }
    middle, saved_one = layer_forward(widen(tokens), w, core, bounds, 2)
    result, saved_two = layer_forward(middle, w, core, bounds, 4)
    d_middle, vectors_two, pairs_two = layer_backward(
        widen(cotangent), w, saved_two, core, bounds, 6
    )
    d_tokens, vectors_one, pairs_one = layer_backward(d_middle, w, saved_one, core, bounds, 8)

    def gradient(k):
        former = jnp.concatenate([pairs_one[k][0], pairs_two[k][0]], axis=0)
        latter = jnp.concatenate([pairs_one[k][1], pairs_two[k][1]], axis=0)
        return bfloat(product_tn(former, latter))

    da = jnp.stack([gradient(k).reshape(64, 16, HALF) for k in range(3)], axis=1)
    do = gradient(3).reshape(32, 16, 2, HALF).transpose(2, 0, 1, 3)
    db = gradient(4).reshape(64, 16, 4, HALF).transpose(0, 2, 1, 3)
    dc = gradient(5).reshape(32, 64, 2, HALF).transpose(2, 0, 1, 3)
    sums = [a + b for a, b in zip(vectors_one, vectors_two)]

    def placed(vector):
        zeros = jnp.zeros((2 * vector.shape[0],), F32)
        return lax.dynamic_update_slice_in_dim(zeros, vector, core * vector.shape[0], 0)

    sums = [placed(sums[0]), placed(sums[1])] + sums[2:8] + [placed(sums[8])]
    lines = jnp.concatenate(
        [
            jnp.stack(sums[:8]).reshape(8, 8, 128).transpose(1, 0, 2),
            sums[8].reshape(8, 4, 128),
            jnp.zeros((8, 4, 128), F32),
        ],
        axis=1,
    )
    lines = lines + swap(lines)
    ds = jnp.broadcast_to(bfloat(lines)[:, None], (8, 8, 16, 128)).reshape(CUBE + (16, 128))
    grads = scatter_gradients(
        da.reshape(CUBE + (48, HALF)),
        do.reshape(2, 2, 2, 2, 4, 16, HALF),
        db.reshape(CUBE + (64, HALF)),
        dc.reshape(2, 2, 2, 2, 4, 64, HALF),
        ds,
    )
    g_query, g_key, g_value, g_out, g_in, g_back, tiny = grads
    eight = lax.dynamic_slice(tiny, (0, tok * 8), (8, 8))
    g_b_in = lax.dynamic_slice(tiny, (8 + tok // 4, (tok % 4) * 32), (1, 32))[0]
    (
        g_b_query, g_b_value, g_b_out, g_gain_attn, g_shift_attn, g_b_back, g_gain_ffn, g_shift_ffn,
    ) = [eight[k] for k in range(8)]
    return (
        bfloat(result), bfloat(d_tokens), g_query, g_b_query, g_key, g_value, g_b_value, g_out,
        g_b_out, g_gain_attn, g_shift_attn, g_in, g_b_in, g_back, g_b_back, g_gain_ffn, g_shift_ffn,
    )


def solution(mesh):
    both = ("seq", "tok")
    rows, vector = P(both, None), P(both)
    ins = (
        rows, rows, P("seq", None), P("seq"), rows, vector, rows, rows, vector, rows, vector, vector,
        vector, rows, vector, rows, vector, vector, vector,
    )
    outs = (
        rows, rows, rows, vector, rows, rows, vector, rows, vector, vector, vector, rows, vector,
        rows, vector, vector, vector,
    )
    return jax.shard_map(on_device, mesh=mesh, in_specs=ins, out_specs=outs, check_vma=False)
```

```python
import math
import types

import jax
import jax.numpy as jnp
from jax import lax
from jax.experimental import pallas as pl
from jax.experimental.pallas import tpu as pltpu
from jax.sharding import PartitionSpec as P

HEADS = 16
WINDOW = 1024
D = 1024
FF = 4096
HEAD = 64
CHIPS = 8
ROWS = 192
CHIP_ROWS = 2 * ROWS
LENGTH = CHIP_ROWS * CHIPS
HALF = 512
EPSILON = 1e-05
MASKED = -1e30
SCALE = 1.0 / math.sqrt(HEAD)
LOG2E = 1.4426950408889634
MESH = pl.DeviceIdType.MESH
BF = jnp.bfloat16
F32 = jnp.float32
CUBE = (4, 2, 2, 4)
X, Y, Z, CORE = range(4)


def bfloat(tensor):
    return tensor.astype(BF)


def widen(tensor):
    return tensor.astype(F32)


def place():
    seq, tok = lax.axis_index("seq"), lax.axis_index("tok")
    x = (tok // 8) * 2 + seq % 2
    return {X: x, Y: seq // 2, Z: (tok // 2) % 4, CORE: tok % 2}


def device(x, y, z, core):
    return (y * 2 + x % 2, (x // 2) * 8 + z * 2 + core)


def moved(here, axis, steps):
    there = dict(here)
    there[axis] = lax.rem(here[axis] + steps + 4, 4)
    return device(there[X], there[Y], there[Z], there[CORE])


def partner(here):
    return device(here[X], here[Y], here[Z], 1 - here[CORE])


def cube_index(here, whole, axis, value):
    index = []
    for name in (Y, X, Z):
        if name in whole:
            index += [slice(None)] * (2 if name == X else 1)
        else:
            at = value if name == axis else here[name]
            index += [at % 2, at // 2] if name == X else [at]
    return tuple(index)


def greet(targets):
    barrier = pltpu.get_barrier_semaphore()
    for target in targets:
        pl.semaphore_signal(barrier, inc=1, device_id=target, device_id_type=MESH)
    pl.semaphore_wait(barrier, len(targets))


def neighbours(here, steps):
    return [moved(here, axis, step) for axis in (X, Y, Z) for step in steps] + [partner(here)]


def group_device(here, number):
    seq = lax.axis_index("seq")
    return (seq, (number // 4) * 8 + (number % 4) * 2 + here[CORE])


def group_number(here):
    return (here[X] // 2) * 4 + here[Z]


def group(here):
    me = group_number(here)
    return [group_device(here, lax.rem(me + k, CHIPS)) for k in range(1, CHIPS)]


class Wire:
    def __init__(self, here, send, recv, local):
        self.send, self.recv, self.local = send, recv, local
        self.here, self.number, self.locals = here, 0, 0
        self.core, self.me = here[CORE], group_number(here)
        self.own = pl.ds(pl.multiple_of(self.core * ROWS, ROWS), ROWS)
        self.other = pl.ds(pl.multiple_of((1 - self.core) * ROWS, ROWS), ROWS)

    def to(self, source, target, device_id):
        copy = pltpu.make_async_remote_copy(
            src_ref=source,
            dst_ref=target,
            send_sem=self.send.at[self.number],
            recv_sem=self.recv.at[self.number],
            device_id=device_id,
            device_id_type=MESH,
        )
        self.number += 1
        copy.start()
        return copy

    def swap(self, source, target):
        return self.to(source, target, partner(self.here))

    def fetch(self, source, target):
        copy = pltpu.make_async_copy(source, target, self.local.at[self.locals])
        self.locals += 1
        copy.start()
        return copy

    def spread(self, stage, target):
        span = chunk_span(self.me)
        copies = []
        for k in range(1, CHIPS):
            to = lax.rem(self.me + k, CHIPS)
            copies.append(self.to(stage.at[to], target.at[:, span], group_device(self.here, to)))
        copies.append(self.fetch(stage.at[self.me], target.at[:, span]))
        return copies


def chunk_span(number):
    return pl.ds(pl.multiple_of(number * CHIP_ROWS, CHIP_ROWS), CHIP_ROWS)


EVERY = slice(None)
CUBE_ALL = (EVERY,) * 4
SIDES = (pl.ds(0, HALF // 2), pl.ds(HALF // 2, HALF // 2))
SIZES = {Y: (4,), X: (2, 2), Z: (4,)}
GATHER_ORDERS = ((X, Z, Y), (Y, X, Z), (Z, Y, X), (X, Z, Y))
SCATTER_ORDERS = ((Y, Z, X), (Z, X, Y), (X, Y, Z), (Y, Z, X))


def ring_gather(wire, parts):
    here = wire.here
    sent, kept = [], []
    for buffer, prefix, order, own, _, _ in parts:
        kept.append(wire.fetch(own, buffer.at[prefix + cube_index(here, (), None, None)]))
    for phase in range(2):
        copies = []
        for step in (1, -1, 2):
            for buffer, prefix, order, own, _, _ in parts:
                axis = order[phase]
                block = buffer.at[prefix + cube_index(here, order[:phase], axis, here[axis])]
                source = own if phase == 0 else block
                copies.append(wire.to(source, block, moved(here, axis, step)))
        yield
        for copy in copies:
            copy.wait_recv()
        sent += copies
        if phase == 0:
            for copy in kept:
                copy.wait()
    one, two = [], []
    for buffer, prefix, order, _, _, complete in parts:
        axis = order[2]
        block = buffer.at[prefix + cube_index(here, order[:2], axis, here[axis])]
        one.append([wire.to(block, block, moved(here, axis, step)) for step in (1, -1)])
    for _, _, order, _, _, complete in parts:
        complete(here[order[2]])
    yield
    for (buffer, prefix, order, _, cut, complete), pair in zip(parts, one):
        axis = order[2]
        for side, step in enumerate((1, -1)):
            pair[side].wait_recv()
            come = lax.rem(here[axis] - step + 4, 4)
            index = prefix + cube_index(here, order[:2], axis, come)
            if cut:
                index += (EVERY, SIDES[side])
            if cut or side == 0:
                block = buffer.at[index]
                two.append(wire.to(block, block, moved(here, axis, step)))
            complete(come)
        sent += pair
    yield
    for copy in two:
        copy.wait_recv()
    for _, _, order, _, _, complete in parts:
        complete(lax.rem(here[order[2]] + 2, 4))
    for copy in sent + two:
        copy.wait_send()


GATHER_COPIES = 3 + 3 + 4


def lengths_of(full):
    return tuple(n for name in (Y, X, Z) if name in full for n in SIZES[name])


def digits_of(i, lengths):
    digits = []
    for length in reversed(lengths):
        digits.append(lax.rem(i, length))
        i = lax.div(i, length)
    return tuple(digits[::-1])


def one_chip(here, full, axis, value, digits):
    digits, index = list(digits), []
    for name in (Y, X, Z):
        if name in full:
            index += [digits.pop(0) for _ in SIZES[name]]
        else:
            at = value if name == axis else here[name]
            index += [at % 2, at // 2] if name == X else [at]
    return tuple(index)


SCATTER_COPIES = (4, 3, 3)


def scatter_slots(order, rows, cut):
    wide = HALF if cut else 128
    dims = lengths_of(order[1:])
    slots = [
        pltpu.VMEM((2,) + dims + (rows, wide // 2 if cut else wide), BF),
        pltpu.VMEM((2,) + dims + (rows, wide), BF),
    ]
    return slots + [
        pltpu.VMEM((3,) + lengths_of(order[phase + 1 :]) + (rows, wide), BF) for phase in (1, 2)
    ]


def ring_scatter(wire, parts, phases):
    here = wire.here
    sent = []
    for phase in phases:
        ahead, arriving = [], []
        for buffer, prefix, order, cut, slots, _ in parts:
            axis, full = order[phase], order[phase + 1 :]
            row = []
            if phase == 0:
                far = prefix + cube_index(here, full, axis, lax.rem(here[axis] + 2, 4))
                for side, step in enumerate((1, -1)):
                    if cut or side == 0:
                        block = buffer.at[far + ((EVERY, SIDES[side]) if cut else ())]
                        row.append(wire.to(block, slots[0].at[side], moved(here, axis, step)))
                ahead.append(row)
            else:
                for k, step in enumerate((1, -1, 2)):
                    value = lax.rem(here[axis] + step + 4, 4)
                    block = buffer.at[prefix + cube_index(here, full, axis, value)]
                    row.append(
                        wire.to(block, slots[1 + phase].at[k], moved(here, axis, step))
                    )
                arriving.append(row)
            sent += row
        yield
        if phase == 0:
            for (buffer, prefix, order, cut, slots, _), row in zip(parts, ahead):
                axis, full = order[phase], order[phase + 1 :]
                pair = []
                for side, step in enumerate((1, -1)):
                    value = lax.rem(here[axis] + step + 4, 4)
                    if side < len(row):
                        row[side].wait_recv()
                        half = slots[0]
                        columns_ = SIDES[side] if cut else EVERY

                        def add(
                            i, _, buffer=buffer, prefix=prefix, axis=axis, full=full, value=value,
                            half=half, side=side, columns_=columns_,
                        ):
                            digits = digits_of(i, lengths_of(full))
                            at = prefix + one_chip(here, full, axis, value, digits)
                            at += (EVERY, columns_)
                            buffer[at] = bfloat(widen(buffer[at]) + widen(half[(side,) + digits]))
                            return 0

                        lax.fori_loop(0, math.prod(lengths_of(full)), add, 0)
                    block = buffer.at[prefix + cube_index(here, full, axis, value)]
                    pair.append(wire.to(block, slots[1].at[side], moved(here, axis, step)))
                arriving.append(pair)
                sent += pair
            yield
        for (buffer, prefix, order, _, slots, final), row in zip(parts, arriving):
            axis, full = order[phase], order[phase + 1 :]
            come = slots[1 + phase]
            for copy in row:
                copy.wait_recv()

            def total(
                i, _, buffer=buffer, prefix=prefix, axis=axis, full=full, come=come, final=final,
                count=len(row),
            ):
                digits = digits_of(i, lengths_of(full))
                at = prefix + one_chip(here, full, axis, here[axis], digits)
                value = widen(buffer[at])
                for k in range(count):
                    value = value + widen(come[(k,) + digits])
                if phase < 2:
                    buffer[at] = bfloat(value)
                else:
                    final(value)
                return 0

            lax.fori_loop(0, math.prod(lengths_of(full)), total, 0)
    for copy in sent:
        copy.wait_send()


def advance(stages, count=1):
    for _ in range(count):
        next(stages, None)


class Mail:
    def __init__(self, here, send, recv):
        self.here, self.me, self.send, self.recv = here, group_number(here), send, recv
        self.count = 0
        self.sent = []

    def to(self, number, source, target):
        copy = pltpu.make_async_remote_copy(
            src_ref=source,
            dst_ref=target,
            send_sem=self.send.at[self.count],
            recv_sem=self.recv.at[self.me],
            device_id=group_device(self.here, number),
            device_id_type=MESH,
        )
        self.count += 1
        copy.start()
        self.sent.append(copy)

    def finish(self, source, target):
        for k in range(1, CHIPS):
            sender = lax.rem(self.me + k, CHIPS)
            pltpu.make_async_remote_copy(
                src_ref=source,
                dst_ref=target,
                send_sem=self.send.at[0],
                recv_sem=self.recv.at[sender],
                device_id=group_device(self.here, sender),
                device_id_type=MESH,
            ).wait_recv()
        for copy in self.sent:
            copy.wait_send()


BLOCK = 256
SPAN = 1280
STEPS = LENGTH // BLOCK
SLOTS = 4
LAST_START = LENGTH - SPAN


def limits(bounds, first, count):
    places = first + lax.broadcasted_iota(jnp.int32, (1, count), 1)
    low = jnp.maximum(places - (WINDOW // 2 - 1), 0)
    high = jnp.minimum(places + WINDOW // 2, LENGTH)
    for bound in bounds:
        low = jnp.maximum(low, jnp.where(bound <= places, bound, 0))
        high = jnp.minimum(high, jnp.where(bound > places, bound, LENGTH))
    return low, high


def dot(former, latter):
    return jnp.dot(former, latter, preferred_element_type=F32)


def attend_steps(refs, mail, between):
    qkv, mixed_t, mixed, inverse = refs.qkv, refs.mixed_t, refs.mixed_head, refs.inverse
    live, end, bounds = LENGTH - refs.pads[0], 0, []
    for k in range(4):
        end = end + refs.lengths[0, k]
        bounds.append(jnp.minimum(end, live))
    kv, ones_v, chances, stage, local = refs.kv, refs.ones_v, refs.held, refs.mixed_stage, refs.attend_local
    me = mail.me
    kv[...] = jnp.concatenate([qkv[1], qkv[2]], axis=0).T
    ones_v[0:HEAD, :] = jnp.ones((HEAD, LENGTH), BF)
    ones_v[HEAD:, :] = qkv[2]
    kept = []

    def step(i):
        first = pl.multiple_of(i * BLOCK, BLOCK)
        start = pl.multiple_of(jnp.clip(first - 512, 0, LAST_START), BLOCK)
        queries = qkv[0, :, pl.ds(first, BLOCK)]
        padded = jnp.concatenate([queries, jnp.zeros_like(queries)], axis=0)
        scores = dot(kv[pl.ds(start, SPAN), :], padded)
        low, high = limits(bounds, first, BLOCK)
        places = start + lax.broadcasted_iota(jnp.int32, (SPAN, BLOCK), 0)
        scores = jnp.where((places >= low) & (places < high), scores, MASKED)
        highest = jnp.max(scores, axis=0, keepdims=True)
        raised = bfloat(jnp.exp2((scores - highest) * (SCALE * LOG2E)))
        chances[i] = raised
        out = dot(ones_v[:, pl.ds(start, SPAN)], raised)
        back = 1.0 / out[0:1]
        result = out[HEAD:] * back
        mixed[:, pl.ds(first, BLOCK)] = result
        stage[:, pl.ds(first, BLOCK)] = bfloat(result)
        inverse[:, pl.ds(first, BLOCK)] = back

    for slot in range(SLOTS):
        pair = lax.rem(me // 2 + 1 + slot, SLOTS)

        def run(t, _, pair=pair):
            step(pair * 3 + t)
            return 0

        lax.fori_loop(0, 3, run, 0)
        blocks = pl.ds(pair * 3, 3)
        copy = pltpu.make_async_copy(chances.at[blocks], refs.chances.at[blocks], local.at[slot])
        copy.start()
        kept.append(copy)
        if slot < SLOTS - 1:
            for number in (2 * pair, 2 * pair + 1):
                mail.to(number, stage.at[:, chunk_span(number)], mixed_t.at[me])
        else:
            number = me + 1 - 2 * (me % 2)
            mail.to(number, stage.at[:, chunk_span(number)], mixed_t.at[me])
            copy = pltpu.make_async_copy(
                stage.at[:, chunk_span(me)], mixed_t.at[me], local.at[SLOTS]
            )
            copy.start()
            kept.append(copy)
        between(slot)
    refs.keep(mixed, inverse)
    for copy in kept:
        copy.wait()
    mail.finish(stage.at[:, chunk_span(me)], mixed_t.at[me])


MIXED_T = dict(mixed_t=((CHIPS, HEAD, CHIP_ROWS), BF))
ATTEND_SAVED = dict(mixed_head=((HEAD, LENGTH), F32), inverse=((1, LENGTH), F32))
CHANCES = ((STEPS, SPAN, BLOCK), BF)
ATTEND_SCRATCH = dict(
    kv=((LENGTH, 2 * HEAD), BF), ones_v=((2 * HEAD, LENGTH), BF), held=CHANCES,
    mixed_stage=((HEAD, LENGTH), BF),
)
MAIL_SEMS = [pltpu.SemaphoreType.DMA((CHIPS - 1,)), pltpu.SemaphoreType.DMA((CHIPS,))]


def call(
    body, name, number, near, loaded, sources, outputs, saved, far, scratch, semaphores, scalars={}
):
    vmem, hbm = pl.BlockSpec(memory_space=pltpu.VMEM), pl.BlockSpec(memory_space=pltpu.HBM)
    smem = pl.BlockSpec(memory_space=pltpu.SMEM)
    scratch = dict(scratch)
    for key, value in loaded.items():
        scratch[key] = (value.shape, value.dtype)
    scratch.update(saved)
    specs = [*outputs.values(), *saved.values(), *far.values()]

    def size(shape, dtype):
        rows, lanes = (1,) * (2 - len(shape[-2:])) + tuple(shape[-2:])
        rows, lanes = -(-rows // 8) * 8, -(-lanes // 128) * 128
        return math.prod(shape[:-2]) * rows * lanes * jnp.dtype(dtype).itemsize

    held = [(value.shape, value.dtype) for value in near.values()] + list(outputs.values())
    held += [s if isinstance(s, tuple) else (s.shape, s.dtype) for s in scratch.values()]
    limit = sum(size(*spec) for spec in held) + 10 * 2**20

    def kernel(*values):
        values = list(values)

        def take(names):
            return {key: values.pop(0) for key in names}

        refs = types.SimpleNamespace(**take(scalars), **take(near))
        heres = take(loaded)
        for key, ref in take(sources).items():
            setattr(refs, key, ref)
        for key, ref in take(outputs).items():
            setattr(refs, key, ref)
        outs = take(saved)
        for names in (far, scratch):
            for key, ref in take(names).items():
                setattr(refs, key, ref)
        copies = values.pop(0)
        pending = [
            pltpu.make_async_copy(ref, getattr(refs, key), copies.at[k])
            for k, (key, ref) in enumerate(heres.items())
        ]
        for copy in pending:
            copy.start()
        kept = []

        def arrive():
            for copy in pending:
                copy.wait()

        def keep(*arrays):
            for k, (key, out) in enumerate(outs.items()):
                if any(getattr(refs, key) is array for array in arrays):
                    copy = pltpu.make_async_copy(
                        getattr(refs, key), out, copies.at[len(heres) + k]
                    )
                    copy.start()
                    kept.append(copy)

        refs.arrive, refs.keep = arrive, keep
        body(refs, values)
        for copy in kept:
            copy.wait()

    results = pl.pallas_call(
        kernel,
        out_shape=tuple(jax.ShapeDtypeStruct(*spec) for spec in specs),
        in_specs=[smem] * len(scalars)
        + [vmem] * len(near)
        + [hbm] * (len(loaded) + len(sources)),
        out_specs=(vmem,) * len(outputs) + (hbm,) * (len(saved) + len(far)),
        scratch_shapes=[
            pltpu.VMEM(*spec) if isinstance(spec, tuple) else spec for spec in scratch.values()
        ]
        + [dma(max(1, len(loaded) + len(saved)))]
        + list(semaphores),
        name=name,
        compiler_params=pltpu.CompilerParams(
            collective_id=number, has_side_effects=True, vmem_limit_bytes=max(limit, 58 * 2**20)
        ),
    )(*scalars.values(), *near.values(), *loaded.values(), *sources.values())
    return types.SimpleNamespace(**dict(zip([*outputs, *saved, *far], results)))


def dma(count):
    return pltpu.SemaphoreType.DMA((count,))


def attend(lengths, pads, qkv, number):
    def body(refs, semaphores):
        send, recv, refs.attend_local = semaphores
        here = place()
        greet(group(here))
        refs.arrive()
        attend_steps(refs, Mail(here, send, recv), lambda slot: None)

    return call(
        body, "attend", number, dict(qkv=qkv), {}, {}, MIXED_T, ATTEND_SAVED,
        dict(chances=CHANCES), ATTEND_SCRATCH, MAIL_SEMS + [dma(SLOTS + 1)],
        dict(lengths=lengths, pads=pads),
    )


PAD = 2 * BLOCK
PADDED = LENGTH + 2 * PAD


def attend_back_steps(refs, mail_q, mail_kv, between):
    qkv, mixed, inverse, d_mixed = refs.qkv, refs.mixed_head, refs.inverse, refs.d_mixed
    d_q_t, d_kv_t, chances, kv = refs.d_q_t, refs.d_kv_t, refs.held, refs.kv
    rows_q, rows_d, turned_d, shift = refs.rows_q, refs.rows_d, refs.turned_d, refs.shift
    total_q, stage_q, stage_kv = refs.total_q, refs.stage_q, refs.stage_kv
    me = mail_q.me
    kept = []
    for slot in range(SLOTS):
        blocks = pl.ds(slot * 3, 3)
        copy = pltpu.make_async_copy(
            refs.chances.at[blocks], chances.at[blocks], refs.attend_local.at[slot]
        )
        copy.start()
        kept.append(copy)
    kv[...] = jnp.concatenate([qkv[1], qkv[2]], axis=0).T
    scaled = bfloat(widen(d_mixed[...]) * inverse[...])
    inner = jnp.sum(widen(scaled) * mixed[...], axis=0, keepdims=True)
    for edge in (0, PAD + LENGTH):
        shift[:, edge : edge + PAD] = jnp.zeros((1, PAD), F32)
        turned_d[:, edge : edge + PAD] = jnp.zeros((2 * HEAD, PAD), BF)
        rows_q[edge : edge + PAD, :] = jnp.zeros((PAD, 2 * HEAD), BF)
        rows_d[edge : edge + PAD, :] = jnp.zeros((PAD, 2 * HEAD), BF)
    middle = slice(PAD, PAD + LENGTH)
    shift[:, middle] = inner
    turned_d[0:HEAD, middle] = jnp.zeros((HEAD, LENGTH), BF)
    turned_d[HEAD:, middle] = scaled
    both = jnp.concatenate([qkv[0], scaled], axis=0).T
    left = lax.broadcasted_iota(jnp.int32, both.shape, 1) < HEAD
    rows_q[middle, :] = jnp.where(left, both, jnp.zeros_like(both))
    rows_d[middle, :] = jnp.where(left, jnp.zeros_like(both), both)
    total_q[...] = jnp.zeros_like(total_q)
    between(-1)
    for copy in kept:
        copy.wait()

    def step(i):
        first = pl.multiple_of(i * BLOCK, BLOCK)
        keys = pl.ds(first, BLOCK)
        span = pl.ds(first, SPAN)
        tiles = []
        for t in range(5):
            block = jnp.clip(i - 2 + t, 0, STEPS - 1)
            start = jnp.clip(block * BLOCK - 512, 0, LAST_START)
            offset = pl.multiple_of(jnp.clip(first - start, 0, SPAN - BLOCK), BLOCK)
            tiles.append(chances[block, pl.ds(offset, BLOCK), :])
        weights = jnp.concatenate(tiles, axis=1)
        grad_weights = dot(kv[keys, :], turned_d[:, span])
        grad_scores = bfloat(widen(weights) * (grad_weights - shift[:, span]))
        total = dot(weights, rows_d[span, :]) + dot(grad_scores, rows_q[span, :])
        total_q[:, span] += dot(qkv[1, :, keys], grad_scores)
        turned = total.T
        stage_kv[0:HEAD, keys] = bfloat(turned[:HEAD] * SCALE)
        stage_kv[HEAD:, keys] = bfloat(turned[HEAD:])

    def send_queries(number):
        span = pl.ds(pl.multiple_of(number * CHIP_ROWS + PAD, 128), CHIP_ROWS)
        stage_q[number] = bfloat(total_q[:, span] * SCALE)
        mail_q.to(number, stage_q.at[number], d_q_t.at[me])

    near = me + 1 - 2 * (me % 2)
    for slot in range(SLOTS):
        pair = lax.rem(me // 2 + 1 + slot, SLOTS)

        def run(t, _, pair=pair):
            step(pair * 3 + t)
            return 0

        lax.fori_loop(0, 3, run, 0)
        if slot < SLOTS - 1:
            for number in (2 * pair, 2 * pair + 1):
                mail_kv.to(number, stage_kv.at[:, chunk_span(number)], d_kv_t.at[me])
        else:
            mail_kv.to(near, stage_kv.at[:, chunk_span(near)], d_kv_t.at[me])
        if slot == 2:
            complete = lax.rem(me // 2 + 2, SLOTS)
            send_queries(2 * complete)
            send_queries(2 * complete + 1)
        between(slot)
    for rest in (1, 3):
        pair = lax.rem(me // 2 + rest, SLOTS)
        send_queries(2 * pair)
        send_queries(2 * pair + 1)
    send_queries(near)
    span = pl.ds(pl.multiple_of(me * CHIP_ROWS + PAD, 128), CHIP_ROWS)
    d_q_t[me] = bfloat(total_q[:, span] * SCALE)
    d_kv_t[me] = stage_kv[:, chunk_span(me)]
    mail_kv.finish(stage_kv.at[:, chunk_span(me)], d_kv_t.at[me])
    mail_q.finish(stage_q.at[me], d_q_t.at[me])


BACK_SCRATCH = dict(
    held=CHANCES, kv=((LENGTH, 2 * HEAD), BF), rows_q=((PADDED, 2 * HEAD), BF),
    rows_d=((PADDED, 2 * HEAD), BF), turned_d=((2 * HEAD, PADDED), BF), shift=((1, PADDED), F32),
    total_q=((HEAD, PADDED), F32), stage_q=((CHIPS, HEAD, CHIP_ROWS), BF),
    stage_kv=((2 * HEAD, LENGTH), BF),
)
BACK_OUTPUTS = dict(
    d_q_t=((CHIPS, HEAD, CHIP_ROWS), BF), d_kv_t=((CHIPS, 2 * HEAD, CHIP_ROWS), BF)
)


def attend_back(near, loaded, chances, number):
    def body(refs, semaphores):
        send_q, recv_q, send_kv, recv_kv, refs.attend_local = semaphores
        here = place()
        greet(group(here))
        refs.arrive()
        attend_back_steps(
            refs, Mail(here, send_q, recv_q), Mail(here, send_kv, recv_kv), lambda slot: None
        )

    return call(
        body, "attend_back", number, near, loaded, dict(chances=chances), BACK_OUTPUTS, {}, {},
        BACK_SCRATCH, MAIL_SEMS + MAIL_SEMS + [dma(SLOTS)],
    )


REST_ROWS = 48


def rest_planes(here):
    return [
        (part,) + cube_index(here, SCATTER_ORDERS[part][1:], SCATTER_ORDERS[part][0], here[SCATTER_ORDERS[part][0]])
        for part in range(3)
    ]


def attend_back_scatter(near, loaded, chances, g_in, g_back, g_out, number):
    slots = [
        scatter_slots(SCATTER_ORDERS[part], REST_ROWS, True) for part in range(3)
    ]

    def body(refs, semaphores):
        send, recv, local, send_q, recv_q, send_kv, recv_kv, refs.attend_local = semaphores
        here = place()
        wire = Wire(here, send, recv, local)
        core = wire.core
        greet(neighbours(here, (1, -1)) + group(here))
        refs.arrive()
        mine = pl.ds(2 * core, 2)
        own_columns = pl.ds(pl.multiple_of(core * HALF, HALF), HALF)
        your_columns = pl.ds(pl.multiple_of((1 - core) * HALF, HALF), HALF)
        blocks = (EVERY,) * 3
        halves = (
            (refs.g_back, pl.ds(0, 48), refs.rest.at[(1, mine) + blocks]),
            (refs.g_back, pl.ds(48, 16), refs.rest.at[(2, mine) + blocks + (pl.ds(16, 16),)]),
            (refs.g_out, EVERY, refs.rest.at[(2, mine) + blocks + (pl.ds(32, 16),)]),
        )
        copies = [
            wire.swap(ref.at[CUBE_ALL + (rows, your_columns)], target)
            for ref, rows, target in halves
        ]
        copies += [
            wire.fetch(ref.at[CUBE_ALL + (rows, own_columns)], target)
            for ref, rows, target in halves
        ]
        for k in range(4):
            source = refs.g_in.at[CUBE_ALL + (EVERY, pl.ds(k * HALF, HALF))]
            part, low = ((0, 16 * k), (2, 0))[k // 3]
            copies.append(
                wire.fetch(source, refs.rest.at[(part,) + CUBE_ALL + (pl.ds(low, 16),)])
            )
        arrivals = [
            [getattr(refs, "slot_%d_%d" % (part, k)) for k in range(2)] for part in range(3)
        ]
        stages = ring_scatter(
            wire,
            [
                (refs.rest, (part,), SCATTER_ORDERS[part], True, arrivals[part], None)
                for part in range(3)
            ],
            (0,),
        )

        def between(slot):
            if slot == -1:
                for copy in copies:
                    copy.wait()
                advance(stages)
            elif slot == 0:
                advance(stages)

        attend_back_steps(
            refs, Mail(here, send_q, recv_q), Mail(here, send_kv, recv_kv), between
        )
        for _ in stages:
            pass
        kept = [
            wire.fetch(refs.rest.at[at], refs.rest_summed.at[at]) for at in rest_planes(here)
        ]
        for copy in kept:
            copy.wait()

    rest = ((3,) + CUBE + (REST_ROWS, HALF), BF)
    scratch = dict(BACK_SCRATCH, rest=rest)
    for part in range(3):
        for k in range(2):
            scratch["slot_%d_%d" % (part, k)] = slots[part][k]
    copies = 3 * SCATTER_COPIES[0] + 3
    return call(
        body, "attend_back_scatter", number, near, loaded,
        dict(chances=chances, g_in=g_in, g_back=g_back, g_out=g_out),
        BACK_OUTPUTS, {}, dict(rest_summed=rest), scratch,
        [dma(copies), dma(copies), dma(10)] + MAIL_SEMS + MAIL_SEMS + [dma(SLOTS)],
    )


def dot_nt(former, latter):
    return lax.dot_general(former, latter, (((1,), (1,)), ((), ())), preferred_element_type=F32)


QKV, OUT, IN, BACK = range(4)


class Weights:
    def __init__(self, refs, wire, names):
        core = wire.core
        mine = pl.ds(2 * core, 2)
        own = (mine,) + (EVERY,) * 3
        self.refs, self.pending = refs, {}
        for name in names:
            if name == QKV:
                pairs = [(refs.gqkv, refs.w_qkv)]
            elif name == OUT:
                pairs = [
                    (refs.rest_three.at[own + (pl.ds(32, 16),)], refs.w_out.at[core]),
                    (refs.yours_three.at[CUBE_ALL + (pl.ds(16, 16),)], refs.w_out.at[1 - core]),
                ]
            elif name == IN:
                pairs = [
                    (refs.rest_one.at[CUBE_ALL + (pl.ds(16 * k, 16),)], refs.w_in.at[k])
                    for k in range(3)
                ] + [(refs.rest_three.at[CUBE_ALL + (pl.ds(0, 16),)], refs.w_in.at[3])]
            else:
                blocks = (EVERY,) * 4
                low, high = blocks + (pl.ds(0, 48),), blocks + (pl.ds(48, 16),)
                pairs = [
                    (refs.rest_two.at[own], refs.w_back.at[(core,) + low]),
                    (refs.rest_three.at[own + (pl.ds(16, 16),)], refs.w_back.at[(core,) + high]),
                    (refs.yours_two, refs.w_back.at[(1 - core,) + low]),
                    (refs.yours_three.at[CUBE_ALL + (pl.ds(0, 16),)], refs.w_back.at[(1 - core,) + high]),
                ]
            self.pending[name] = [wire.fetch(*pair) for pair in pairs]

    def ready(self, name):
        for copy in self.pending.pop(name, []):
            copy.wait()

    def qkv(self, k):
        self.ready(QKV)
        return self.refs.w_qkv[k].reshape(D, HALF)

    def out(self, half):
        self.ready(OUT)
        return self.refs.w_out[half].reshape(HALF, HALF)

    def into(self, chunk):
        self.ready(IN)
        return self.refs.w_in[chunk].reshape(D, HALF)

    def back(self, half, chunk):
        self.ready(BACK)
        return self.refs.w_back[half, chunk // 2, chunk % 2].reshape(HALF, HALF)


def columns(k):
    return slice(k * HALF, k * HALF + HALF)


def vector(refs, k):
    return refs.vecs[k : k + 1, :]


def half_vector(refs, core, k):
    return refs.vecs[k : k + 1, pl.ds(pl.multiple_of(core * HALF, HALF), HALF)]


B_QUERY, B_VALUE, B_OUT, GAIN_ATTN, SHIFT_ATTN, B_BACK, GAIN_FFN, SHIFT_FFN = range(8)


def normalized(tensor):
    centred = tensor - jnp.mean(tensor, axis=-1, keepdims=True)
    factor = lax.rsqrt(jnp.mean(centred * centred, axis=-1, keepdims=True) + EPSILON)
    return centred * factor, factor


def normalize_back(grad_out, normed, factor, gain):
    grad_normed = grad_out * gain
    grad_input = factor * (
        grad_normed
        - jnp.mean(grad_normed, axis=-1, keepdims=True)
        - normed * jnp.mean(grad_normed * normed, axis=-1, keepdims=True)
    )
    return (
        grad_input,
        jnp.sum(grad_out * normed, axis=0, keepdims=True),
        jnp.sum(grad_out, axis=0, keepdims=True),
    )


def row_sum(tensor):
    return jnp.sum(widen(tensor), axis=0, keepdims=True)


def gelu_pair(v):
    root = math.sqrt(2.0 / math.pi)
    squared = v * v
    bent = jnp.tanh(root * v * (1.0 + 0.044715 * squared))
    half = 0.5 + 0.5 * bent
    slope = half + (0.5 * root) * v * (1.0 - bent * bent) * (1.0 + (3 * 0.044715) * squared)
    return v * half, slope


def summed_over_cores(refs, wire, number, fill):
    send, come, kept = refs.outgoing.at[number], refs.incoming.at[number], refs.kept
    fill(wire.other, send)
    copy = wire.swap(send, come)
    fill(wire.own, kept)
    copy.wait()
    return kept[...] + come[...]


def project_rows(refs, wire, weight, copy, between):
    entry, rows_of, stage = refs.entry, refs.qkv_rows, refs.qkv_stage
    biases = (half_vector(refs, wire.core, B_QUERY), None, half_vector(refs, wire.core, B_VALUE))

    def project(rows, k):
        result = dot(entry[rows, :], weight(k))
        if biases[k] is not None:
            result = result + biases[k]
        rows_of[k, rows, :] = bfloat(result)

    for k in range(3):
        project(wire.own, k)
    copy.wait()
    refs.keep(entry)
    copies = []
    for k in range(3):
        project(wire.other, k)
        stage[k] = rows_of[k].T.reshape(CHIPS, HEAD, CHIP_ROWS)
        copies += wire.spread(stage.at[k], refs.qkv.at[k])
        if k < 2:
            between()
    return copies


def part_project(refs, wire, weights, hidden):
    entry = refs.entry
    entry[wire.own, :] = bfloat(hidden)
    copy = wire.swap(entry.at[wire.own], entry.at[wire.own])
    return project_rows(refs, wire, weights.qkv, copy, lambda: None)


def part_post(refs, wire, weights):
    mixed = refs.mixed
    mixed[...] = refs.mixed_t[...].reshape(HALF, CHIP_ROWS).T
    refs.keep(mixed)

    def leave(rows, target):
        for half in range(2):
            target[:, columns(half)] = dot(mixed[rows, :], weights.out(half))

    branch = summed_over_cores(refs, wire, 0, leave)
    normed, factor = normalized(widen(refs.hidden[...]) + branch + vector(refs, B_OUT))
    refs.normed_one[...] = normed
    refs.factor_one[...] = factor
    refs.keep(refs.normed_one, refs.factor_one)
    first = normed * vector(refs, GAIN_ATTN) + vector(refs, SHIFT_ATTN)
    refs.first[...] = first
    entry_two, active, slope = refs.entry_two, refs.active, refs.slope
    entry_two[wire.own, :] = bfloat(first)
    copy = wire.swap(entry_two.at[wire.own], entry_two.at[wire.own])

    def inner(rows):
        for chunk in range(4):
            start = pl.multiple_of(wire.core * 2048 + chunk * HALF, HALF)
            before = dot(entry_two[rows, :], weights.into(chunk)) + refs.b_in[:, pl.ds(start, HALF)]
            value, steep = gelu_pair(before)
            active[rows, columns(chunk)] = bfloat(value)
            slope[rows, columns(chunk)] = bfloat(steep)

    inner(wire.own)
    copy.wait()
    refs.keep(entry_two)
    inner(wire.other)
    refs.keep(active, slope)

    def leave_two(rows, target):
        for half in range(2):
            total = dot(active[rows, columns(0)], weights.back(half, 0))
            for chunk in range(1, 4):
                total = total + dot(active[rows, columns(chunk)], weights.back(half, chunk))
            target[:, columns(half)] = total

    second = summed_over_cores(refs, wire, 1, leave_two)
    normed, factor = normalized(refs.first[...] + second + vector(refs, B_BACK))
    refs.normed_two[...] = normed
    refs.factor_two[...] = factor
    refs.keep(refs.normed_two, refs.factor_two)
    return normed * vector(refs, GAIN_FFN) + vector(refs, SHIFT_FFN)


def part_back_dense(refs, wire, weights, grad_out):
    d_branch, d_before, d_attn = refs.d_branch, refs.d_before, refs.d_attn
    sums = refs.sums
    d_second, g_gain, g_shift = normalize_back(
        grad_out, refs.normed_two[...], refs.factor_two[...], vector(refs, GAIN_FFN)
    )
    refs.d_second[...] = d_second
    d_branch[wire.own, :] = bfloat(d_second)
    copy = wire.swap(d_branch.at[wire.own], d_branch.at[wire.own])
    sums[GAIN_FFN : GAIN_FFN + 1, :] = g_gain
    sums[SHIFT_FFN : SHIFT_FFN + 1, :] = g_shift
    sums[B_BACK : B_BACK + 1, :] = row_sum(d_branch[wire.own, :])

    def inner(rows):
        for chunk in range(4):
            d_active = dot_nt(d_branch[rows, columns(0)], weights.back(0, chunk)) + dot_nt(
                d_branch[rows, columns(1)], weights.back(1, chunk)
            )
            d_before[rows, columns(chunk)] = bfloat(
                d_active * widen(refs.slope[rows, columns(chunk)])
            )

    inner(wire.own)
    copy.wait()
    refs.keep(d_branch)
    inner(wire.other)
    refs.keep(d_before)
    for chunk in range(4):
        start = pl.multiple_of(wire.core * 2048 + chunk * HALF, HALF)
        refs.sums_in[:, pl.ds(start, HALF)] = row_sum(d_before[:, columns(chunk)])

    def leave(rows, target):
        total = dot_nt(d_before[rows, columns(0)], weights.into(0))
        for chunk in range(1, 4):
            total = total + dot_nt(d_before[rows, columns(chunk)], weights.into(chunk))
        target[...] = total

    d_first = refs.d_second[...] + summed_over_cores(refs, wire, 2, leave)
    d_inner, g_gain, g_shift = normalize_back(
        d_first, refs.normed_one[...], refs.factor_one[...], vector(refs, GAIN_ATTN)
    )
    refs.d_inner_out[...] = d_inner
    refs.keep(refs.d_inner_out)
    d_attn[wire.own, :] = bfloat(d_inner)
    copy = wire.swap(d_attn.at[wire.own], d_attn.at[wire.own])
    sums[GAIN_ATTN : GAIN_ATTN + 1, :] = g_gain
    sums[SHIFT_ATTN : SHIFT_ATTN + 1, :] = g_shift
    sums[B_OUT : B_OUT + 1, :] = row_sum(d_attn[wire.own, :])
    rows_of, stage = refs.d_mixed_rows, refs.d_mixed_stage

    def enter(rows):
        rows_of[rows, :] = bfloat(
            dot_nt(d_attn[rows, columns(0)], weights.out(0))
            + dot_nt(d_attn[rows, columns(1)], weights.out(1))
        )

    enter(wire.own)
    copy.wait()
    refs.keep(d_attn, refs.sums, refs.sums_in)
    enter(wire.other)
    stage[...] = rows_of[...].T.reshape(CHIPS, HEAD, CHIP_ROWS)
    return wire.spread(stage, refs.d_mixed)


def turn_gradients(refs):
    rows_of = refs.d_qkv
    rows_of[0] = refs.d_q_t[...].reshape(HALF, CHIP_ROWS).T
    rows_of[1] = refs.d_kv_t[:, :HEAD, :].reshape(HALF, CHIP_ROWS).T
    rows_of[2] = refs.d_kv_t[:, HEAD:, :].reshape(HALF, CHIP_ROWS).T


def add_half(refs, wire, k, value):
    half = pl.ds(pl.multiple_of(wire.core * HALF, HALF), HALF)
    refs.sums[k : k + 1, half] = refs.sums[k : k + 1, half] + value


def part_back_project(refs, wire, weights):
    rows_of = refs.d_qkv

    def leave(rows, target):
        total = dot_nt(rows_of[0, rows, :], weights.qkv(0))
        for k in range(1, 3):
            total = total + dot_nt(rows_of[k, rows, :], weights.qkv(k))
        target[...] = total

    return refs.d_inner[...] + summed_over_cores(refs, wire, 3, leave)


ROW_F32 = ((ROWS, D), F32)
COLUMN_F32 = ((ROWS, 1), F32)
CHIP_BF = ((CHIP_ROWS, D), BF)
WIDE_BF = ((CHIP_ROWS, 2048), BF)
HEADS_BF = ((CHIP_ROWS, HALF), BF)
STAGE = (CHIPS, HEAD, CHIP_ROWS)
PROJECT, POST, BACK_DENSE, BACK_PROJECT = range(4)
PARTS = (
    (
        (QKV,),
        dict(entry=CHIP_BF),
        dict(qkv=((3, HEAD, LENGTH), BF)),
        dict(qkv_rows=((3, CHIP_ROWS, HALF), BF), qkv_stage=((3,) + STAGE, BF)),
        1 + 3 * 7,
        3,
    ),
    (
        (OUT, IN, BACK),
        dict(
            mixed=HEADS_BF, normed_one=ROW_F32, factor_one=COLUMN_F32, entry_two=CHIP_BF,
            active=WIDE_BF, slope=WIDE_BF, normed_two=ROW_F32, factor_two=COLUMN_F32,
        ),
        {},
        dict(first=ROW_F32),
        4,
        0,
    ),
    (
        (BACK, IN, OUT),
        dict(
            d_branch=CHIP_BF, d_before=WIDE_BF, d_attn=CHIP_BF, d_inner_out=ROW_F32,
            sums=((8, D), F32), sums_in=((1, FF), F32),
        ),
        dict(d_mixed=((HEAD, LENGTH), BF)),
        dict(d_second=ROW_F32, d_mixed_rows=HEADS_BF, d_mixed_stage=(STAGE, BF)),
        3 + 7,
        1,
    ),
    (
        (QKV,),
        dict(d_qkv=((3, CHIP_ROWS, HALF), BF)),
        {},
        {},
        1,
        0,
    ),
)
WEIGHT_SHAPES = (
    dict(w_qkv=((3,) + CUBE + (16, HALF), BF)),
    dict(w_out=((2, 2, 2, 2, 4, 16, HALF), BF)),
    dict(w_in=((4,) + CUBE + (16, HALF), BF)),
    dict(w_back=((2, 2, 2, 2, 4, 64, HALF), BF)),
)


WEIGHT_COPIES = (1, 2, 4, 4)


def dense(parts, number, gathered, near, loaded, extra, dropped=()):
    outputs, saved, weight_names = {}, dict(extra), []
    scratch = dict(outgoing=((4, ROWS, D), F32), incoming=((4, ROWS, D), F32), kept=ROW_F32)
    copies = locals_ = 0
    for part in parts:
        its_weights, its_saved, its_outputs, its_scratch, its_copies, its_locals = PARTS[part]
        weight_names += [name for name in its_weights if name not in weight_names]
        outputs.update(its_outputs)
        saved.update(its_saved)
        scratch.update(its_scratch)
        copies += its_copies
        locals_ += its_locals
    for name in dropped:
        scratch[name] = saved.pop(name)
    for name in weight_names:
        scratch.update(WEIGHT_SHAPES[name])
        locals_ += WEIGHT_COPIES[name]

    def body(refs, semaphores):
        here = place()
        wire = Wire(here, *semaphores)
        weights = Weights(refs, wire, weight_names)
        if BACK_DENSE in parts:
            refs.sums[...] = jnp.zeros((8, D), F32)
            refs.sums_in[...] = jnp.zeros((1, FF), F32)
        greet([partner(here)] + group(here))
        refs.arrive()
        pending = []
        value = None
        for part in parts:
            if part == PROJECT:
                pending += part_project(refs, wire, weights, value)
            elif part == POST:
                value = part_post(refs, wire, weights)
                refs.result[...] = value.astype(refs.result.dtype)
                refs.keep(refs.result)
            elif part == BACK_DENSE:
                if POST in parts:
                    value = widen(refs.cotangent[...])
                pending += part_back_dense(refs, wire, weights, value)
            else:
                turn_gradients(refs)
                refs.keep(refs.d_qkv)
                add_half(refs, wire, B_QUERY, row_sum(refs.d_qkv[0]))
                add_half(refs, wire, B_VALUE, row_sum(refs.d_qkv[2]))
                value = part_back_project(refs, wire, weights)
        for copy in pending:
            copy.wait()

    return call(
        body, "dense_%d" % number, number, near,
        dict(loaded, vecs=gathered.vecs, b_in=gathered.b_in),
        dict(
            gqkv=gathered.gqkv, rest_one=gathered.rest_one, rest_two=gathered.rest_two,
            rest_three=gathered.rest_three, yours_two=gathered.yours_two,
            yours_three=gathered.yours_three,
        ),
        outputs, saved, {}, scratch, [dma(copies), dma(copies), dma(locals_)],
    )


def opening(lengths, pads, shards, vectors, tokens, number):
    def body(refs, semaphores):
        send, recv, local, mail_send, mail_recv, refs.attend_local = semaphores
        here = place()
        wire = Wire(here, send, recv, local)
        core = wire.core
        greet(neighbours(here, (1, -1, 2)) + group(here))
        refs.arrive()
        tok = lax.axis_index("tok")
        lanes = lax.broadcasted_iota(jnp.int32, (1, 128), 1)
        line = refs.vectors[...]
        rows = []
        for k in range(8):
            turned = pltpu.roll(line, lax.rem(tok * 8 - 8 * k + 128, 128), 1)
            rows.append(jnp.where(lanes // 8 == tok, turned, 0.0))
        turned = pltpu.roll(line, lax.rem(lax.rem(tok, 4) * 32 + 64, 128), 1)
        turned = jnp.where(lanes // 32 == lax.rem(tok, 4), turned, 0.0)
        for k in range(4):
            rows.append(jnp.where(lax.div(tok, 4) == k, turned, jnp.zeros_like(turned)))
        rows.append(jnp.zeros((4, 128), F32))
        refs.small[...] = bfloat(jnp.concatenate(rows, axis=0))
        thin = [widen(ref[...]) for ref in (refs.w_query, refs.w_key, refs.w_value, refs.w_out)]
        wide, back = widen(refs.w_in[...]), refs.w_back[...]
        for half in range(2):
            span = columns(half)
            spread = [wide[:, columns(4 * half + k)] for k in range(4)]
            pieces = [thin[k][:, span] for k in range(3)] + spread[:3]
            refs.pack[half, 0:48, :] = bfloat(jnp.concatenate(pieces, axis=0))
            refs.pack[half, 48:80, :] = back[:, span]
            refs.pack[half, 80:96, :] = bfloat(
                jnp.concatenate([spread[3], thin[3][:, span]], axis=0)
            )
        swaps = [
            wire.swap(refs.pack.at[1 - core], refs.theirs),
            wire.swap(refs.small, refs.small_theirs),
        ]
        entry = refs.entry
        entry[wire.own, :] = refs.tokens[...]
        entry_copy = wire.swap(refs.tokens, entry.at[wire.own])
        for copy in swaps:
            copy.wait()

        def build(low, high):
            low, high = widen(low), widen(high)

            def both(row):
                return bfloat(jnp.concatenate([low[row : row + 8], high[row : row + 8]], axis=0))

            for k in range(3):
                refs.own_qkv[k] = both(8 * k)
                refs.own_rest[0, 16 * k : 16 * k + 16, :] = both(24 + 8 * k)
            back = bfloat(jnp.concatenate([low[48:80], high[48:80]], axis=0))
            refs.own_rest[1] = back[:48]
            refs.own_rest[2, 0:16, :] = both(80)
            refs.own_rest[2, 16:32, :] = back[48:]
            refs.own_rest[2, 32:48, :] = both(88)

        @pl.when(core == 0)
        def _():
            build(refs.pack[0], refs.theirs[...])

        @pl.when(core == 1)
        def _():
            build(refs.theirs[...], refs.pack[1])

        refs.own_small[...] = refs.small[...] + refs.small_theirs[...]

        def nothing(value):
            pass

        parts = [
            (refs.w_qkv, (k,), GATHER_ORDERS[k], refs.own_qkv.at[k], True, nothing)
            for k in range(3)
        ]
        parts.append((refs.all_small, (), GATHER_ORDERS[3], refs.own_small, False, nothing))
        first_stages = ring_gather(wire, parts)
        yours = pl.ds(2 * (1 - core), 2)
        passed = []

        def pass_two(value):
            passed.append(
                wire.swap(
                    refs.rest_two.at[yours, :, :, value], refs.yours_two.at[:, :, :, value]
                )
            )

        def pass_three(value):
            passed.append(
                wire.swap(
                    refs.rest_three.at[yours, value % 2, value // 2, :, pl.ds(16, 32)],
                    refs.yours_three.at[:, value % 2, value // 2],
                )
            )

        stages = ring_gather(
            wire,
            [
                (ref, (), GATHER_ORDERS[part], refs.own_rest.at[part], True, complete)
                for part, (ref, complete) in enumerate(
                    (
                        (refs.rest_one, nothing),
                        (refs.rest_two, pass_two),
                        (refs.rest_three, pass_three),
                    )
                )
            ],
        )
        for _ in range(2):
            advance(first_stages)
            advance(stages)
        for _ in first_stages:
            pass
        kept = wire.fetch(refs.w_qkv, refs.gqkv)
        for s in range(8):
            tile = jnp.zeros((16, 128), F32)
            for x_hi in range(2):
                for z in range(4):
                    tile = tile + widen(refs.all_small[s // 2, s % 2, x_hi, z])
            refs.vecs[:, 128 * s : 128 * s + 128] = tile[:8]
            for j in range(4):
                low = HALF * s + 128 * j
                refs.b_in[:, low : low + 128] = tile[8 + j : 9 + j]
        refs.keep(refs.vecs, refs.b_in)
        pending = project_rows(
            refs, wire, lambda k: refs.w_qkv[k].reshape(D, HALF), entry_copy, lambda: None
        )
        for copy in pending:
            copy.wait()
        refs.keep(refs.qkv)
        advance(stages)

        def between(slot):
            if slot == 2:
                advance(stages)

        attend_steps(refs, Mail(here, mail_send, mail_recv), between)
        for _ in stages:
            pass
        for copy in passed:
            copy.wait()
        kept.wait()

    scratch = dict(
        ATTEND_SCRATCH, pack=((2, 96, HALF), BF), small=((16, 128), BF), theirs=((96, HALF), BF),
        small_theirs=((16, 128), BF),
        own_qkv=((3, 16, HALF), BF), own_rest=((3, REST_ROWS, HALF), BF), own_small=((16, 128), BF),
        w_qkv=((3,) + CUBE + (16, HALF), BF), all_small=(CUBE + (16, 128), BF),
        qkv_rows=((3, CHIP_ROWS, HALF), BF), qkv_stage=((3,) + STAGE, BF),
    )
    rest = (CUBE + (REST_ROWS, HALF), BF)
    copies = 3 + 7 * GATHER_COPIES + 8 + 21
    return call(
        body, "opening", number, dict(vectors=vectors), dict(shards, tokens=tokens), {}, MIXED_T,
        dict(
            ATTEND_SAVED, entry=CHIP_BF, qkv=((3, HEAD, LENGTH), BF), vecs=((8, D), F32),
            b_in=((1, FF), F32),
        ),
        dict(
            chances=CHANCES, gqkv=((3,) + CUBE + (16, HALF), BF), rest_one=rest, rest_two=rest,
            rest_three=rest, yours_two=((2, 2, 2, 4, 48, HALF), BF),
            yours_three=((2, 2, 2, 4, 32, HALF), BF),
        ),
        scratch, [dma(copies), dma(copies), dma(11)] + MAIL_SEMS + [dma(SLOTS + 1)],
        dict(lengths=lengths, pads=pads),
    )


def closing(near, loaded, gqkv, rest_summed, number):
    def body(refs, semaphores):
        here = place()
        wire = Wire(here, *semaphores)
        core = wire.core
        planes = [
            wire.fetch(refs.rest_summed.at[at], refs.rest.at[at]) for at in rest_planes(here)
        ]
        weights = Weights(refs, wire, (QKV,))
        rest_slots = [
            [None] * 2 + [getattr(refs, "late_%d_%d" % (part, k)) for k in (2, 3)]
            for part in range(3)
        ]

        def keep_rest(part):
            def store(value):
                refs.sums_rest[part] = value

            return store

        rest_stages = ring_scatter(
            wire,
            [
                (refs.rest, (part,), SCATTER_ORDERS[part], True, rest_slots[part], keep_rest(part))
                for part in range(3)
            ],
            (1, 2),
        )
        greet(neighbours(here, (1, -1, 2)))
        refs.arrive()
        for copy in planes:
            copy.wait()
        advance(rest_stages)
        turn_gradients(refs)
        refs.sums[...] = refs.sums_three[...] + refs.sums_four[...]
        refs.sums_in[...] = refs.in_three[...] + refs.in_four[...]
        add_half(refs, wire, B_QUERY, row_sum(refs.d_qkv[0]))
        add_half(refs, wire, B_VALUE, row_sum(refs.d_qkv[2]))
        swaps = [wire.swap(refs.sums, refs.sums_come), wire.swap(refs.sums_in, refs.in_come)]
        for k in range(3):
            total = dot(refs.entry[...].T, refs.d_qkv[k])
            total = total + dot(refs.entry_later[...].T, refs.d_qkv_later[k])
            refs.gradients[k] = bfloat(total).reshape(CUBE + (16, HALF))
            if k == 1:
                advance(rest_stages)
        for copy in swaps:
            copy.wait()
        both = refs.sums[...] + refs.sums_come[...]
        both_in = refs.sums_in[...] + refs.in_come[...]
        for s in range(8):
            pieces = [both[:, 128 * s : 128 * s + 128]]
            for j in range(4):
                low = HALF * s + 128 * j
                pieces.append(both_in[:, low : low + 128])
            pieces.append(jnp.zeros((4, 128), F32))
            tile = bfloat(jnp.concatenate(pieces, axis=0))
            for x_hi in range(2):
                for z in range(4):
                    refs.small_sums[s // 2, s % 2, x_hi, z] = tile

        def keep(part):
            def store(value):
                if part == 3:
                    refs.tiny[...] = value
                else:
                    refs.final[part] = value

            return store

        arrivals = [
            [getattr(refs, "slot_%d_%d" % (part, k)) for k in range(4)] for part in range(4)
        ]
        parts = [
            (refs.gradients, (part,), SCATTER_ORDERS[part], True, arrivals[part], keep(part))
            for part in range(3)
        ]
        parts.append((refs.small_sums, (), SCATTER_ORDERS[3], False, arrivals[3], keep(3)))
        stages = ring_scatter(wire, parts, (0, 1, 2))
        advance(stages)
        for _ in rest_stages:
            pass
        advance(stages)
        refs.d_tokens[...] = bfloat(part_back_project(refs, wire, weights))
        for _ in stages:
            pass

        def finish(own):
            rest = refs.sums_rest
            rows = [refs.final[k, 8 * own : 8 * own + 8, :] for k in range(3)]
            rows.append(rest[2, 32 + 8 * own : 40 + 8 * own, :])
            for k in range(3):
                rows.append(rest[0, 16 * k + 8 * own : 16 * k + 8 * own + 8, :])
            rows.append(rest[2, 8 * own : 8 * own + 8, :])
            if own == 0:
                rows.append(rest[1, 0:32, :])
            else:
                rows += [rest[1, 32:48, :], rest[2, 16:32, :]]
            return jnp.concatenate(rows, axis=0)

        @pl.when(core == 0)
        def _():
            refs.leaving[...] = finish(1)
            refs.landed[0] = finish(0)

        @pl.when(core == 1)
        def _():
            refs.leaving[...] = finish(0)
            refs.landed[1] = finish(1)

        wire.swap(refs.leaving, refs.landed.at[core]).wait()
    few = ((8, D), F32)
    scratch = dict(
        outgoing=((4, ROWS, D), F32), incoming=((4, ROWS, D), F32), kept=ROW_F32,
        d_qkv=((3, CHIP_ROWS, HALF), BF), sums=few, sums_in=((1, FF), F32), sums_come=few,
        in_come=((1, FF), F32), gradients=((3,) + CUBE + (16, HALF), BF),
        small_sums=(CUBE + (16, 128), BF), final=((3, 16, HALF), F32),
        leaving=((96, HALF), F32), sums_rest=((3, REST_ROWS, HALF), F32),
        rest=((3,) + CUBE + (REST_ROWS, HALF), BF),
    )
    scratch.update(WEIGHT_SHAPES[QKV])
    for part in range(4):
        slots = scatter_slots(SCATTER_ORDERS[part], 16, part < 3)
        for k in range(4):
            scratch["slot_%d_%d" % (part, k)] = slots[k]
        if part < 3:
            slots = scatter_slots(SCATTER_ORDERS[part], REST_ROWS, True)
            for k in (2, 3):
                scratch["late_%d_%d" % (part, k)] = slots[k]
    copies = 4 * sum(SCATTER_COPIES) + 3 * sum(SCATTER_COPIES[1:]) + 4
    return call(
        body, "closing", number, near, loaded, dict(gqkv=gqkv, rest_summed=rest_summed),
        dict(
            d_tokens=((ROWS, D), BF), landed=((2, 96, HALF), F32), tiny=((16, 128), F32),
        ),
        {}, {}, scratch, [dma(copies), dma(copies), dma(4)],
    )


def unpack_kernel(
    result, d_tokens, landed, tiny, o_result, o_tokens, o_query, o_key, o_value, o_out, o_in, o_back,
    o_vectors,
):
    o_result[...] = result[...]
    o_tokens[...] = d_tokens[...]
    for column in (0, 1):
        span = columns(column)
        for piece, ref in enumerate((o_query, o_key, o_value, o_out)):
            ref[:, span] = landed[column, 8 * piece : 8 * piece + 8, :]
        for chunk in range(4):
            o_in[:, columns(4 * column + chunk)] = landed[
                column, 32 + 8 * chunk : 40 + 8 * chunk, :
            ]
        o_back[:, span] = landed[column, 64:96, :]
    tok = lax.axis_index("tok")
    o_vectors[0:8, :] = pltpu.roll(tiny[0:8, :], lax.rem(128 - tok * 8, 128), 1)
    wide = tiny[8:9, :]
    for k in range(1, 4):
        wide = jnp.where(lax.div(tok, 4) == k, tiny[8 + k : 9 + k, :], wide)
    wide = pltpu.roll(wide, lax.rem(128 - lax.rem(tok, 4) * 32, 128), 1)
    o_vectors[8:16, :] = jnp.broadcast_to(wide, (8, 128))


def unpack(result, d_tokens, landed, tiny):
    vmem = pl.BlockSpec(memory_space=pltpu.VMEM)
    few = ((8, D), F32)
    specs = (
        ((ROWS, D), BF), ((ROWS, D), BF), few, few, few, few, ((8, FF), F32), ((32, D), F32),
        ((16, 128), F32),
    )
    return pl.pallas_call(
        unpack_kernel,
        out_shape=tuple(jax.ShapeDtypeStruct(*spec) for spec in specs),
        in_specs=[vmem] * 4,
        out_specs=(vmem,) * len(specs),
        name="unpack",
        compiler_params=pltpu.CompilerParams(vmem_limit_bytes=16 * 2**20),
    )(result, d_tokens, landed, tiny)


def on_device(
    tokens, cotangent, doc_lengths, pad_counts, w_query, b_query, w_key, w_value, b_value, w_out,
    b_out, gain_attn, shift_attn, w_in, b_in, w_back, b_back, gain_ffn, shift_ffn,
):
    vectors = jnp.concatenate(
        [
            b_query, b_value, b_out, gain_attn, shift_attn, b_back, gain_ffn, shift_ffn, b_in,
            jnp.zeros((32,), BF),
        ]
    )
    one = opening(
        doc_lengths, pad_counts,
        dict(
            w_query=w_query, w_key=w_key, w_value=w_value, w_out=w_out, w_in=w_in, w_back=w_back
        ),
        widen(vectors)[None], tokens, 0,
    )
    two = dense(
        (POST, PROJECT), 2, one, dict(mixed_t=one.mixed_t), dict(hidden=tokens),
        dict(result=ROW_F32),
    )
    two_attend = attend(doc_lengths, pad_counts, two.qkv, 3)
    three = dense(
        (POST, BACK_DENSE), 4, one, dict(mixed_t=two_attend.mixed_t),
        dict(hidden=two.result, cotangent=cotangent), dict(result=((ROWS, D), BF)),
        ("normed_one", "factor_one", "normed_two", "factor_two", "slope"),
    )
    back_two = attend_back(
        dict(d_mixed=three.d_mixed),
        dict(qkv=two.qkv, mixed_head=two_attend.mixed_head, inverse=two_attend.inverse),
        two_attend.chances, 5,
    )
    four = dense(
        (BACK_PROJECT, BACK_DENSE), 6, one,
        dict(d_q_t=back_two.d_q_t, d_kv_t=back_two.d_kv_t),
        dict(
            d_inner=three.d_inner_out, normed_one=two.normed_one, factor_one=two.factor_one,
            normed_two=two.normed_two, factor_two=two.factor_two, slope=two.slope,
        ),
        {},
    )

    def gradient(one_former, one_latter, two_former, two_latter):
        former = jnp.concatenate([one_former, two_former], axis=0)
        latter = jnp.concatenate([one_latter, two_latter], axis=0)
        return bfloat(
            lax.dot_general(
                former, latter, (((0,), (0,)), ((), ())), preferred_element_type=F32
            )
        )

    half_cube = (2, 2, 2, 4)
    back_one = attend_back_scatter(
        dict(d_mixed=four.d_mixed),
        dict(qkv=one.qkv, mixed_head=one.mixed_head, inverse=one.inverse),
        one.chances,
        gradient(two.entry_two, four.d_before, three.entry_two, three.d_before).reshape(
            CUBE + (16, 2048)
        ),
        gradient(two.active, four.d_branch, three.active, three.d_branch).reshape(
            half_cube + (64, D)
        ),
        gradient(two.mixed, four.d_attn, three.mixed, three.d_attn).reshape(half_cube + (16, D)),
        7,
    )
    last = closing(
        dict(d_q_t=back_one.d_q_t, d_kv_t=back_one.d_kv_t),
        dict(
            d_inner=four.d_inner_out,
            entry=one.entry, entry_later=two.entry, d_qkv_later=four.d_qkv,
            sums_three=three.sums, sums_four=four.sums,
            in_three=three.sums_in, in_four=four.sums_in,
        ),
        one.gqkv, back_one.rest_summed, 8,
    )
    result, d_tokens, g_query, g_key, g_value, g_out, g_in, g_back, lines = unpack(
        three.result, last.d_tokens, last.landed, last.tiny
    )
    (
        g_b_query, g_b_value, g_b_out, g_gain_attn, g_shift_attn, g_b_back, g_gain_ffn, g_shift_ffn,
    ) = [lines[k, :8] for k in range(8)]
    return (
        result, d_tokens, g_query, g_b_query, g_key, g_value, g_b_value, g_out, g_b_out, g_gain_attn,
        g_shift_attn, g_in, lines[8, :32], g_back, g_b_back, g_gain_ffn, g_shift_ffn,
    )


def solution(mesh):
    both = ("seq", "tok")
    rows, vector = P(both, None), P(both)
    ins = (
        rows, rows, P("seq", None), P("seq"), rows, vector, rows, rows, vector, rows, vector, vector,
        vector, rows, vector, rows, vector, vector, vector,
    )
    outs = (
        rows, rows, rows, vector, rows, rows, vector, rows, vector, vector, vector, rows, vector,
        rows, vector, vector, vector,
    )
    return jax.shard_map(on_device, mesh=mesh, in_specs=ins, out_specs=outs, check_vma=False)
```

```python
import math
import types

import jax
import jax.numpy as jnp
from jax import lax
from jax.experimental import pallas as pl
from jax.experimental.pallas import tpu as pltpu
from jax.sharding import PartitionSpec as P

HEADS = 16
WINDOW = 1024
D = 1024
FF = 4096
HEAD = 64
CHIPS = 8
ROWS = 192
CHIP_ROWS = 2 * ROWS
LENGTH = CHIP_ROWS * CHIPS
HALF = 512
EPSILON = 1e-05
MASKED = -1e30
SCALE = 1.0 / math.sqrt(HEAD)
LOG2E = 1.4426950408889634
MESH = pl.DeviceIdType.MESH
BF = jnp.bfloat16
F32 = jnp.float32
CUBE = (4, 2, 2, 4)
X, Y, Z, CORE = range(4)


def bfloat(tensor):
    return tensor.astype(BF)


def widen(tensor):
    return tensor.astype(F32)


def place():
    seq, tok = lax.axis_index("seq"), lax.axis_index("tok")
    x = (tok // 8) * 2 + seq % 2
    return {X: x, Y: seq // 2, Z: (tok // 2) % 4, CORE: tok % 2}


def device(x, y, z, core):
    return (y * 2 + x % 2, (x // 2) * 8 + z * 2 + core)


def moved(here, axis, steps):
    there = dict(here)
    there[axis] = lax.rem(here[axis] + steps + 4, 4)
    return device(there[X], there[Y], there[Z], there[CORE])


def partner(here):
    return device(here[X], here[Y], here[Z], 1 - here[CORE])


def cube_index(here, whole, axis, value):
    index = []
    for name in (Y, X, Z):
        if name in whole:
            index += [slice(None)] * (2 if name == X else 1)
        else:
            at = value if name == axis else here[name]
            index += [at % 2, at // 2] if name == X else [at]
    return tuple(index)


def greet(targets):
    barrier = pltpu.get_barrier_semaphore()
    for target in targets:
        pl.semaphore_signal(barrier, inc=1, device_id=target, device_id_type=MESH)
    pl.semaphore_wait(barrier, len(targets))


def neighbours(here, steps):
    return [moved(here, axis, step) for axis in (X, Y, Z) for step in steps] + [partner(here)]


def group_device(here, number):
    seq = lax.axis_index("seq")
    return (seq, (number // 4) * 8 + (number % 4) * 2 + here[CORE])


def group_number(here):
    return (here[X] // 2) * 4 + here[Z]


def group(here):
    me = group_number(here)
    return [group_device(here, lax.rem(me + k, CHIPS)) for k in range(1, CHIPS)]


class Wire:
    def __init__(self, here, send, recv, local):
        self.send, self.recv, self.local = send, recv, local
        self.here, self.number, self.locals = here, 0, 0
        self.core, self.me = here[CORE], group_number(here)
        self.own = pl.ds(pl.multiple_of(self.core * ROWS, ROWS), ROWS)
        self.other = pl.ds(pl.multiple_of((1 - self.core) * ROWS, ROWS), ROWS)

    def to(self, source, target, device_id):
        copy = pltpu.make_async_remote_copy(
            src_ref=source,
            dst_ref=target,
            send_sem=self.send.at[self.number],
            recv_sem=self.recv.at[self.number],
            device_id=device_id,
            device_id_type=MESH,
        )
        self.number += 1
        copy.start()
        return copy

    def swap(self, source, target):
        return self.to(source, target, partner(self.here))

    def fetch(self, source, target):
        copy = pltpu.make_async_copy(source, target, self.local.at[self.locals])
        self.locals += 1
        copy.start()
        return copy

    def spread(self, stage, target):
        span = chunk_span(self.me)
        copies = []
        for k in range(1, CHIPS):
            to = lax.rem(self.me + k, CHIPS)
            copies.append(self.to(stage.at[to], target.at[:, span], group_device(self.here, to)))
        copies.append(self.fetch(stage.at[self.me], target.at[:, span]))
        return copies


def chunk_span(number):
    return pl.ds(pl.multiple_of(number * CHIP_ROWS, CHIP_ROWS), CHIP_ROWS)


EVERY = slice(None)
CUBE_ALL = (EVERY,) * 4


def side_columns(width, side):
    return pl.ds(side * (width // 2), width // 2)


SIZES = {Y: (4,), X: (2, 2), Z: (4,)}
GATHER_ORDERS = ((X, Z, Y), (Y, X, Z), (Z, Y, X), (X, Z, Y))
SCATTER_ORDERS = ((Y, Z, X), (Z, X, Y), (X, Y, Z), (Y, Z, X))


def ring_gather(wire, parts):
    here = wire.here
    sent, kept = [], []
    for buffer, prefix, order, own, _, _ in parts:
        kept.append(wire.fetch(own, buffer.at[prefix + cube_index(here, (), None, None)]))
    for phase in range(2):
        copies = []
        for step in (1, -1, 2):
            for buffer, prefix, order, own, _, _ in parts:
                axis = order[phase]
                block = buffer.at[prefix + cube_index(here, order[:phase], axis, here[axis])]
                source = own if phase == 0 else block
                copies.append(wire.to(source, block, moved(here, axis, step)))
        yield
        for copy in copies:
            copy.wait_recv()
        sent += copies
        if phase == 0:
            for copy in kept:
                copy.wait()
    one, two = [], []
    for buffer, prefix, order, _, _, complete in parts:
        axis = order[2]
        block = buffer.at[prefix + cube_index(here, order[:2], axis, here[axis])]
        one.append([wire.to(block, block, moved(here, axis, step)) for step in (1, -1)])
    for _, _, order, _, _, complete in parts:
        complete(here[order[2]])
    yield
    for (buffer, prefix, order, _, cut, complete), pair in zip(parts, one):
        axis = order[2]
        for side, step in enumerate((1, -1)):
            pair[side].wait_recv()
            come = lax.rem(here[axis] - step + 4, 4)
            index = prefix + cube_index(here, order[:2], axis, come)
            if cut:
                index += (EVERY, side_columns(cut, side))
            if cut or side == 0:
                block = buffer.at[index]
                two.append(wire.to(block, block, moved(here, axis, step)))
            complete(come)
        sent += pair
    yield
    for copy in two:
        copy.wait_recv()
    for _, _, order, _, _, complete in parts:
        complete(lax.rem(here[order[2]] + 2, 4))
    for copy in sent + two:
        copy.wait_send()


GATHER_COPIES = 3 + 3 + 4


def lengths_of(full):
    return tuple(n for name in (Y, X, Z) if name in full for n in SIZES[name])


def digits_of(i, lengths):
    digits = []
    for length in reversed(lengths):
        digits.append(lax.rem(i, length))
        i = lax.div(i, length)
    return tuple(digits[::-1])


def one_chip(here, full, axis, value, digits):
    digits, index = list(digits), []
    for name in (Y, X, Z):
        if name in full:
            index += [digits.pop(0) for _ in SIZES[name]]
        else:
            at = value if name == axis else here[name]
            index += [at % 2, at // 2] if name == X else [at]
    return tuple(index)


SCATTER_COPIES = (4, 3, 3)


def scatter_slots(order, rows, wide, cut):
    dims = lengths_of(order[1:])
    slots = [
        pltpu.VMEM((2,) + dims + (rows, wide // 2 if cut else wide), BF),
        pltpu.VMEM((2,) + dims + (rows, wide), BF),
    ]
    return slots + [
        pltpu.VMEM((3,) + lengths_of(order[phase + 1 :]) + (rows, wide), BF) for phase in (1, 2)
    ]


def ring_scatter(wire, parts, phases):
    here = wire.here
    sent = []
    for phase in phases:
        ahead, arriving = [], []
        for buffer, prefix, order, cut, slots, _ in parts:
            axis, full = order[phase], order[phase + 1 :]
            row = []
            if phase == 0:
                far = prefix + cube_index(here, full, axis, lax.rem(here[axis] + 2, 4))
                for side, step in enumerate((1, -1)):
                    if cut or side == 0:
                        block = buffer.at[far + ((EVERY, side_columns(cut, side)) if cut else ())]
                        row.append(wire.to(block, slots[0].at[side], moved(here, axis, step)))
                ahead.append(row)
            else:
                for k, step in enumerate((1, -1, 2)):
                    value = lax.rem(here[axis] + step + 4, 4)
                    block = buffer.at[prefix + cube_index(here, full, axis, value)]
                    row.append(
                        wire.to(block, slots[1 + phase].at[k], moved(here, axis, step))
                    )
                arriving.append(row)
            sent += row
        yield
        if phase == 0:
            for (buffer, prefix, order, cut, slots, _), row in zip(parts, ahead):
                axis, full = order[phase], order[phase + 1 :]
                pair = []
                for side, step in enumerate((1, -1)):
                    value = lax.rem(here[axis] + step + 4, 4)
                    if side < len(row):
                        row[side].wait_recv()
                        half = slots[0]
                        columns_ = side_columns(cut, side) if cut else EVERY

                        def add(
                            i, _, buffer=buffer, prefix=prefix, axis=axis, full=full, value=value,
                            half=half, side=side, columns_=columns_,
                        ):
                            digits = digits_of(i, lengths_of(full))
                            at = prefix + one_chip(here, full, axis, value, digits)
                            at += (EVERY, columns_)
                            buffer[at] = bfloat(widen(buffer[at]) + widen(half[(side,) + digits]))
                            return 0

                        lax.fori_loop(0, math.prod(lengths_of(full)), add, 0)
                    block = buffer.at[prefix + cube_index(here, full, axis, value)]
                    pair.append(wire.to(block, slots[1].at[side], moved(here, axis, step)))
                arriving.append(pair)
                sent += pair
            yield
        for (buffer, prefix, order, _, slots, final), row in zip(parts, arriving):
            axis, full = order[phase], order[phase + 1 :]
            come = slots[1 + phase]
            for copy in row:
                copy.wait_recv()

            def total(
                i, _, buffer=buffer, prefix=prefix, axis=axis, full=full, come=come, final=final,
                count=len(row),
            ):
                digits = digits_of(i, lengths_of(full))
                at = prefix + one_chip(here, full, axis, here[axis], digits)
                value = widen(buffer[at])
                for k in range(count):
                    value = value + widen(come[(k,) + digits])
                if phase < 2:
                    buffer[at] = bfloat(value)
                else:
                    final(value)
                return 0

            lax.fori_loop(0, math.prod(lengths_of(full)), total, 0)
    for copy in sent:
        copy.wait_send()


def advance(stages, count=1):
    for _ in range(count):
        next(stages, None)


class Mail:
    def __init__(self, here, send, recv):
        self.here, self.me, self.send, self.recv = here, group_number(here), send, recv
        self.count = 0
        self.sent = []

    def to(self, number, source, target):
        copy = pltpu.make_async_remote_copy(
            src_ref=source,
            dst_ref=target,
            send_sem=self.send.at[self.count],
            recv_sem=self.recv.at[self.me],
            device_id=group_device(self.here, number),
            device_id_type=MESH,
        )
        self.count += 1
        copy.start()
        self.sent.append(copy)

    def finish(self, source, target):
        for k in range(1, CHIPS):
            sender = lax.rem(self.me + k, CHIPS)
            pltpu.make_async_remote_copy(
                src_ref=source,
                dst_ref=target,
                send_sem=self.send.at[0],
                recv_sem=self.recv.at[sender],
                device_id=group_device(self.here, sender),
                device_id_type=MESH,
            ).wait_recv()
        for copy in self.sent:
            copy.wait_send()


BLOCK = 256
SPAN = 1280
STEPS = LENGTH // BLOCK
SLOTS = 4
LAST_START = LENGTH - SPAN


def limits(bounds, first, count):
    places = first + lax.broadcasted_iota(jnp.int32, (1, count), 1)
    low = jnp.maximum(places - (WINDOW // 2 - 1), 0)
    high = jnp.minimum(places + WINDOW // 2, LENGTH)
    for bound in bounds:
        low = jnp.maximum(low, jnp.where(bound <= places, bound, 0))
        high = jnp.minimum(high, jnp.where(bound > places, bound, LENGTH))
    return low, high


def dot(former, latter):
    return jnp.dot(former, latter, preferred_element_type=F32)


def attend_steps(refs, mail, between):
    qkv, mixed_t, mixed, inverse = refs.qkv, refs.mixed_t, refs.mixed_head, refs.inverse
    live, end, bounds = LENGTH - refs.pads[0], 0, []
    for k in range(4):
        end = end + refs.lengths[0, k]
        bounds.append(jnp.minimum(end, live))
    kv, ones_v, chances, stage, local = refs.kv, refs.ones_v, refs.held, refs.mixed_stage, refs.attend_local
    me = mail.me
    kv[...] = jnp.concatenate([qkv[1], qkv[2]], axis=0).T
    ones_v[0:HEAD, :] = jnp.ones((HEAD, LENGTH), BF)
    ones_v[HEAD:, :] = qkv[2]
    kept = []

    def step(i):
        first = pl.multiple_of(i * BLOCK, BLOCK)
        start = pl.multiple_of(jnp.clip(first - 512, 0, LAST_START), BLOCK)
        queries = qkv[0, :, pl.ds(first, BLOCK)]
        padded = jnp.concatenate([queries, jnp.zeros_like(queries)], axis=0)
        scores = dot(kv[pl.ds(start, SPAN), :], padded)
        low, high = limits(bounds, first, BLOCK)
        places = start + lax.broadcasted_iota(jnp.int32, (SPAN, BLOCK), 0)
        scores = jnp.where((places >= low) & (places < high), scores, MASKED)
        highest = jnp.max(scores, axis=0, keepdims=True)
        raised = bfloat(jnp.exp2((scores - highest) * (SCALE * LOG2E)))
        chances[i] = raised
        out = dot(ones_v[:, pl.ds(start, SPAN)], raised)
        back = 1.0 / out[0:1]
        result = out[HEAD:] * back
        mixed[:, pl.ds(first, BLOCK)] = result
        stage[:, pl.ds(first, BLOCK)] = bfloat(result)
        inverse[:, pl.ds(first, BLOCK)] = back

    for slot in range(SLOTS):
        pair = lax.rem(me // 2 + 1 + slot, SLOTS)

        def run(t, _, pair=pair):
            step(pair * 3 + t)
            return 0

        lax.fori_loop(0, 3, run, 0)
        blocks = pl.ds(pair * 3, 3)
        copy = pltpu.make_async_copy(chances.at[blocks], refs.chances.at[blocks], local.at[slot])
        copy.start()
        kept.append(copy)
        if slot < SLOTS - 1:
            for number in (2 * pair, 2 * pair + 1):
                mail.to(number, stage.at[:, chunk_span(number)], mixed_t.at[me])
        else:
            number = me + 1 - 2 * (me % 2)
            mail.to(number, stage.at[:, chunk_span(number)], mixed_t.at[me])
            copy = pltpu.make_async_copy(
                stage.at[:, chunk_span(me)], mixed_t.at[me], local.at[SLOTS]
            )
            copy.start()
            kept.append(copy)
        between(slot)
    refs.keep(mixed, inverse)
    for copy in kept:
        copy.wait()
    mail.finish(stage.at[:, chunk_span(me)], mixed_t.at[me])


MIXED_T = dict(mixed_t=((CHIPS, HEAD, CHIP_ROWS), BF))
ATTEND_SAVED = dict(mixed_head=((HEAD, LENGTH), F32), inverse=((1, LENGTH), F32))
CHANCES = ((STEPS, SPAN, BLOCK), BF)
ATTEND_SCRATCH = dict(
    kv=((LENGTH, 2 * HEAD), BF), ones_v=((2 * HEAD, LENGTH), BF), held=CHANCES,
    mixed_stage=((HEAD, LENGTH), BF),
)
MAIL_SEMS = [pltpu.SemaphoreType.DMA((CHIPS - 1,)), pltpu.SemaphoreType.DMA((CHIPS,))]


def call(
    body, name, number, near, loaded, sources, outputs, saved, far, scratch, semaphores, scalars={}
):
    vmem, hbm = pl.BlockSpec(memory_space=pltpu.VMEM), pl.BlockSpec(memory_space=pltpu.HBM)
    smem = pl.BlockSpec(memory_space=pltpu.SMEM)
    scratch = dict(scratch)
    for key, value in loaded.items():
        scratch[key] = (value.shape, value.dtype)
    scratch.update(saved)
    specs = [*outputs.values(), *saved.values(), *far.values()]

    def size(shape, dtype):
        rows, lanes = (1,) * (2 - len(shape[-2:])) + tuple(shape[-2:])
        rows, lanes = -(-rows // 8) * 8, -(-lanes // 128) * 128
        return math.prod(shape[:-2]) * rows * lanes * jnp.dtype(dtype).itemsize

    held = [(value.shape, value.dtype) for value in near.values()] + list(outputs.values())
    held += [s if isinstance(s, tuple) else (s.shape, s.dtype) for s in scratch.values()]
    limit = sum(size(*spec) for spec in held) + 10 * 2**20

    def kernel(*values):
        values = list(values)

        def take(names):
            return {key: values.pop(0) for key in names}

        refs = types.SimpleNamespace(**take(scalars), **take(near))
        heres = take(loaded)
        for key, ref in take(sources).items():
            setattr(refs, key, ref)
        for key, ref in take(outputs).items():
            setattr(refs, key, ref)
        outs = take(saved)
        for names in (far, scratch):
            for key, ref in take(names).items():
                setattr(refs, key, ref)
        copies = values.pop(0)
        pending = [
            pltpu.make_async_copy(ref, getattr(refs, key), copies.at[k])
            for k, (key, ref) in enumerate(heres.items())
        ]
        for copy in pending:
            copy.start()
        kept = []

        def arrive():
            for copy in pending:
                copy.wait()

        def keep(*arrays):
            for k, (key, out) in enumerate(outs.items()):
                if any(getattr(refs, key) is array for array in arrays):
                    copy = pltpu.make_async_copy(
                        getattr(refs, key), out, copies.at[len(heres) + k]
                    )
                    copy.start()
                    kept.append(copy)

        refs.arrive, refs.keep = arrive, keep
        body(refs, values)
        for copy in kept:
            copy.wait()

    results = pl.pallas_call(
        kernel,
        out_shape=tuple(jax.ShapeDtypeStruct(*spec) for spec in specs),
        in_specs=[smem] * len(scalars)
        + [vmem] * len(near)
        + [hbm] * (len(loaded) + len(sources)),
        out_specs=(vmem,) * len(outputs) + (hbm,) * (len(saved) + len(far)),
        scratch_shapes=[
            pltpu.VMEM(*spec) if isinstance(spec, tuple) else spec for spec in scratch.values()
        ]
        + [dma(max(1, len(loaded) + len(saved)))]
        + list(semaphores),
        name=name,
        compiler_params=pltpu.CompilerParams(
            collective_id=number, has_side_effects=True, vmem_limit_bytes=max(limit, 58 * 2**20)
        ),
    )(*scalars.values(), *near.values(), *loaded.values(), *sources.values())
    return types.SimpleNamespace(**dict(zip([*outputs, *saved, *far], results)))


def dma(count):
    return pltpu.SemaphoreType.DMA((count,))


PAD = 2 * BLOCK
PADDED = LENGTH + 2 * PAD


def fetch_chances(refs):
    copies = []
    for slot in range(SLOTS):
        blocks = pl.ds(slot * 3, 3)
        copy = pltpu.make_async_copy(
            refs.chances.at[blocks], refs.held.at[blocks], refs.attend_local.at[slot]
        )
        copy.start()
        copies.append(copy)
    refs.early = copies


def attend_back_steps(refs, mail_q, mail_kv, between):
    qkv, mixed, inverse, d_mixed = refs.qkv, refs.mixed_head, refs.inverse, refs.d_mixed
    d_q_t, d_kv_t, chances, kv = refs.d_q_t, refs.d_kv_t, refs.held, refs.kv
    rows_q, rows_d, turned_d, shift = refs.rows_q, refs.rows_d, refs.turned_d, refs.shift
    total_q, stage_q, stage_kv = refs.total_q, refs.stage_q, refs.stage_kv
    me = mail_q.me
    kv[...] = jnp.concatenate([qkv[1], qkv[2]], axis=0).T
    scaled = bfloat(widen(d_mixed[...]) * inverse[...])
    inner = jnp.sum(widen(scaled) * mixed[...], axis=0, keepdims=True)
    for edge in (0, PAD + LENGTH):
        shift[:, edge : edge + PAD] = jnp.zeros((1, PAD), F32)
        turned_d[:, edge : edge + PAD] = jnp.zeros((2 * HEAD, PAD), BF)
        rows_q[edge : edge + PAD, :] = jnp.zeros((PAD, 2 * HEAD), BF)
        rows_d[edge : edge + PAD, :] = jnp.zeros((PAD, 2 * HEAD), BF)
    middle = slice(PAD, PAD + LENGTH)
    shift[:, middle] = inner
    turned_d[0:HEAD, middle] = jnp.zeros((HEAD, LENGTH), BF)
    turned_d[HEAD:, middle] = scaled
    both = jnp.concatenate([qkv[0], scaled], axis=0).T
    left = lax.broadcasted_iota(jnp.int32, both.shape, 1) < HEAD
    rows_q[middle, :] = jnp.where(left, both, jnp.zeros_like(both))
    rows_d[middle, :] = jnp.where(left, jnp.zeros_like(both), both)
    total_q[...] = jnp.zeros_like(total_q)
    for copy in refs.early:
        copy.wait()
    between(-1)

    def step(i):
        first = pl.multiple_of(i * BLOCK, BLOCK)
        keys = pl.ds(first, BLOCK)
        span = pl.ds(first, SPAN)
        tiles = []
        for t in range(5):
            block = jnp.clip(i - 2 + t, 0, STEPS - 1)
            start = jnp.clip(block * BLOCK - 512, 0, LAST_START)
            offset = pl.multiple_of(jnp.clip(first - start, 0, SPAN - BLOCK), BLOCK)
            tiles.append(chances[block, pl.ds(offset, BLOCK), :])
        weights = jnp.concatenate(tiles, axis=1)
        grad_weights = dot(kv[keys, :], turned_d[:, span])
        grad_scores = bfloat(widen(weights) * (grad_weights - shift[:, span]))
        total = dot(weights, rows_d[span, :]) + dot(grad_scores, rows_q[span, :])
        total_q[:, span] += dot(qkv[1, :, keys], grad_scores)
        turned = total.T
        stage_kv[0:HEAD, keys] = bfloat(turned[:HEAD] * SCALE)
        stage_kv[HEAD:, keys] = bfloat(turned[HEAD:])

    def send_queries(number):
        span = pl.ds(pl.multiple_of(number * CHIP_ROWS + PAD, 128), CHIP_ROWS)
        stage_q[number] = bfloat(total_q[:, span] * SCALE)
        mail_q.to(number, stage_q.at[number], d_q_t.at[me])

    near = me + 1 - 2 * (me % 2)
    for slot in range(SLOTS):
        pair = lax.rem(me // 2 + 1 + slot, SLOTS)

        def run(t, _, pair=pair):
            step(pair * 3 + t)
            return 0

        lax.fori_loop(0, 3, run, 0)
        if slot < SLOTS - 1:
            for number in (2 * pair, 2 * pair + 1):
                mail_kv.to(number, stage_kv.at[:, chunk_span(number)], d_kv_t.at[me])
        else:
            mail_kv.to(near, stage_kv.at[:, chunk_span(near)], d_kv_t.at[me])
        if slot == 2:
            complete = lax.rem(me // 2 + 2, SLOTS)
            send_queries(2 * complete)
            send_queries(2 * complete + 1)
        between(slot)
    for rest in (1, 3):
        pair = lax.rem(me // 2 + rest, SLOTS)
        send_queries(2 * pair)
        send_queries(2 * pair + 1)
    send_queries(near)
    span = pl.ds(pl.multiple_of(me * CHIP_ROWS + PAD, 128), CHIP_ROWS)
    d_q_t[me] = bfloat(total_q[:, span] * SCALE)
    d_kv_t[me] = stage_kv[:, chunk_span(me)]
    mail_kv.finish(stage_kv.at[:, chunk_span(me)], d_kv_t.at[me])
    mail_q.finish(stage_q.at[me], d_q_t.at[me])


BACK_SCRATCH = dict(
    held=CHANCES, kv=((LENGTH, 2 * HEAD), BF), rows_q=((PADDED, 2 * HEAD), BF),
    rows_d=((PADDED, 2 * HEAD), BF), turned_d=((2 * HEAD, PADDED), BF), shift=((1, PADDED), F32),
    total_q=((HEAD, PADDED), F32), stage_q=((CHIPS, HEAD, CHIP_ROWS), BF),
    stage_kv=((2 * HEAD, LENGTH), BF),
)
BACK_OUTPUTS = dict(
    d_q_t=((CHIPS, HEAD, CHIP_ROWS), BF), d_kv_t=((CHIPS, 2 * HEAD, CHIP_ROWS), BF)
)


REST = ((64, HALF), (80, HALF // 2), (80, HALF // 2))


def dot_nt(former, latter):
    return lax.dot_general(former, latter, (((1,), (1,)), ((), ())), preferred_element_type=F32)


QKV, OUT, IN, BACK = range(4)


class Weights:
    def __init__(self, refs, wire, names):
        core = wire.core
        mine = pl.ds(2 * core, 2)
        own = (mine,) + (EVERY,) * 3
        self.refs, self.pending = refs, {}
        for name in names:
            if name == QKV:
                pairs = [(refs.gqkv, refs.w_qkv)]
            elif name == IN:
                pairs = [
                    (refs.rest_one.at[CUBE_ALL + (pl.ds(16 * k, 16),)], refs.w_in.at[k])
                    for k in range(4)
                ]
            else:
                rows, target = (pl.ds(0, 64), refs.w_back) if name == BACK else (pl.ds(64, 16), refs.w_out)
                pairs = []
                for part, (ref, come) in enumerate(
                    ((refs.rest_two, refs.yours_two), (refs.rest_three, refs.yours_three))
                ):
                    span = (EVERY,) * 5 + (side_columns(HALF, part),)
                    pairs.append((ref.at[own + (rows,)], target.at[(core,) + span]))
                    pairs.append((come.at[CUBE_ALL + (rows,)], target.at[(1 - core,) + span]))
            self.pending[name] = [wire.fetch(*pair) for pair in pairs]

    def ready(self, name):
        for copy in self.pending.pop(name, []):
            copy.wait()

    def qkv(self, k):
        self.ready(QKV)
        return self.refs.w_qkv[k].reshape(D, HALF)

    def out(self, half):
        self.ready(OUT)
        return self.refs.w_out[half].reshape(HALF, HALF)

    def into(self, chunk):
        self.ready(IN)
        return self.refs.w_in[chunk].reshape(D, HALF)

    def back(self, half, chunk):
        self.ready(BACK)
        return self.refs.w_back[half, chunk // 2, chunk % 2].reshape(HALF, HALF)


def columns(k):
    return slice(k * HALF, k * HALF + HALF)


def vector(refs, k):
    return refs.vecs[k : k + 1, :]


def half_vector(refs, core, k):
    return refs.vecs[k : k + 1, pl.ds(pl.multiple_of(core * HALF, HALF), HALF)]


B_QUERY, B_VALUE, B_OUT, GAIN_ATTN, SHIFT_ATTN, B_BACK, GAIN_FFN, SHIFT_FFN = range(8)


def normalized(tensor):
    centred = tensor - jnp.mean(tensor, axis=-1, keepdims=True)
    factor = lax.rsqrt(jnp.mean(centred * centred, axis=-1, keepdims=True) + EPSILON)
    return centred * factor, factor


def normalize_back(grad_out, normed, factor, gain):
    grad_normed = grad_out * gain
    grad_input = factor * (
        grad_normed
        - jnp.mean(grad_normed, axis=-1, keepdims=True)
        - normed * jnp.mean(grad_normed * normed, axis=-1, keepdims=True)
    )
    return (
        grad_input,
        jnp.sum(grad_out * normed, axis=0, keepdims=True),
        jnp.sum(grad_out, axis=0, keepdims=True),
    )


def row_sum(tensor):
    return jnp.sum(widen(tensor), axis=0, keepdims=True)


def gelu_pair(v):
    root = math.sqrt(2.0 / math.pi)
    squared = v * v
    bent = jnp.tanh(root * v * (1.0 + 0.044715 * squared))
    half = 0.5 + 0.5 * bent
    slope = half + (0.5 * root) * v * (1.0 - bent * bent) * (1.0 + (3 * 0.044715) * squared)
    return v * half, slope


def summed_over_cores(refs, wire, fill):
    send, come, kept = refs.outgoing.at[refs.round], refs.incoming.at[refs.round], refs.kept
    refs.round += 1
    fill(wire.other, send)
    copy = wire.swap(send, come)
    fill(wire.own, kept)
    copy.wait()
    return kept[...] + come[...]


def project_rows(refs, wire, weight, copy, between):
    entry, rows_of, stage = refs.entry, refs.qkv_rows, refs.qkv_stage
    biases = (half_vector(refs, wire.core, B_QUERY), None, half_vector(refs, wire.core, B_VALUE))

    def project(rows, k):
        result = dot(entry[rows, :], weight(k))
        if biases[k] is not None:
            result = result + biases[k]
        rows_of[k, rows, :] = bfloat(result)

    for k in range(3):
        project(wire.own, k)
    copy.wait()
    refs.keep(entry)
    between()
    copies = []
    for k in range(3):
        project(wire.other, k)
        stage[k] = rows_of[k].T.reshape(CHIPS, HEAD, CHIP_ROWS)
        copies += wire.spread(stage.at[k], refs.qkv.at[k])
    return copies


def part_project(refs, wire, weights, hidden):
    entry = refs.entry
    entry[wire.own, :] = bfloat(hidden)
    copy = wire.swap(entry.at[wire.own], entry.at[wire.own])
    return project_rows(refs, wire, weights.qkv, copy, lambda: None)


def part_post(refs, wire, weights):
    mixed = refs.mixed
    mixed[...] = refs.mixed_t_in[...].reshape(HALF, CHIP_ROWS).T

    def leave(rows, target):
        for half in range(2):
            target[:, columns(half)] = dot(mixed[rows, :], weights.out(half))

    branch = summed_over_cores(refs, wire, leave)
    normed, factor = normalized(widen(refs.hidden[...]) + branch + vector(refs, B_OUT))
    refs.normed_one[...] = normed
    refs.factor_one[...] = factor
    refs.keep(refs.normed_one, refs.factor_one)
    first = normed * vector(refs, GAIN_ATTN) + vector(refs, SHIFT_ATTN)
    refs.first[...] = first
    entry_two, active, slope = refs.entry_two, refs.active, refs.slope
    entry_two[wire.own, :] = bfloat(first)
    copy = wire.swap(entry_two.at[wire.own], entry_two.at[wire.own])

    def inner(rows):
        for chunk in range(4):
            start = pl.multiple_of(wire.core * 2048 + chunk * HALF, HALF)
            before = dot(entry_two[rows, :], weights.into(chunk)) + refs.b_in[:, pl.ds(start, HALF)]
            value, steep = gelu_pair(before)
            active[rows, columns(chunk)] = bfloat(value)
            slope[rows, columns(chunk)] = bfloat(steep)

    inner(wire.own)
    copy.wait()
    refs.keep(entry_two)
    inner(wire.other)
    refs.keep(active, slope)

    def leave_two(rows, target):
        for half in range(2):
            total = dot(active[rows, columns(0)], weights.back(half, 0))
            for chunk in range(1, 4):
                total = total + dot(active[rows, columns(chunk)], weights.back(half, chunk))
            target[:, columns(half)] = total

    second = summed_over_cores(refs, wire, leave_two)
    normed, factor = normalized(refs.first[...] + second + vector(refs, B_BACK))
    refs.normed_two[...] = normed
    refs.factor_two[...] = factor
    refs.keep(refs.normed_two, refs.factor_two)
    return normed * vector(refs, GAIN_FFN) + vector(refs, SHIFT_FFN)


def part_back_dense(refs, wire, weights, grad_out):
    d_branch, d_before, d_attn = refs.d_branch, refs.d_before, refs.d_attn
    sums = refs.sums
    d_second, g_gain, g_shift = normalize_back(
        grad_out, refs.normed_two[...], refs.factor_two[...], vector(refs, GAIN_FFN)
    )
    refs.d_second[...] = d_second
    d_branch[wire.own, :] = bfloat(d_second)
    copy = wire.swap(d_branch.at[wire.own], d_branch.at[wire.own])
    sums[GAIN_FFN : GAIN_FFN + 1, :] = g_gain
    sums[SHIFT_FFN : SHIFT_FFN + 1, :] = g_shift
    sums[B_BACK : B_BACK + 1, :] = row_sum(d_branch[wire.own, :])

    def inner(rows):
        for chunk in range(4):
            d_active = dot_nt(d_branch[rows, columns(0)], weights.back(0, chunk)) + dot_nt(
                d_branch[rows, columns(1)], weights.back(1, chunk)
            )
            d_before[rows, columns(chunk)] = bfloat(
                d_active * widen(refs.slope[rows, columns(chunk)])
            )

    inner(wire.own)
    copy.wait()
    refs.keep(d_branch)
    inner(wire.other)
    refs.keep(d_before)
    for chunk in range(4):
        start = pl.multiple_of(wire.core * 2048 + chunk * HALF, HALF)
        refs.sums_in[:, pl.ds(start, HALF)] = row_sum(d_before[:, columns(chunk)])

    def leave(rows, target):
        total = dot_nt(d_before[rows, columns(0)], weights.into(0))
        for chunk in range(1, 4):
            total = total + dot_nt(d_before[rows, columns(chunk)], weights.into(chunk))
        target[...] = total

    d_first = refs.d_second[...] + summed_over_cores(refs, wire, leave)
    d_inner, g_gain, g_shift = normalize_back(
        d_first, refs.normed_one[...], refs.factor_one[...], vector(refs, GAIN_ATTN)
    )
    refs.d_inner_out[...] = d_inner
    refs.keep(refs.d_inner_out)
    d_attn[wire.own, :] = bfloat(d_inner)
    copy = wire.swap(d_attn.at[wire.own], d_attn.at[wire.own])
    sums[GAIN_ATTN : GAIN_ATTN + 1, :] = g_gain
    sums[SHIFT_ATTN : SHIFT_ATTN + 1, :] = g_shift
    sums[B_OUT : B_OUT + 1, :] = row_sum(d_attn[wire.own, :])
    rows_of, stage = refs.d_mixed_rows, refs.d_mixed_stage

    def enter(rows):
        rows_of[rows, :] = bfloat(
            dot_nt(d_attn[rows, columns(0)], weights.out(0))
            + dot_nt(d_attn[rows, columns(1)], weights.out(1))
        )

    enter(wire.own)
    copy.wait()
    refs.keep(d_attn, refs.sums, refs.sums_in)
    enter(wire.other)
    stage[...] = rows_of[...].T.reshape(CHIPS, HEAD, CHIP_ROWS)
    return wire.spread(stage, refs.d_mixed)


def turn_gradients(refs):
    rows_of = refs.d_qkv
    rows_of[0] = refs.d_q_t[...].reshape(HALF, CHIP_ROWS).T
    rows_of[1] = refs.d_kv_t[:, :HEAD, :].reshape(HALF, CHIP_ROWS).T
    rows_of[2] = refs.d_kv_t[:, HEAD:, :].reshape(HALF, CHIP_ROWS).T


def add_half(refs, wire, k, value):
    half = pl.ds(pl.multiple_of(wire.core * HALF, HALF), HALF)
    refs.sums[k : k + 1, half] = refs.sums[k : k + 1, half] + value


def part_back_project(refs, wire, weights):
    rows_of = refs.d_qkv

    def leave(rows, target):
        total = dot_nt(rows_of[0, rows, :], weights.qkv(0))
        for k in range(1, 3):
            total = total + dot_nt(rows_of[k, rows, :], weights.qkv(k))
        target[...] = total

    return refs.d_inner[...] + summed_over_cores(refs, wire, leave)


ROW_F32 = ((ROWS, D), F32)
COLUMN_F32 = ((ROWS, 1), F32)
CHIP_BF = ((CHIP_ROWS, D), BF)
WIDE_BF = ((CHIP_ROWS, 2048), BF)
HEADS_BF = ((CHIP_ROWS, HALF), BF)
STAGE = (CHIPS, HEAD, CHIP_ROWS)
PROJECT, POST, BACK_DENSE, BACK_PROJECT, ATTEND, ATTEND_BACK, GRADIENTS = range(7)
WHOLE_GRADIENTS = dict(
    g_in=(CUBE + (16, 2048), BF), g_back=((2, 2, 2, 4, 64, D), BF), g_out=((2, 2, 2, 4, 16, D), BF)
)
PARTS = (
    (
        (QKV,),
        dict(entry=CHIP_BF, qkv=((3, HEAD, LENGTH), BF)),
        {},
        dict(qkv_rows=((3, CHIP_ROWS, HALF), BF), qkv_stage=((3,) + STAGE, BF)),
        1 + 3 * 7,
        3,
    ),
    (
        (OUT, IN, BACK),
        dict(
            normed_one=ROW_F32, factor_one=COLUMN_F32, entry_two=CHIP_BF,
            active=WIDE_BF, slope=WIDE_BF, normed_two=ROW_F32, factor_two=COLUMN_F32,
        ),
        {},
        dict(first=ROW_F32, mixed=HEADS_BF),
        4,
        0,
    ),
    (
        (BACK, IN, OUT),
        dict(
            d_branch=CHIP_BF, d_before=WIDE_BF, d_attn=CHIP_BF, d_inner_out=ROW_F32,
            sums=((8, D), F32), sums_in=((1, FF), F32),
        ),
        dict(d_mixed=((HEAD, LENGTH), BF)),
        dict(d_second=ROW_F32, d_mixed_rows=HEADS_BF, d_mixed_stage=(STAGE, BF)),
        3 + 7,
        1,
    ),
    (
        (QKV,),
        dict(d_qkv=((3, CHIP_ROWS, HALF), BF)),
        {},
        {},
        1,
        0,
    ),
    ((), ATTEND_SAVED, MIXED_T, ATTEND_SCRATCH, 0, 0),
    ((), {}, BACK_OUTPUTS, BACK_SCRATCH, 0, 0),
    ((), WHOLE_GRADIENTS, {}, {}, 0, 0),
)
WEIGHT_SHAPES = (
    dict(w_qkv=((3,) + CUBE + (16, HALF), BF)),
    dict(w_out=((2, 2, 2, 2, 4, 16, HALF), BF)),
    dict(w_in=((4,) + CUBE + (16, HALF), BF)),
    dict(w_back=((2, 2, 2, 2, 4, 64, HALF), BF)),
)


WEIGHT_COPIES = (1, 4, 4, 4)


def weight_gradients(refs, mixed_t, add):
    def store(ref, at, value):
        value = value.reshape(ref[at].shape)
        ref[at] = bfloat(value + widen(ref[at])) if add else bfloat(value)

    turned = refs.entry_two[...].T
    for chunk in range(4):
        value = dot(turned, refs.d_before[:, columns(chunk)])
        store(refs.g_in, CUBE_ALL + (EVERY, columns(chunk)), value)
    refs.keep(refs.g_in)
    for chunk in range(4):
        value = dot(refs.active[:, columns(chunk)].T, refs.d_branch[...])
        store(refs.g_back, (chunk // 2, chunk % 2), value)
    refs.keep(refs.g_back)
    store(refs.g_out, CUBE_ALL, dot(mixed_t.reshape(HALF, CHIP_ROWS), refs.d_attn[...]))
    refs.keep(refs.g_out)


def dense(
    parts, number, gathered, near, loaded, extra, dropped=(), sources={}, scalars={}, added={}
):
    outputs, saved, far, weight_names, sems = {}, dict(extra), {}, [], []
    rounds = 2 * (POST in parts) + (BACK_DENSE in parts) + (BACK_PROJECT in parts)
    sums = ((rounds, ROWS, D), F32)
    scratch = dict(outgoing=sums, incoming=sums, kept=ROW_F32)
    copies = locals_ = 0
    for part in parts:
        its_weights, its_saved, its_outputs, its_scratch, its_copies, its_locals = PARTS[part]
        weight_names += [name for name in its_weights if name not in weight_names]
        outputs.update(its_outputs)
        saved.update(its_saved)
        scratch.update(its_scratch)
        copies += its_copies
        locals_ += its_locals
    for name in dropped:
        scratch[name] = {**saved, **outputs}[name]
        saved.pop(name, None)
        outputs.pop(name, None)
    for name in weight_names:
        scratch.update(WEIGHT_SHAPES[name])
        locals_ += WEIGHT_COPIES[name]
    if ATTEND in parts:
        far.update(chances=CHANCES)
        sems = MAIL_SEMS + [dma(SLOTS + 1)]
    if ATTEND_BACK in parts:
        sems = MAIL_SEMS + MAIL_SEMS + [dma(SLOTS)]

    def body(refs, semaphores):
        here = place()
        wire = Wire(here, *semaphores[:3])
        refs.round = 0
        weights = Weights(refs, wire, weight_names)
        partial = [
            wire.fetch(getattr(refs, key + LATER), getattr(refs, key)) for key in added
        ]
        if BACK_DENSE in parts:
            refs.sums[...] = jnp.zeros((8, D), F32)
            refs.sums_in[...] = jnp.zeros((1, FF), F32)
        if ATTEND_BACK in parts:
            refs.attend_local = semaphores[-1]
            fetch_chances(refs)
        greet([partner(here)] + group(here))
        refs.arrive()
        pending = []
        value = None
        for part in parts:
            if part == PROJECT:
                pending += part_project(refs, wire, weights, value)
            elif part == POST:
                value = part_post(refs, wire, weights)
                refs.result[...] = value.astype(refs.result.dtype)
                refs.keep(refs.result)
            elif part == BACK_DENSE:
                if POST in parts:
                    value = widen(refs.cotangent[...])
                pending += part_back_dense(refs, wire, weights, value)
            elif part == BACK_PROJECT:
                turn_gradients(refs)
                refs.keep(refs.d_qkv)
                add_half(refs, wire, B_QUERY, row_sum(refs.d_qkv[0]))
                add_half(refs, wire, B_VALUE, row_sum(refs.d_qkv[2]))
                value = part_back_project(refs, wire, weights)
            elif part == GRADIENTS:
                for copy in partial:
                    copy.wait()
                weight_gradients(refs, refs.mixed_t_in[...], bool(added))
            else:
                for copy in pending:
                    copy.wait()
                pending = []
                if part == ATTEND:
                    send, recv, refs.attend_local = semaphores[3:]
                    refs.keep(refs.qkv)
                    attend_steps(refs, Mail(here, send, recv), lambda slot: None)
                else:
                    send, recv, send_two, recv_two, _ = semaphores[3:]
                    attend_back_steps(
                        refs, Mail(here, send, recv), Mail(here, send_two, recv_two),
                        lambda slot: None,
                    )
        for copy in pending:
            copy.wait()

    return call(
        body, "dense_%d" % number, number, near,
        dict(loaded, vecs=gathered.vecs, b_in=gathered.b_in),
        dict(
            sources, gqkv=gathered.gqkv, rest_one=gathered.rest_one, rest_two=gathered.rest_two,
            rest_three=gathered.rest_three, yours_two=gathered.yours_two,
            yours_three=gathered.yours_three,
            **{key + LATER: value for key, value in added.items()},
        ),
        outputs, saved, far, scratch, [dma(copies), dma(copies), dma(locals_ + 3)] + sems, scalars,
    )


LATER = "_later"


def opening(lengths, pads, shards, vectors, tokens, number):
    def body(refs, semaphores):
        send, recv, local, mail_send, mail_recv, refs.attend_local = semaphores
        here = place()
        wire = Wire(here, send, recv, local)
        core = wire.core
        greet(neighbours(here, (1, -1, 2)) + group(here))
        refs.arrive()
        tok = lax.axis_index("tok")
        lanes = lax.broadcasted_iota(jnp.int32, (1, 128), 1)
        line = refs.vectors[...]
        rows = []
        for k in range(8):
            turned = pltpu.roll(line, lax.rem(tok * 8 - 8 * k + 128, 128), 1)
            rows.append(jnp.where(lanes // 8 == tok, turned, 0.0))
        turned = pltpu.roll(line, lax.rem(lax.rem(tok, 4) * 32 + 64, 128), 1)
        turned = jnp.where(lanes // 32 == lax.rem(tok, 4), turned, 0.0)
        for k in range(4):
            rows.append(jnp.where(lax.div(tok, 4) == k, turned, jnp.zeros_like(turned)))
        rows.append(jnp.zeros((4, 128), F32))
        refs.small[...] = bfloat(jnp.concatenate(rows, axis=0))
        thin = [widen(ref[...]) for ref in (refs.w_query, refs.w_key, refs.w_value, refs.w_out)]
        wide, back = widen(refs.w_in[...]), refs.w_back[...]
        for half in range(2):
            span = columns(half)
            spread = [wide[:, columns(4 * half + k)] for k in range(4)]
            pieces = [thin[k][:, span] for k in range(3)] + spread[:3]
            refs.pack[half, 0:48, :] = bfloat(jnp.concatenate(pieces, axis=0))
            refs.pack[half, 48:80, :] = back[:, span]
            refs.pack[half, 80:96, :] = bfloat(
                jnp.concatenate([spread[3], thin[3][:, span]], axis=0)
            )
        swaps = [
            wire.swap(refs.pack.at[1 - core], refs.theirs),
            wire.swap(refs.small, refs.small_theirs),
        ]
        entry = refs.entry
        entry[wire.own, :] = refs.tokens[...]
        entry_copy = wire.swap(refs.tokens, entry.at[wire.own])
        for copy in swaps:
            copy.wait()

        def build(low, high):
            low, high = widen(low), widen(high)

            def both(row):
                return bfloat(jnp.concatenate([low[row : row + 8], high[row : row + 8]], axis=0))

            for k in range(3):
                refs.own_qkv[k] = both(8 * k)
                refs.own_one[16 * k : 16 * k + 16, :] = both(24 + 8 * k)
            refs.own_one[48:64, :] = both(80)
            back = bfloat(jnp.concatenate([low[48:80], high[48:80]], axis=0))
            out = both(88)
            for ref, span in ((refs.own_two, slice(0, 256)), (refs.own_three, slice(256, 512))):
                ref[0:64, :] = back[:, span]
                ref[64:80, :] = out[:, span]

        @pl.when(core == 0)
        def _():
            build(refs.pack[0], refs.theirs[...])

        @pl.when(core == 1)
        def _():
            build(refs.theirs[...], refs.pack[1])

        refs.own_small[...] = refs.small[...] + refs.small_theirs[...]

        def nothing(value):
            pass

        parts = [
            (refs.w_qkv, (k,), GATHER_ORDERS[k], refs.own_qkv.at[k], HALF, nothing)
            for k in range(3)
        ]
        parts.append((refs.all_small, (), GATHER_ORDERS[3], refs.own_small, 0, nothing))
        first_stages = ring_gather(wire, parts)
        yours = pl.ds(2 * (1 - core), 2)
        passed = []

        def pass_two(value):
            passed.append(
                wire.swap(
                    refs.rest_two.at[yours, :, :, value], refs.yours_two.at[:, :, :, value]
                )
            )

        def pass_three(value):
            passed.append(
                wire.swap(
                    refs.rest_three.at[yours, value % 2, value // 2],
                    refs.yours_three.at[:, value % 2, value // 2],
                )
            )

        long_stages = ring_gather(
            wire, [(refs.rest_one, (), GATHER_ORDERS[0], refs.own_one, HALF, nothing)]
        )
        stages = ring_gather(
            wire,
            [
                (refs.rest_two, (), GATHER_ORDERS[1], refs.own_two, HALF // 2, pass_two),
                (refs.rest_three, (), GATHER_ORDERS[2], refs.own_three, HALF // 2, pass_three),
            ],
        )
        for ring in (first_stages, long_stages, stages, first_stages, first_stages, long_stages):
            advance(ring)
        advance(stages)
        for _ in first_stages:
            pass
        kept = wire.fetch(refs.w_qkv, refs.gqkv)
        for s in range(8):
            tile = jnp.zeros((16, 128), F32)
            for x_hi in range(2):
                for z in range(4):
                    tile = tile + widen(refs.all_small[s // 2, s % 2, x_hi, z])
            refs.vecs[:, 128 * s : 128 * s + 128] = tile[:8]
            for j in range(4):
                low = HALF * s + 128 * j
                refs.b_in[:, low : low + 128] = tile[8 + j : 9 + j]
        refs.keep(refs.vecs, refs.b_in)
        pending = project_rows(
            refs, wire, lambda k: refs.w_qkv[k].reshape(D, HALF), entry_copy, lambda: advance(long_stages)
        )
        for copy in pending:
            copy.wait()
        refs.keep(refs.qkv)
        advance(stages)

        def between(slot):
            if slot == 2:
                advance(long_stages)
            elif slot == 3:
                advance(stages)

        attend_steps(refs, Mail(here, mail_send, mail_recv), between)
        for _ in long_stages:
            pass
        for _ in stages:
            pass
        for copy in passed:
            copy.wait()
        kept.wait()

    scratch = dict(
        ATTEND_SCRATCH, pack=((2, 96, HALF), BF), small=((16, 128), BF), theirs=((96, HALF), BF),
        small_theirs=((16, 128), BF),
        own_qkv=((3, 16, HALF), BF), own_one=((64, HALF), BF), own_two=((80, HALF // 2), BF), own_three=((80, HALF // 2), BF), own_small=((16, 128), BF),
        w_qkv=((3,) + CUBE + (16, HALF), BF), all_small=(CUBE + (16, 128), BF),
        qkv_rows=((3, CHIP_ROWS, HALF), BF), qkv_stage=((3,) + STAGE, BF),
    )
    narrow = (CUBE + (80, HALF // 2), BF)
    come = ((2, 2, 2, 4, 80, HALF // 2), BF)
    copies = 3 + 7 * GATHER_COPIES + 8 + 21
    return call(
        body, "opening", number, dict(vectors=vectors), dict(shards, tokens=tokens), {}, MIXED_T,
        dict(
            ATTEND_SAVED, entry=CHIP_BF, qkv=((3, HEAD, LENGTH), BF), vecs=((8, D), F32),
            b_in=((1, FF), F32),
        ),
        dict(
            chances=CHANCES, gqkv=((3,) + CUBE + (16, HALF), BF), rest_one=(CUBE + (64, HALF), BF),
            rest_two=narrow, rest_three=narrow, yours_two=come, yours_three=come,
        ),
        scratch, [dma(copies), dma(copies), dma(11)] + MAIL_SEMS + [dma(SLOTS + 1)],
        dict(lengths=lengths, pads=pads),
    )


def closing(near, loaded, sources, number):
    rest_slots = [scatter_slots(order, *REST[k], True) for k, order in enumerate(SCATTER_ORDERS[:3])]

    def body(refs, semaphores):
        send, recv, local, send_q, recv_q, send_kv, recv_kv, refs.attend_local = semaphores
        here = place()
        wire = Wire(here, send, recv, local)
        core = wire.core
        refs.round = 0
        fetch_chances(refs)
        weights = Weights(refs, wire, (QKV,))
        greet(neighbours(here, (1, -1, 2)) + group(here))
        mine = pl.ds(2 * core, 2)
        blocks = (EVERY,) * 3
        halves = [
            (ref, (mine,) + blocks + (rows,), gradient, side)
            for side, ref in enumerate((refs.rest_two, refs.rest_three))
            for rows, gradient in ((pl.ds(0, 64), refs.g_back), (pl.ds(64, 16), refs.g_out))
        ]

        def part_columns(half, side):
            low = pl.multiple_of(half * HALF + side * (HALF // 2), HALF // 2)
            return CUBE_ALL + (EVERY, pl.ds(low, HALF // 2))

        copies = [
            wire.swap(gradient.at[part_columns(1 - core, side)], ref.at[at])
            for ref, at, gradient, side in halves
        ]
        copies += [
            wire.fetch(gradient.at[part_columns(core, side)], ref.at[at])
            for ref, at, gradient, side in halves
        ]
        for k in range(4):
            source = refs.g_in.at[CUBE_ALL + (EVERY, pl.ds(k * HALF, HALF))]
            copies.append(wire.fetch(source, refs.rest_one.at[CUBE_ALL + (pl.ds(16 * k, 16),)]))
        refs.arrive()

        def keep_rest(part):
            def store(value):
                (refs.sums_one, refs.sums_two, refs.sums_six)[part][...] = value

            return store

        rest_arrivals = [
            [getattr(refs, "rest_%d_%d" % (part, k)) for k in range(4)] for part in range(3)
        ]
        rest_stages = ring_scatter(
            wire,
            [
                (ref, (), SCATTER_ORDERS[part], REST[part][1], rest_arrivals[part], keep_rest(part))
                for part, ref in enumerate((refs.rest_one, refs.rest_two, refs.rest_three))
            ],
            (0, 1, 2),
        )

        def between(slot):
            if slot == -1:
                for copy in copies:
                    copy.wait()
                advance(rest_stages)
                turned = refs.entry_later[...].T
                for k in range(3):
                    total = dot(turned, refs.d_qkv_later[k])
                    refs.gradients[k] = bfloat(total).reshape(CUBE + (16, HALF))
            elif slot == 0:
                advance(rest_stages)

        attend_back_steps(
            refs, Mail(here, send_q, recv_q), Mail(here, send_kv, recv_kv), between
        )
        advance(rest_stages)
        turn_gradients(refs)
        refs.sums[...] = refs.sums_three[...] + refs.sums_four[...]
        refs.sums_in[...] = refs.in_three[...] + refs.in_four[...]
        add_half(refs, wire, B_QUERY, row_sum(refs.d_qkv[0]))
        add_half(refs, wire, B_VALUE, row_sum(refs.d_qkv[2]))
        swaps = [wire.swap(refs.sums, refs.sums_come), wire.swap(refs.sums_in, refs.in_come)]
        turned = refs.entry[...].T
        for k in range(3):
            total = dot(turned, refs.d_qkv[k]).reshape(CUBE + (16, HALF))
            refs.gradients[k] = bfloat(widen(refs.gradients[k]) + total)
            if k == 1:
                advance(rest_stages)
        for copy in swaps:
            copy.wait()
        both = refs.sums[...] + refs.sums_come[...]
        both_in = refs.sums_in[...] + refs.in_come[...]
        for s in range(8):
            pieces = [both[:, 128 * s : 128 * s + 128]]
            for j in range(4):
                low = HALF * s + 128 * j
                pieces.append(both_in[:, low : low + 128])
            pieces.append(jnp.zeros((4, 128), F32))
            tile = bfloat(jnp.concatenate(pieces, axis=0))
            for x_hi in range(2):
                for z in range(4):
                    refs.small_sums[s // 2, s % 2, x_hi, z] = tile

        def keep(part):
            def store(value):
                if part == 3:
                    refs.tiny[...] = value
                else:
                    refs.final[part] = value

            return store

        arrivals = [
            [getattr(refs, "slot_%d_%d" % (part, k)) for k in range(4)] for part in range(4)
        ]
        parts = [
            (refs.gradients, (part,), SCATTER_ORDERS[part], HALF, arrivals[part], keep(part))
            for part in range(3)
        ]
        parts.append((refs.small_sums, (), SCATTER_ORDERS[3], 0, arrivals[3], keep(3)))
        stages = ring_scatter(wire, parts, (0, 1, 2))
        advance(stages)
        for _ in rest_stages:
            pass
        advance(stages)
        refs.d_tokens[...] = bfloat(part_back_project(refs, wire, weights))
        for _ in stages:
            pass

        def finish(own):
            def both(low, count):
                span = slice(low, low + count)
                return jnp.concatenate([refs.sums_two[span, :], refs.sums_six[span, :]], axis=1)

            rows = [refs.final[k, 8 * own : 8 * own + 8, :] for k in range(3)]
            rows.append(both(64 + 8 * own, 8))
            for k in range(4):
                rows.append(refs.sums_one[16 * k + 8 * own : 16 * k + 8 * own + 8, :])
            rows.append(both(32 * own, 32))
            return jnp.concatenate(rows, axis=0)

        @pl.when(core == 0)
        def _():
            refs.leaving[...] = finish(1)
            refs.landed[0] = finish(0)

        @pl.when(core == 1)
        def _():
            refs.leaving[...] = finish(0)
            refs.landed[1] = finish(1)

        wire.swap(refs.leaving, refs.landed.at[core]).wait()
    few = ((8, D), F32)
    scratch = dict(
        BACK_SCRATCH, **BACK_OUTPUTS, outgoing=((1, ROWS, D), F32), incoming=((1, ROWS, D), F32),
        kept=ROW_F32, d_qkv=((3, CHIP_ROWS, HALF), BF), sums=few, sums_in=((1, FF), F32), sums_come=few,
        in_come=((1, FF), F32), gradients=((3,) + CUBE + (16, HALF), BF),
        small_sums=(CUBE + (16, 128), BF), final=((3, 16, HALF), F32),
        leaving=((96, HALF), F32), sums_one=(REST[0], F32), sums_two=(REST[1], F32),
        sums_six=(REST[2], F32), rest_one=(CUBE + REST[0], BF), rest_two=(CUBE + REST[1], BF),
        rest_three=(CUBE + REST[2], BF),
    )
    scratch.update(WEIGHT_SHAPES[QKV])
    for part in range(4):
        slots = scatter_slots(SCATTER_ORDERS[part], 16, HALF if part < 3 else 128, part < 3)
        for k in range(4):
            scratch["slot_%d_%d" % (part, k)] = slots[k]
    for part in range(3):
        for k in range(4):
            scratch["rest_%d_%d" % (part, k)] = rest_slots[part][k]
    copies = 7 * sum(SCATTER_COPIES) + 8
    return call(
        body, "closing", number, near, loaded, sources,
        dict(
            d_tokens=((ROWS, D), BF), landed=((2, 96, HALF), F32), tiny=((16, 128), F32),
        ),
        {}, {}, scratch,
        [dma(copies), dma(copies), dma(9)] + MAIL_SEMS + MAIL_SEMS + [dma(SLOTS)],
    )


def unpack_kernel(
    result, d_tokens, landed, tiny, o_result, o_tokens, o_query, o_key, o_value, o_out, o_in, o_back,
    o_vectors,
):
    o_result[...] = result[...]
    o_tokens[...] = d_tokens[...]
    for column in (0, 1):
        span = columns(column)
        for piece, ref in enumerate((o_query, o_key, o_value, o_out)):
            ref[:, span] = landed[column, 8 * piece : 8 * piece + 8, :]
        for chunk in range(4):
            o_in[:, columns(4 * column + chunk)] = landed[
                column, 32 + 8 * chunk : 40 + 8 * chunk, :
            ]
        o_back[:, span] = landed[column, 64:96, :]
    tok = lax.axis_index("tok")
    o_vectors[0:8, :] = pltpu.roll(tiny[0:8, :], lax.rem(128 - tok * 8, 128), 1)
    wide = tiny[8:9, :]
    for k in range(1, 4):
        wide = jnp.where(lax.div(tok, 4) == k, tiny[8 + k : 9 + k, :], wide)
    wide = pltpu.roll(wide, lax.rem(128 - lax.rem(tok, 4) * 32, 128), 1)
    o_vectors[8:16, :] = jnp.broadcast_to(wide, (8, 128))


def unpack(result, d_tokens, landed, tiny):
    vmem = pl.BlockSpec(memory_space=pltpu.VMEM)
    few = ((8, D), F32)
    specs = (
        ((ROWS, D), BF), ((ROWS, D), BF), few, few, few, few, ((8, FF), F32), ((32, D), F32),
        ((16, 128), F32),
    )
    return pl.pallas_call(
        unpack_kernel,
        out_shape=tuple(jax.ShapeDtypeStruct(*spec) for spec in specs),
        in_specs=[vmem] * 4,
        out_specs=(vmem,) * len(specs),
        name="unpack",
        compiler_params=pltpu.CompilerParams(vmem_limit_bytes=16 * 2**20),
    )(result, d_tokens, landed, tiny)


def on_device(
    tokens, cotangent, doc_lengths, pad_counts, w_query, b_query, w_key, w_value, b_value, w_out,
    b_out, gain_attn, shift_attn, w_in, b_in, w_back, b_back, gain_ffn, shift_ffn,
):
    vectors = jnp.concatenate(
        [
            b_query, b_value, b_out, gain_attn, shift_attn, b_back, gain_ffn, shift_ffn, b_in,
            jnp.zeros((32,), BF),
        ]
    )
    one = opening(
        doc_lengths, pad_counts,
        dict(
            w_query=w_query, w_key=w_key, w_value=w_value, w_out=w_out, w_in=w_in, w_back=w_back
        ),
        widen(vectors)[None], tokens, 0,
    )
    two = dense(
        (POST, PROJECT, ATTEND), 2, one, dict(mixed_t_in=one.mixed_t), dict(hidden=tokens),
        dict(result=ROW_F32), scalars=dict(lengths=doc_lengths, pads=pad_counts),
    )
    three = dense(
        (POST, BACK_DENSE, GRADIENTS, ATTEND_BACK), 4, one, dict(mixed_t_in=two.mixed_t),
        dict(
            hidden=two.result, cotangent=cotangent, qkv=two.qkv, mixed_head=two.mixed_head,
            inverse=two.inverse,
        ),
        dict(result=((ROWS, D), BF)),
        (
            "normed_one", "factor_one", "entry_two", "active", "slope", "normed_two",
            "factor_two", "d_branch", "d_before", "d_attn", "d_mixed",
        ),
        dict(chances=two.chances),
    )
    four = dense(
        (BACK_PROJECT, BACK_DENSE, GRADIENTS), 6, one, dict(d_q_t=three.d_q_t, d_kv_t=three.d_kv_t),
        dict(
            d_inner=three.d_inner_out, normed_one=two.normed_one, factor_one=two.factor_one,
            normed_two=two.normed_two, factor_two=two.factor_two, slope=two.slope,
            entry_two=two.entry_two, active=two.active, mixed_t_in=one.mixed_t,
        ),
        {}, ("d_branch", "d_before", "d_attn"),
        added=dict(g_in=three.g_in, g_back=three.g_back, g_out=three.g_out),
    )
    last = closing(
        dict(d_mixed=four.d_mixed),
        dict(
            qkv=one.qkv, mixed_head=one.mixed_head, inverse=one.inverse, d_inner=four.d_inner_out,
            entry=one.entry, entry_later=two.entry, d_qkv_later=four.d_qkv, sums_three=three.sums,
            sums_four=four.sums, in_three=three.sums_in, in_four=four.sums_in,
        ),
        dict(
            chances=one.chances, gqkv=one.gqkv, g_in=four.g_in, g_back=four.g_back, g_out=four.g_out
        ),
        8,
    )
    result, d_tokens, g_query, g_key, g_value, g_out, g_in, g_back, lines = unpack(
        three.result, last.d_tokens, last.landed, last.tiny
    )
    (
        g_b_query, g_b_value, g_b_out, g_gain_attn, g_shift_attn, g_b_back, g_gain_ffn, g_shift_ffn,
    ) = [lines[k, :8] for k in range(8)]
    return (
        result, d_tokens, g_query, g_b_query, g_key, g_value, g_b_value, g_out, g_b_out, g_gain_attn,
        g_shift_attn, g_in, lines[8, :32], g_back, g_b_back, g_gain_ffn, g_shift_ffn,
    )


def solution(mesh):
    both = ("seq", "tok")
    rows, vector = P(both, None), P(both)
    ins = (
        rows, rows, P("seq", None), P("seq"), rows, vector, rows, rows, vector, rows, vector, vector,
        vector, rows, vector, rows, vector, vector, vector,
    )
    outs = (
        rows, rows, rows, vector, rows, rows, vector, rows, vector, vector, vector, rows, vector,
        rows, vector, vector, vector,
    )
    return jax.shard_map(on_device, mesh=mesh, in_specs=ins, out_specs=outs, check_vma=False)
```

```python
import math
import types

import jax
import jax.numpy as jnp
from jax import lax
from jax.experimental import pallas as pl
from jax.experimental.pallas import tpu as pltpu
from jax.sharding import PartitionSpec as P

HEADS = 16
WINDOW = 1024
D = 1024
FF = 4096
HEAD = 64
CHIPS = 8
ROWS = 192
CHIP_ROWS = 2 * ROWS
LENGTH = CHIP_ROWS * CHIPS
HALF = 512
EPSILON = 1e-05
MASKED = -1e30
SCALE = 1.0 / math.sqrt(HEAD)
LOG2E = 1.4426950408889634
MESH = pl.DeviceIdType.MESH
BF = jnp.bfloat16
F32 = jnp.float32
CUBE = (4, 2, 2, 4)
X, Y, Z, CORE = range(4)


def bfloat(tensor):
    return tensor.astype(BF)


def widen(tensor):
    return tensor.astype(F32)


def place():
    seq, tok = lax.axis_index("seq"), lax.axis_index("tok")
    x = (tok // 8) * 2 + seq % 2
    return {X: x, Y: seq // 2, Z: (tok // 2) % 4, CORE: tok % 2}


def device(x, y, z, core):
    return (y * 2 + x % 2, (x // 2) * 8 + z * 2 + core)


def moved(here, axis, steps):
    there = dict(here)
    there[axis] = lax.rem(here[axis] + steps + 4, 4)
    return device(there[X], there[Y], there[Z], there[CORE])


def partner(here):
    return device(here[X], here[Y], here[Z], 1 - here[CORE])


def cube_index(here, whole, axis, value):
    index = []
    for name in (Y, X, Z):
        if name in whole:
            index += [slice(None)] * (2 if name == X else 1)
        else:
            at = value if name == axis else here[name]
            index += [at % 2, at // 2] if name == X else [at]
    return tuple(index)


def greet(targets):
    barrier = pltpu.get_barrier_semaphore()
    for target in targets:
        pl.semaphore_signal(barrier, inc=1, device_id=target, device_id_type=MESH)
    pl.semaphore_wait(barrier, len(targets))


def neighbours(here, steps):
    return [moved(here, axis, step) for axis in (X, Y, Z) for step in steps] + [partner(here)]


def group_device(here, number):
    seq = lax.axis_index("seq")
    return (seq, (number // 4) * 8 + (number % 4) * 2 + here[CORE])


def group_number(here):
    return (here[X] // 2) * 4 + here[Z]


def group(here):
    me = group_number(here)
    return [group_device(here, lax.rem(me + k, CHIPS)) for k in range(1, CHIPS)]


class Wire:
    def __init__(self, here, send, recv, local):
        self.send, self.recv, self.local = send, recv, local
        self.here, self.number, self.locals = here, 0, 0
        self.core, self.me = here[CORE], group_number(here)
        self.own = pl.ds(pl.multiple_of(self.core * ROWS, ROWS), ROWS)
        self.other = pl.ds(pl.multiple_of((1 - self.core) * ROWS, ROWS), ROWS)

    def to(self, source, target, device_id):
        copy = pltpu.make_async_remote_copy(
            src_ref=source,
            dst_ref=target,
            send_sem=self.send.at[self.number],
            recv_sem=self.recv.at[self.number],
            device_id=device_id,
            device_id_type=MESH,
        )
        self.number += 1
        copy.start()
        return copy

    def swap(self, source, target):
        return self.to(source, target, partner(self.here))

    def fetch(self, source, target):
        copy = pltpu.make_async_copy(source, target, self.local.at[self.locals])
        self.locals += 1
        copy.start()
        return copy

    def spread(self, stage, target):
        span = chunk_span(self.me)
        copies = []
        for k in range(1, CHIPS):
            to = lax.rem(self.me + k, CHIPS)
            copies.append(self.to(stage.at[to], target.at[:, span], group_device(self.here, to)))
        copies.append(self.fetch(stage.at[self.me], target.at[:, span]))
        return copies


def chunk_span(number):
    return pl.ds(pl.multiple_of(number * CHIP_ROWS, CHIP_ROWS), CHIP_ROWS)


EVERY = slice(None)
CUBE_ALL = (EVERY,) * 4


def side_columns(width, side):
    return pl.ds(side * (width // 2), width // 2)


SIZES = {Y: (4,), X: (2, 2), Z: (4,)}
GATHER_ORDERS = ((X, Z, Y), (Y, X, Z), (Z, Y, X), (X, Z, Y))
SCATTER_ORDERS = ((Y, Z, X), (Z, X, Y), (X, Y, Z), (Y, Z, X))


def ring_gather(wire, parts):
    here = wire.here
    sent, kept = [], []
    for buffer, prefix, order, own, _, _ in parts:
        kept.append(wire.fetch(own, buffer.at[prefix + cube_index(here, (), None, None)]))
    for phase in range(2):
        copies = []
        for step in (1, -1, 2):
            for buffer, prefix, order, own, _, _ in parts:
                axis = order[phase]
                block = buffer.at[prefix + cube_index(here, order[:phase], axis, here[axis])]
                source = own if phase == 0 else block
                copies.append(wire.to(source, block, moved(here, axis, step)))
        yield
        for copy in copies:
            copy.wait_recv()
        sent += copies
        if phase == 0:
            for copy in kept:
                copy.wait()
    first, second, onward = [], [], []

    def block_at(part, value, side):
        buffer, prefix, order, _, cut, _ = part
        index = prefix + cube_index(here, order[:2], order[2], value)
        return buffer.at[index + ((EVERY, side_columns(cut, side)) if cut else ())]

    for turn, copies in enumerate((first, second)):
        for part in parts:
            axis, cut = part[2][2], part[4]
            if cut or turn == 0:
                for side, step in enumerate((1, -1)):
                    block = block_at(part, here[axis], (side + turn) % 2)
                    copies.append(wire.to(block, block, moved(here, axis, step)))
    for _, _, order, _, _, complete in parts:
        complete(here[order[2]])
    yield
    pending = list(first)
    for part in parts:
        axis, cut = part[2][2], part[4]
        for side, step in enumerate((1, -1)):
            pending.pop(0).wait_recv()
            if cut or side == 0:
                block = block_at(part, lax.rem(here[axis] - step + 4, 4), side)
                onward.append(wire.to(block, block, moved(here, axis, step)))
    yield
    for copy in second:
        copy.wait_recv()
    for _, _, order, _, _, complete in parts:
        for step in (1, 3):
            complete(lax.rem(here[order[2]] + step, 4))
    yield
    for copy in onward:
        copy.wait_recv()
    for _, _, order, _, _, complete in parts:
        complete(lax.rem(here[order[2]] + 2, 4))
    for copy in sent + first + second + onward:
        copy.wait_send()


GATHER_COPIES = 3 + 3 + 6


def lengths_of(full):
    return tuple(n for name in (Y, X, Z) if name in full for n in SIZES[name])


def digits_of(i, lengths):
    digits = []
    for length in reversed(lengths):
        digits.append(lax.rem(i, length))
        i = lax.div(i, length)
    return tuple(digits[::-1])


def one_chip(here, full, axis, value, digits):
    digits, index = list(digits), []
    for name in (Y, X, Z):
        if name in full:
            index += [digits.pop(0) for _ in SIZES[name]]
        else:
            at = value if name == axis else here[name]
            index += [at % 2, at // 2] if name == X else [at]
    return tuple(index)


SCATTER_COPIES = (6, 3, 3)


def scatter_slots(order, rows, wide, cut):
    dims = lengths_of(order[1:])
    slots = [
        pltpu.VMEM((2,) + dims + (rows, wide // 2 if cut else wide), BF),
        pltpu.VMEM((2,) + dims + (rows, wide), BF),
    ]
    return slots + [
        pltpu.VMEM((3,) + lengths_of(order[phase + 1 :]) + (rows, wide), BF) for phase in (1, 2)
    ]


def ring_scatter(wire, parts, phases):
    here = wire.here
    sent = []
    for phase in phases:
        ahead, arriving, early = [], [], []
        for buffer, prefix, order, cut, slots, _ in parts:
            axis, full = order[phase], order[phase + 1 :]
            row = []
            if phase == 0:
                far = prefix + cube_index(here, full, axis, lax.rem(here[axis] + 2, 4))
                for side, step in enumerate((1, -1)):
                    if cut or side == 0:
                        block = buffer.at[far + ((EVERY, side_columns(cut, side)) if cut else ())]
                        row.append(wire.to(block, slots[0].at[side], moved(here, axis, step)))
                ahead.append(row)
                if cut:
                    for side, step in enumerate((1, -1)):
                        near = cube_index(here, full, axis, lax.rem(here[axis] + step + 4, 4))
                        ready = (EVERY, side_columns(cut, 1 - side))
                        early.append(
                            wire.to(
                                buffer.at[prefix + near + ready],
                                slots[1].at[(side,) + (EVERY,) * len(lengths_of(full)) + ready],
                                moved(here, axis, step),
                            )
                        )
            else:
                for k, step in enumerate((1, -1, 2)):
                    value = lax.rem(here[axis] + step + 4, 4)
                    block = buffer.at[prefix + cube_index(here, full, axis, value)]
                    row.append(
                        wire.to(block, slots[1 + phase].at[k], moved(here, axis, step))
                    )
                arriving.append(row)
            sent += row
        yield
        if phase == 0:
            for (buffer, prefix, order, cut, slots, _), row in zip(parts, ahead):
                axis, full = order[phase], order[phase + 1 :]
                pair = []
                for side, step in enumerate((1, -1)):
                    value = lax.rem(here[axis] + step + 4, 4)
                    if side < len(row):
                        row[side].wait_recv()
                        half = slots[0]
                        columns_ = side_columns(cut, side) if cut else EVERY

                        def add(
                            i, _, buffer=buffer, prefix=prefix, axis=axis, full=full, value=value,
                            half=half, side=side, columns_=columns_,
                        ):
                            digits = digits_of(i, lengths_of(full))
                            at = prefix + one_chip(here, full, axis, value, digits)
                            at += (EVERY, columns_)
                            buffer[at] = bfloat(widen(buffer[at]) + widen(half[(side,) + digits]))
                            return 0

                        lax.fori_loop(0, math.prod(lengths_of(full)), add, 0)
                    summed = (EVERY, columns_) if cut else ()
                    block = buffer.at[prefix + cube_index(here, full, axis, value) + summed]
                    target = slots[1].at[(side,) + (EVERY,) * len(lengths_of(full)) + summed]
                    pair.append(wire.to(block, target, moved(here, axis, step)))
                arriving.append(pair)
                sent += pair
            yield
        for copy in early:
            copy.wait_recv()
        sent += early
        for (buffer, prefix, order, _, slots, final), row in zip(parts, arriving):
            axis, full = order[phase], order[phase + 1 :]
            come = slots[1 + phase]
            for copy in row:
                copy.wait_recv()

            def total(
                i, _, buffer=buffer, prefix=prefix, axis=axis, full=full, come=come, final=final,
                count=len(row),
            ):
                digits = digits_of(i, lengths_of(full))
                at = prefix + one_chip(here, full, axis, here[axis], digits)
                value = widen(buffer[at])
                for k in range(count):
                    value = value + widen(come[(k,) + digits])
                if phase < 2:
                    buffer[at] = bfloat(value)
                else:
                    final(value)
                return 0

            lax.fori_loop(0, math.prod(lengths_of(full)), total, 0)
    for copy in sent:
        copy.wait_send()


def advance(stages, count=1):
    for _ in range(count):
        next(stages, None)


class Mail:
    def __init__(self, here, send, recv):
        self.here, self.me, self.send, self.recv = here, group_number(here), send, recv
        self.count = 0
        self.sent = []

    def to(self, number, source, target):
        copy = pltpu.make_async_remote_copy(
            src_ref=source,
            dst_ref=target,
            send_sem=self.send.at[self.count],
            recv_sem=self.recv.at[self.me],
            device_id=group_device(self.here, number),
            device_id_type=MESH,
        )
        self.count += 1
        copy.start()
        self.sent.append(copy)

    def finish(self, source, target):
        for k in range(1, CHIPS):
            sender = lax.rem(self.me + k, CHIPS)
            pltpu.make_async_remote_copy(
                src_ref=source,
                dst_ref=target,
                send_sem=self.send.at[0],
                recv_sem=self.recv.at[sender],
                device_id=group_device(self.here, sender),
                device_id_type=MESH,
            ).wait_recv()
        for copy in self.sent:
            copy.wait_send()


BLOCK = 256
SPAN = 1280
STEPS = LENGTH // BLOCK
SLOTS = 4
LAST_START = LENGTH - SPAN


def limits(bounds, first, count):
    places = first + lax.broadcasted_iota(jnp.int32, (1, count), 1)
    low = jnp.maximum(places - (WINDOW // 2 - 1), 0)
    high = jnp.minimum(places + WINDOW // 2, LENGTH)
    for bound in bounds:
        low = jnp.maximum(low, jnp.where(bound <= places, bound, 0))
        high = jnp.minimum(high, jnp.where(bound > places, bound, LENGTH))
    return low, high


def dot(former, latter):
    return jnp.dot(former, latter, preferred_element_type=F32)


def attend_steps(refs, mail, values_ready, between):
    qkv, mixed_t, mixed, inverse = refs.qkv, refs.mixed_t, refs.mixed_head, refs.inverse
    live, end, bounds = LENGTH - refs.pads[0], 0, []
    for k in range(4):
        end = end + refs.lengths[0, k]
        bounds.append(jnp.minimum(end, live))
    keys_rows, ones_v, chances, stage = refs.keys_rows, refs.ones_v, refs.held, refs.mixed_stage
    local = refs.attend_local
    me = mail.me
    keys_rows[...] = qkv[1].T
    ones_v[0:HEAD, :] = jnp.ones((HEAD, LENGTH), BF)
    kept = []

    def weigh(i):
        first = pl.multiple_of(i * BLOCK, BLOCK)
        start = pl.multiple_of(jnp.clip(first - 512, 0, LAST_START), BLOCK)
        scores = dot(keys_rows[pl.ds(start, SPAN), :], qkv[0, :, pl.ds(first, BLOCK)])
        low, high = limits(bounds, first, BLOCK)
        base = lax.broadcasted_iota(jnp.int32, (8, BLOCK), 0) + (start - low)
        steps = 8 * lax.broadcasted_iota(jnp.int32, (SPAN // 8, 8, BLOCK), 0)
        inside = (base[None] + steps).astype(jnp.uint32) < (high - low).astype(jnp.uint32)[None]
        scores = jnp.where(inside, scores.reshape(SPAN // 8, 8, BLOCK), MASKED)
        scores = scores.reshape(SPAN, BLOCK)
        highest = jnp.max(scores, axis=0, keepdims=True)
        chances[i] = bfloat(jnp.exp2((scores - highest) * (SCALE * LOG2E)))

    def mix(i):
        first = pl.multiple_of(i * BLOCK, BLOCK)
        start = pl.multiple_of(jnp.clip(first - 512, 0, LAST_START), BLOCK)
        out = dot(ones_v[:, pl.ds(start, SPAN)], chances[i])
        back = 1.0 / out[0:1]
        result = out[HEAD:] * back
        mixed[:, pl.ds(first, BLOCK)] = result
        stage[:, pl.ds(first, BLOCK)] = bfloat(result)
        inverse[:, pl.ds(first, BLOCK)] = back

    def each(action, slot):
        pair = lax.rem(me // 2 + 1 + slot, SLOTS)

        for t in range(3):
            action(pair * 3 + t)
        return pair

    for slot in range(SLOTS):
        if slot == 0:
            each(weigh, 0)
            each(weigh, 1)
            values_ready()
            ones_v[HEAD:, :] = qkv[2]
        elif slot < SLOTS - 1:
            each(weigh, slot + 1)
        pair = each(mix, slot)
        blocks = pl.ds(pair * 3, 3)
        copy = pltpu.make_async_copy(chances.at[blocks], refs.chances.at[blocks], local.at[slot])
        copy.start()
        kept.append(copy)
        if slot < SLOTS - 1:
            for number in (2 * pair, 2 * pair + 1):
                mail.to(number, stage.at[:, chunk_span(number)], mixed_t.at[me])
        else:
            number = me + 1 - 2 * (me % 2)
            mail.to(number, stage.at[:, chunk_span(number)], mixed_t.at[me])
            copy = pltpu.make_async_copy(
                stage.at[:, chunk_span(me)], mixed_t.at[me], local.at[SLOTS]
            )
            copy.start()
            kept.append(copy)
        between(slot)
    refs.keep(mixed, inverse)
    for copy in kept:
        copy.wait()
    mail.finish(stage.at[:, chunk_span(me)], mixed_t.at[me])


MIXED_T = dict(mixed_t=((CHIPS, HEAD, CHIP_ROWS), BF))
ATTEND_SAVED = dict(mixed_head=((HEAD, LENGTH), F32), inverse=((1, LENGTH), F32))
CHANCES = ((STEPS, SPAN, BLOCK), BF)
ATTEND_SCRATCH = dict(
    keys_rows=((LENGTH, HEAD), BF), ones_v=((2 * HEAD, LENGTH), BF), held=CHANCES,
    mixed_stage=((HEAD, LENGTH), BF),
)
MAIL_SEMS = [pltpu.SemaphoreType.DMA((CHIPS - 1,)), pltpu.SemaphoreType.DMA((CHIPS,))]


def call(
    body, name, number, near, loaded, sources, outputs, saved, far, scratch, semaphores, scalars={}
):
    vmem, hbm = pl.BlockSpec(memory_space=pltpu.VMEM), pl.BlockSpec(memory_space=pltpu.HBM)
    smem = pl.BlockSpec(memory_space=pltpu.SMEM)
    scratch = dict(scratch)
    for key, value in loaded.items():
        scratch[key] = (value.shape, value.dtype)
    scratch.update(saved)
    specs = [*outputs.values(), *saved.values(), *far.values()]

    def size(shape, dtype):
        rows, lanes = (1,) * (2 - len(shape[-2:])) + tuple(shape[-2:])
        rows, lanes = -(-rows // 8) * 8, -(-lanes // 128) * 128
        return math.prod(shape[:-2]) * rows * lanes * jnp.dtype(dtype).itemsize

    held = [(value.shape, value.dtype) for value in near.values()] + list(outputs.values())
    held += [s if isinstance(s, tuple) else (s.shape, s.dtype) for s in scratch.values()]
    limit = sum(size(*spec) for spec in held) + 10 * 2**20

    def kernel(*values):
        values = list(values)

        def take(names):
            return {key: values.pop(0) for key in names}

        refs = types.SimpleNamespace(**take(scalars), **take(near))
        heres = take(loaded)
        for key, ref in take(sources).items():
            setattr(refs, key, ref)
        for key, ref in take(outputs).items():
            setattr(refs, key, ref)
        outs = take(saved)
        for names in (far, scratch):
            for key, ref in take(names).items():
                setattr(refs, key, ref)
        copies = values.pop(0)
        pending = [
            pltpu.make_async_copy(ref, getattr(refs, key), copies.at[k])
            for k, (key, ref) in enumerate(heres.items())
        ]
        for copy in pending:
            copy.start()
        kept = []

        def arrive():
            for copy in pending:
                copy.wait()

        def keep(*arrays):
            for k, (key, out) in enumerate(outs.items()):
                if any(getattr(refs, key) is array for array in arrays):
                    copy = pltpu.make_async_copy(
                        getattr(refs, key), out, copies.at[len(heres) + k]
                    )
                    copy.start()
                    kept.append(copy)

        refs.arrive, refs.keep = arrive, keep
        body(refs, values)
        for copy in kept:
            copy.wait()

    results = pl.pallas_call(
        kernel,
        out_shape=tuple(jax.ShapeDtypeStruct(*spec) for spec in specs),
        in_specs=[smem] * len(scalars)
        + [vmem] * len(near)
        + [hbm] * (len(loaded) + len(sources)),
        out_specs=(vmem,) * len(outputs) + (hbm,) * (len(saved) + len(far)),
        scratch_shapes=[
            pltpu.VMEM(*spec) if isinstance(spec, tuple) else spec for spec in scratch.values()
        ]
        + [dma(max(1, len(loaded) + len(saved)))]
        + list(semaphores),
        name=name,
        compiler_params=pltpu.CompilerParams(
            collective_id=number, has_side_effects=True, vmem_limit_bytes=max(limit, 58 * 2**20)
        ),
    )(*scalars.values(), *near.values(), *loaded.values(), *sources.values())
    return types.SimpleNamespace(**dict(zip([*outputs, *saved, *far], results)))


def dma(count):
    return pltpu.SemaphoreType.DMA((count,))


PAD = 2 * BLOCK
PADDED = LENGTH + 2 * PAD


def fetch_chances(refs):
    copies = []
    for slot in range(SLOTS):
        blocks = pl.ds(slot * 3, 3)
        copy = pltpu.make_async_copy(
            refs.chances.at[blocks], refs.held.at[blocks], refs.attend_local.at[slot]
        )
        copy.start()
        copies.append(copy)
    refs.early = copies


def attend_back_steps(refs, mail_q, mail_kv, between):
    qkv, mixed, inverse, d_mixed = refs.qkv, refs.mixed_head, refs.inverse, refs.d_mixed
    d_q_t, d_kv_t, chances, kv = refs.d_q_t, refs.d_kv_t, refs.held, refs.kv
    rows_q, rows_d, turned_d, shift = refs.rows_q, refs.rows_d, refs.turned_d, refs.shift
    total_q, stage_q, stage_kv = refs.total_q, refs.stage_q, refs.stage_kv
    me = mail_q.me
    kv[...] = jnp.concatenate([qkv[1], qkv[2]], axis=0).T
    scaled = bfloat(widen(d_mixed[...]) * inverse[...])
    inner = jnp.sum(widen(scaled) * mixed[...], axis=0, keepdims=True)
    for edge in (0, PAD + LENGTH):
        shift[:, edge : edge + PAD] = jnp.zeros((1, PAD), F32)
        turned_d[:, edge : edge + PAD] = jnp.zeros((2 * HEAD, PAD), BF)
        rows_q[edge : edge + PAD, :] = jnp.zeros((PAD, 2 * HEAD), BF)
        rows_d[edge : edge + PAD, :] = jnp.zeros((PAD, 2 * HEAD), BF)
    middle = slice(PAD, PAD + LENGTH)
    shift[:, middle] = inner
    turned_d[0:HEAD, middle] = jnp.zeros((HEAD, LENGTH), BF)
    turned_d[HEAD:, middle] = scaled
    both = jnp.concatenate([qkv[0], scaled], axis=0).T
    left = lax.broadcasted_iota(jnp.int32, both.shape, 1) < HEAD
    rows_q[middle, :] = jnp.where(left, both, jnp.zeros_like(both))
    rows_d[middle, :] = jnp.where(left, jnp.zeros_like(both), both)
    total_q[...] = jnp.zeros_like(total_q)
    for copy in refs.early:
        copy.wait()
    between(-1)

    def step(i):
        first = pl.multiple_of(i * BLOCK, BLOCK)
        keys = pl.ds(first, BLOCK)
        span = pl.ds(first, SPAN)
        tiles = []
        for t in range(5):
            block = jnp.clip(i - 2 + t, 0, STEPS - 1)
            start = jnp.clip(block * BLOCK - 512, 0, LAST_START)
            offset = pl.multiple_of(jnp.clip(first - start, 0, SPAN - BLOCK), BLOCK)
            tiles.append(chances[block, pl.ds(offset, BLOCK), :])
        weights = jnp.concatenate(tiles, axis=1)
        grad_weights = dot(kv[keys, :], turned_d[:, span])
        grad_scores = bfloat(widen(weights) * (grad_weights - shift[:, span]))
        total = dot(weights, rows_d[span, :]) + dot(grad_scores, rows_q[span, :])
        total_q[:, span] += dot(qkv[1, :, keys], grad_scores)
        turned = total.T
        stage_kv[0:HEAD, keys] = bfloat(turned[:HEAD] * SCALE)
        stage_kv[HEAD:, keys] = bfloat(turned[HEAD:])

    def send_queries(number):
        span = pl.ds(pl.multiple_of(number * CHIP_ROWS + PAD, 128), CHIP_ROWS)
        stage_q[number] = bfloat(total_q[:, span] * SCALE)
        mail_q.to(number, stage_q.at[number], d_q_t.at[me])

    near = me + 1 - 2 * (me % 2)
    for slot in range(SLOTS):
        pair = lax.rem(me // 2 + 1 + slot, SLOTS)

        for t in range(3):
            step(pair * 3 + t)
        if slot < SLOTS - 1:
            for number in (2 * pair, 2 * pair + 1):
                mail_kv.to(number, stage_kv.at[:, chunk_span(number)], d_kv_t.at[me])
        else:
            mail_kv.to(near, stage_kv.at[:, chunk_span(near)], d_kv_t.at[me])
        if slot == 2:
            complete = lax.rem(me // 2 + 2, SLOTS)
            send_queries(2 * complete)
            send_queries(2 * complete + 1)
        between(slot)
    for rest in (1, 3):
        pair = lax.rem(me // 2 + rest, SLOTS)
        send_queries(2 * pair)
        send_queries(2 * pair + 1)
    send_queries(near)
    between(SLOTS)
    span = pl.ds(pl.multiple_of(me * CHIP_ROWS + PAD, 128), CHIP_ROWS)
    d_q_t[me] = bfloat(total_q[:, span] * SCALE)
    d_kv_t[me] = stage_kv[:, chunk_span(me)]
    mail_kv.finish(stage_kv.at[:, chunk_span(me)], d_kv_t.at[me])
    between(SLOTS + 1)
    mail_q.finish(stage_q.at[me], d_q_t.at[me])


BACK_SCRATCH = dict(
    held=CHANCES, kv=((LENGTH, 2 * HEAD), BF), rows_q=((PADDED, 2 * HEAD), BF),
    rows_d=((PADDED, 2 * HEAD), BF), turned_d=((2 * HEAD, PADDED), BF), shift=((1, PADDED), F32),
    total_q=((HEAD, PADDED), F32), stage_q=((CHIPS, HEAD, CHIP_ROWS), BF),
    stage_kv=((2 * HEAD, LENGTH), BF),
)
BACK_OUTPUTS = dict(
    d_q_t=((CHIPS, HEAD, CHIP_ROWS), BF), d_kv_t=((CHIPS, 2 * HEAD, CHIP_ROWS), BF)
)


REST = ((64, HALF), (80, HALF // 2), (80, HALF // 2))


def dot_nt(former, latter):
    return lax.dot_general(former, latter, (((1,), (1,)), ((), ())), preferred_element_type=F32)


QKV, OUT, IN, BACK = range(4)


class Weights:
    def __init__(self, refs, wire, names):
        self.refs, self.pending = refs, {}
        for name in names:
            if name == QKV:
                pairs = [(refs.gqkv, refs.w_qkv)]
            elif name == IN:
                pairs = [
                    (refs.rest_one.at[CUBE_ALL + (pl.ds(16 * k, 16),)], refs.w_in.at[k])
                    for k in range(4)
                ]
            elif name == OUT:
                pairs = [(refs.gout, refs.w_out)]
            else:
                pairs = [(refs.gback, refs.w_back)]
            self.pending[name] = [wire.fetch(*pair) for pair in pairs]

    def ready(self, name):
        for copy in self.pending.pop(name, []):
            copy.wait()

    def qkv(self, k):
        self.ready(QKV)
        return self.refs.w_qkv[k].reshape(D, HALF)

    def out(self, half):
        self.ready(OUT)
        return self.refs.w_out[half].reshape(HALF, HALF)

    def into(self, chunk):
        self.ready(IN)
        return self.refs.w_in[chunk].reshape(D, HALF)

    def back(self, half, chunk):
        self.ready(BACK)
        return self.refs.w_back[half, chunk // 2, chunk % 2].reshape(HALF, HALF)


def columns(k):
    return slice(k * HALF, k * HALF + HALF)


def vector(refs, k):
    return refs.vecs[k : k + 1, :]


def half_vector(refs, core, k):
    return refs.vecs[k : k + 1, pl.ds(pl.multiple_of(core * HALF, HALF), HALF)]


B_QUERY, B_VALUE, B_OUT, GAIN_ATTN, SHIFT_ATTN, B_BACK, GAIN_FFN, SHIFT_FFN = range(8)


def normalized(tensor):
    centred = tensor - jnp.mean(tensor, axis=-1, keepdims=True)
    factor = lax.rsqrt(jnp.mean(centred * centred, axis=-1, keepdims=True) + EPSILON)
    return centred * factor, factor


def normalize_back(grad_out, normed, factor, gain):
    grad_normed = grad_out * gain
    grad_input = factor * (
        grad_normed
        - jnp.mean(grad_normed, axis=-1, keepdims=True)
        - normed * jnp.mean(grad_normed * normed, axis=-1, keepdims=True)
    )
    return (
        grad_input,
        jnp.sum(grad_out * normed, axis=0, keepdims=True),
        jnp.sum(grad_out, axis=0, keepdims=True),
    )


def row_sum(tensor):
    return jnp.sum(widen(tensor), axis=0, keepdims=True)


def gelu_pair(v):
    root = math.sqrt(2.0 / math.pi)
    squared = v * v
    bent = jnp.tanh(root * v * (1.0 + 0.044715 * squared))
    half = 0.5 + 0.5 * bent
    slope = half + (0.5 * root) * v * (1.0 - bent * bent) * (1.0 + (3 * 0.044715) * squared)
    return v * half, slope


def summed_over_cores(refs, wire, fill):
    send, come, kept = refs.outgoing.at[refs.round], refs.incoming.at[refs.round], refs.kept
    refs.round += 1
    fill(wire.other, send)
    copy = wire.swap(send, come)
    fill(wire.own, kept)
    copy.wait()
    return kept[...] + widen(come[...])


def project_rows(refs, wire, weight, copy, between):
    entry, rows_of, stage = refs.entry, refs.qkv_rows, refs.qkv_stage
    biases = (half_vector(refs, wire.core, B_QUERY), None, half_vector(refs, wire.core, B_VALUE))

    def project(rows, k):
        result = dot(entry[rows, :], weight(k))
        if biases[k] is not None:
            result = result + biases[k]
        rows_of[k, rows, :] = bfloat(result)

    for k in range(3):
        project(wire.own, k)
    copy.wait()
    refs.keep(entry)
    between()
    copies = []
    for k in range(3):
        project(wire.other, k)
        stage[k] = rows_of[k].T.reshape(CHIPS, HEAD, CHIP_ROWS)
        copies += wire.spread(stage.at[k], refs.qkv.at[k])
    return copies


def part_project(refs, wire, weights, hidden):
    entry = refs.entry
    entry[wire.own, :] = bfloat(hidden)
    copy = wire.swap(entry.at[wire.own], entry.at[wire.own])
    return project_rows(refs, wire, weights.qkv, copy, lambda: None)


def part_post(refs, wire, weights):
    mixed = refs.mixed
    mixed[...] = refs.mixed_t_in[...].reshape(HALF, CHIP_ROWS).T

    def leave(rows, target):
        for half in range(2):
            target[:, columns(half)] = dot(mixed[rows, :], weights.out(half)).astype(target.dtype)

    branch = summed_over_cores(refs, wire, leave)
    normed, factor = normalized(widen(refs.hidden[...]) + branch + vector(refs, B_OUT))
    refs.normed_one[...] = normed
    refs.factor_one[...] = factor
    refs.keep(refs.normed_one, refs.factor_one)
    first = normed * vector(refs, GAIN_ATTN) + vector(refs, SHIFT_ATTN)
    refs.first[...] = first
    entry_two, active, slope = refs.entry_two, refs.active, refs.slope
    entry_two[wire.own, :] = bfloat(first)
    copy = wire.swap(entry_two.at[wire.own], entry_two.at[wire.own])

    def inner(rows):
        for chunk in range(4):
            start = pl.multiple_of(wire.core * 2048 + chunk * HALF, HALF)
            before = dot(entry_two[rows, :], weights.into(chunk)) + refs.b_in[:, pl.ds(start, HALF)]
            value, steep = gelu_pair(before)
            active[rows, columns(chunk)] = bfloat(value)
            slope[rows, columns(chunk)] = bfloat(steep)

    inner(wire.own)
    copy.wait()
    refs.keep(entry_two)
    inner(wire.other)
    refs.keep(active, slope)

    def leave_two(rows, target):
        for half in range(2):
            total = dot(active[rows, columns(0)], weights.back(half, 0))
            for chunk in range(1, 4):
                total = total + dot(active[rows, columns(chunk)], weights.back(half, chunk))
            target[:, columns(half)] = total.astype(target.dtype)

    second = summed_over_cores(refs, wire, leave_two)
    normed, factor = normalized(refs.first[...] + second + vector(refs, B_BACK))
    refs.normed_two[...] = normed
    refs.factor_two[...] = factor
    refs.keep(refs.normed_two, refs.factor_two)
    return normed * vector(refs, GAIN_FFN) + vector(refs, SHIFT_FFN)


def part_back_dense(refs, wire, weights, grad_out):
    d_branch, d_before, d_attn = refs.d_branch, refs.d_before, refs.d_attn
    sums = refs.sums
    d_second, g_gain, g_shift = normalize_back(
        grad_out, refs.normed_two[...], refs.factor_two[...], vector(refs, GAIN_FFN)
    )
    refs.d_second[...] = d_second
    d_branch[wire.own, :] = bfloat(d_second)
    copy = wire.swap(d_branch.at[wire.own], d_branch.at[wire.own])
    sums[GAIN_FFN : GAIN_FFN + 1, :] = g_gain
    sums[SHIFT_FFN : SHIFT_FFN + 1, :] = g_shift
    sums[B_BACK : B_BACK + 1, :] = row_sum(d_branch[wire.own, :])

    def inner(rows):
        for chunk in range(4):
            d_active = dot_nt(d_branch[rows, columns(0)], weights.back(0, chunk)) + dot_nt(
                d_branch[rows, columns(1)], weights.back(1, chunk)
            )
            d_before[rows, columns(chunk)] = bfloat(
                d_active * widen(refs.slope[rows, columns(chunk)])
            )

    inner(wire.own)
    copy.wait()
    refs.keep(d_branch)
    inner(wire.other)
    refs.keep(d_before)
    for chunk in range(4):
        start = pl.multiple_of(wire.core * 2048 + chunk * HALF, HALF)
        refs.sums_in[:, pl.ds(start, HALF)] = row_sum(d_before[:, columns(chunk)])

    def leave(rows, target):
        total = dot_nt(d_before[rows, columns(0)], weights.into(0))
        for chunk in range(1, 4):
            total = total + dot_nt(d_before[rows, columns(chunk)], weights.into(chunk))
        target[...] = total.astype(target.dtype)

    d_first = refs.d_second[...] + summed_over_cores(refs, wire, leave)
    d_inner, g_gain, g_shift = normalize_back(
        d_first, refs.normed_one[...], refs.factor_one[...], vector(refs, GAIN_ATTN)
    )
    refs.d_inner_out[...] = d_inner
    refs.keep(refs.d_inner_out)
    d_attn[wire.own, :] = bfloat(d_inner)
    copy = wire.swap(d_attn.at[wire.own], d_attn.at[wire.own])
    sums[GAIN_ATTN : GAIN_ATTN + 1, :] = g_gain
    sums[SHIFT_ATTN : SHIFT_ATTN + 1, :] = g_shift
    sums[B_OUT : B_OUT + 1, :] = row_sum(d_attn[wire.own, :])
    rows_of, stage = refs.d_mixed_rows, refs.d_mixed_stage

    def enter(rows):
        rows_of[rows, :] = bfloat(
            dot_nt(d_attn[rows, columns(0)], weights.out(0))
            + dot_nt(d_attn[rows, columns(1)], weights.out(1))
        )

    enter(wire.own)
    copy.wait()
    refs.keep(d_attn, refs.sums, refs.sums_in)
    enter(wire.other)
    stage[...] = rows_of[...].T.reshape(CHIPS, HEAD, CHIP_ROWS)
    return wire.spread(stage, refs.d_mixed)


def turn_queries(refs):
    refs.d_qkv[0] = refs.d_q_t[...].reshape(HALF, CHIP_ROWS).T


def turn_keys_values(refs):
    rows_of = refs.d_qkv
    rows_of[1] = refs.d_kv_t[:, :HEAD, :].reshape(HALF, CHIP_ROWS).T
    rows_of[2] = refs.d_kv_t[:, HEAD:, :].reshape(HALF, CHIP_ROWS).T


def add_half(refs, wire, k, value):
    half = pl.ds(pl.multiple_of(wire.core * HALF, HALF), HALF)
    refs.sums[k : k + 1, half] = refs.sums[k : k + 1, half] + value


def part_back_project(refs, wire, weights):
    rows_of = refs.d_qkv

    def leave(rows, target):
        total = dot_nt(rows_of[0, rows, :], weights.qkv(0))
        for k in range(1, 3):
            total = total + dot_nt(rows_of[k, rows, :], weights.qkv(k))
        target[...] = total.astype(target.dtype)

    return refs.d_inner[...] + summed_over_cores(refs, wire, leave)


ROW_F32 = ((ROWS, D), F32)
COLUMN_F32 = ((ROWS, 1), F32)
CHIP_BF = ((CHIP_ROWS, D), BF)
WIDE_BF = ((CHIP_ROWS, 2048), BF)
HEADS_BF = ((CHIP_ROWS, HALF), BF)
STAGE = (CHIPS, HEAD, CHIP_ROWS)
POST, BACK_DENSE, BACK_PROJECT, ATTEND_BACK, GRADIENTS = range(5)
WHOLE_GRADIENTS = dict(
    g_in=(CUBE + (16, 2048), BF), g_back=((2, 2, 2, 4, 64, D), BF), g_out=((2, 2, 2, 4, 16, D), BF)
)
PARTS = (
    (
        (OUT, IN, BACK),
        dict(
            normed_one=ROW_F32, factor_one=COLUMN_F32, entry_two=CHIP_BF,
            active=WIDE_BF, slope=WIDE_BF, normed_two=ROW_F32, factor_two=COLUMN_F32,
        ),
        {},
        dict(first=ROW_F32, mixed=HEADS_BF),
        4,
        0,
    ),
    (
        (BACK, IN, OUT),
        dict(
            d_branch=CHIP_BF, d_before=WIDE_BF, d_attn=CHIP_BF, d_inner_out=ROW_F32,
            sums=((8, D), F32), sums_in=((1, FF), F32),
        ),
        dict(d_mixed=((HEAD, LENGTH), BF)),
        dict(d_second=ROW_F32, d_mixed_rows=HEADS_BF, d_mixed_stage=(STAGE, BF)),
        3 + 7,
        1,
    ),
    (
        (QKV,),
        dict(d_qkv=((3, CHIP_ROWS, HALF), BF)),
        {},
        {},
        1,
        0,
    ),
    ((), {}, BACK_OUTPUTS, BACK_SCRATCH, 0, 0),
    ((), WHOLE_GRADIENTS, {}, {}, 0, 0),
)
WEIGHT_SHAPES = (
    dict(w_qkv=((3,) + CUBE + (16, HALF), BF)),
    dict(w_out=((2, 2, 2, 2, 4, 16, HALF), BF)),
    dict(w_in=((4,) + CUBE + (16, HALF), BF)),
    dict(w_back=((2, 2, 2, 2, 4, 64, HALF), BF)),
)


WEIGHT_COPIES = (1, 1, 4, 1)


def weight_gradients(refs, mixed_t, add, ready):
    def store(ref, at, value):
        value = value.reshape(ref[at].shape)
        ref[at] = bfloat(value + widen(ref[at])) if add else bfloat(value)

    for chunk in range(4):
        value = dot(refs.active[:, columns(chunk)].T, refs.d_branch[...])
        store(refs.g_back, (chunk // 2, chunk % 2), value)
    refs.keep(refs.g_back)
    store(refs.g_out, CUBE_ALL, dot(mixed_t.reshape(HALF, CHIP_ROWS), refs.d_attn[...]))
    refs.keep(refs.g_out)
    ready()
    turned = refs.entry_two[...].T
    for chunk in range(4):
        value = dot(turned, refs.d_before[:, columns(chunk)])
        store(refs.g_in, CUBE_ALL + (EVERY, columns(chunk)), value)
    refs.keep(refs.g_in)


def dense(
    parts, number, gathered, loaded, late, extra, dropped=(), sources={}, added={}
):
    outputs, saved, weight_names, sems = {}, dict(extra), [], []
    rounds = 2 * (POST in parts) + (BACK_DENSE in parts) + (BACK_PROJECT in parts)
    sums = ((rounds, ROWS, D), BF)
    scratch = dict(outgoing=sums, incoming=sums, kept=ROW_F32)
    copies = locals_ = 0
    for part in parts:
        its_weights, its_saved, its_outputs, its_scratch, its_copies, its_locals = PARTS[part]
        weight_names += [name for name in its_weights if name not in weight_names]
        outputs.update(its_outputs)
        saved.update(its_saved)
        scratch.update(its_scratch)
        copies += its_copies
        locals_ += its_locals
    for name, value in late.items():
        scratch[name] = (value.shape, value.dtype)
    for name in dropped:
        scratch[name] = {**saved, **outputs}[name]
        saved.pop(name, None)
        outputs.pop(name, None)
    for name in weight_names:
        scratch.update(WEIGHT_SHAPES[name])
        locals_ += WEIGHT_COPIES[name]
    far = {}
    if added:
        far = dict(come_back=((2, 2, 2, 4, 64, HALF), BF), come_out=((2, 2, 2, 4, 16, HALF), BF))
    if ATTEND_BACK in parts:
        sems = MAIL_SEMS + MAIL_SEMS + [dma(SLOTS)]

    def body(refs, semaphores):
        here = place()
        wire = Wire(here, *semaphores[:3])
        refs.round = 0
        weights = Weights(refs, wire, weight_names)
        after_first = []
        if BACK_DENSE in parts:
            refs.sums[...] = jnp.zeros((8, D), F32)
            refs.sums_in[...] = jnp.zeros((1, FF), F32)
        if ATTEND_BACK in parts:
            refs.attend_local = semaphores[-1]
        greet([partner(here)] + group(here))
        refs.arrive()
        pending = []
        value = None
        for step, part in enumerate(parts):
            if step == 1:
                for key in (*late, *added):
                    after_first.append(wire.fetch(getattr(refs, key + LATER), getattr(refs, key)))
                if ATTEND_BACK in parts:
                    fetch_chances(refs)
            if part == POST:
                value = part_post(refs, wire, weights)
                refs.result[...] = value.astype(refs.result.dtype)
                refs.keep(refs.result)
            elif part == BACK_DENSE:
                if POST in parts:
                    value = widen(refs.cotangent[...])
                pending += part_back_dense(refs, wire, weights, value)
            elif part == BACK_PROJECT:
                turn_queries(refs)
                turn_keys_values(refs)
                refs.keep(refs.d_qkv)
                add_half(refs, wire, B_QUERY, row_sum(refs.d_qkv[0]))
                add_half(refs, wire, B_VALUE, row_sum(refs.d_qkv[2]))
                value = part_back_project(refs, wire, weights)
            elif part == GRADIENTS:
                for copy in after_first:
                    copy.wait()

                def ready():
                    if added:
                        low = pl.multiple_of((1 - wire.core) * HALF, HALF)
                        span = CUBE_ALL + (EVERY, pl.ds(low, HALF))
                        pending.append(wire.swap(refs.g_back.at[span], refs.come_back))
                        pending.append(wire.swap(refs.g_out.at[span], refs.come_out))

                weight_gradients(refs, refs.mixed_t_in[...], bool(added), ready)
            else:
                for copy in pending:
                    copy.wait()
                pending = []
                send, recv, send_two, recv_two, _ = semaphores[3:]
                attend_back_steps(
                    refs, Mail(here, send, recv), Mail(here, send_two, recv_two), lambda slot: None
                )
        for copy in pending:
            copy.wait()

    return call(
        body, "dense_%d" % number, number, {},
        dict(loaded, vecs=gathered.vecs, b_in=gathered.b_in),
        dict(
            sources, gqkv=gathered.gqkv, gout=gathered.gout, gback=gathered.gback,
            rest_one=gathered.rest_one,
            **{key + LATER: value for key, value in (*late.items(), *added.items())},
        ),
        outputs, saved, far, scratch, [dma(copies + 2), dma(copies + 2), dma(locals_ + 6)] + sems,
    )


LATER = "_later"


class Arriving(Weights):
    def __init__(self, refs, pending):
        self.refs, self.pending = refs, pending

    def ready(self, name):
        self.pending.pop(name, lambda: None)()


LAYER_SAVED = dict(
    mixed_head=((HEAD, LENGTH), F32), inverse=((1, LENGTH), F32), entry=CHIP_BF,
    qkv=((3, HEAD, LENGTH), BF),
)
SECOND = "_second"


def opening(lengths, pads, shards, vectors, tokens, number):
    def body(refs, semaphores):
        send, recv, local = semaphores[:3]
        here = place()
        wire = Wire(here, send, recv, local)
        core = wire.core
        refs.round = 0
        greet(neighbours(here, (1, -1, 2)) + group(here))
        refs.arrive()
        tok = lax.axis_index("tok")
        lanes = lax.broadcasted_iota(jnp.int32, (1, 128), 1)
        line = widen(refs.vectors[...])
        rows = []
        for k in range(8):
            turned = pltpu.roll(line, lax.rem(tok * 8 - 8 * k + 128, 128), 1)
            rows.append(jnp.where(lanes // 8 == tok, turned, 0.0))
        turned = pltpu.roll(line, lax.rem(lax.rem(tok, 4) * 32 + 64, 128), 1)
        turned = jnp.where(lanes // 32 == lax.rem(tok, 4), turned, 0.0)
        for k in range(4):
            rows.append(jnp.where(lax.div(tok, 4) == k, turned, jnp.zeros_like(turned)))
        rows.append(jnp.zeros((4, 128), F32))
        refs.small[...] = bfloat(jnp.concatenate(rows, axis=0))
        thin = [widen(ref[...]) for ref in (refs.s_query, refs.s_key, refs.s_value, refs.s_out)]
        wide, back = widen(refs.s_in[...]), refs.s_back[...]
        for half in range(2):
            span = columns(half)
            spread = [wide[:, columns(4 * half + k)] for k in range(4)]
            pieces = [thin[k][:, span] for k in range(3)] + spread[:3]
            refs.pack[half, 0:48, :] = bfloat(jnp.concatenate(pieces, axis=0))
            refs.pack[half, 48:80, :] = back[:, span]
            refs.pack[half, 80:96, :] = bfloat(
                jnp.concatenate([spread[3], thin[3][:, span]], axis=0)
            )
        swaps = [
            wire.swap(refs.pack.at[1 - core], refs.theirs),
            wire.swap(refs.small, refs.small_theirs),
        ]
        entry = refs.entry
        entry[wire.own, :] = refs.tokens[...]
        entry_copy = wire.swap(refs.tokens, entry.at[wire.own])
        for copy in swaps:
            copy.wait()

        def build(low, high):
            low, high = widen(low), widen(high)

            def both(row):
                return bfloat(jnp.concatenate([low[row : row + 8], high[row : row + 8]], axis=0))

            for k in range(3):
                refs.own_qkv[k] = both(8 * k)
                refs.own_one[16 * k : 16 * k + 16, :] = both(24 + 8 * k)
            refs.own_one[48:64, :] = both(80)
            back = bfloat(jnp.concatenate([low[48:80], high[48:80]], axis=0))
            refs.own_out[...] = both(88)
            refs.own_two[...] = back[:, 0:256]
            refs.own_three[...] = back[:, 256:512]

        @pl.when(core == 0)
        def _():
            build(refs.pack[0], refs.theirs[...])

        @pl.when(core == 1)
        def _():
            build(refs.theirs[...], refs.pack[1])

        refs.own_small[...] = refs.small[...] + refs.small_theirs[...]

        def nothing(value):
            pass

        parts = [
            (refs.w_qkv, (k,), GATHER_ORDERS[k], refs.own_qkv.at[k], HALF, nothing)
            for k in range(3)
        ]
        for k, ref in enumerate((refs.all_out, refs.all_out_two)):
            own = refs.own_out.at[:, side_columns(HALF, k)]
            parts.append((ref, (), GATHER_ORDERS[1 + k], own, HALF // 2, nothing))
        parts.append((refs.all_small, (), GATHER_ORDERS[3], refs.own_small, 0, nothing))
        first_stages = ring_gather(wire, parts)
        mine, yours = pl.ds(2 * core, 2), pl.ds(2 * (1 - core), 2)
        taken, passed = [], []

        def take_one(value):
            for k in range(4):
                taken.append(
                    wire.fetch(
                        refs.rest_one.at[value, :, :, :, pl.ds(16 * k, 16)], refs.w_in.at[k, value]
                    )
                )

        def pass_part(ref, side, place_of):
            def take(value):
                target = refs.w_back.at[
                    (core, EVERY) + place_of(value) + (EVERY, side_columns(HALF, side))
                ]
                passed.append(wire.swap(ref.at[(yours,) + place_of(value)], target))
                passed.append(wire.fetch(ref.at[(mine,) + place_of(value)], target))

            return take

        pass_two = pass_part(refs.rest_two, 0, lambda z: (EVERY, EVERY, z))
        pass_three = pass_part(refs.rest_three, 1, lambda x: (x % 2, x // 2, EVERY))

        long_stages = ring_gather(
            wire, [(refs.rest_one, (), GATHER_ORDERS[0], refs.own_one, HALF, take_one)]
        )
        stages = ring_gather(
            wire,
            [
                (refs.rest_two, (), GATHER_ORDERS[1], refs.own_two, HALF // 2, pass_two),
                (refs.rest_three, (), GATHER_ORDERS[2], refs.own_three, HALF // 2, pass_three),
            ],
        )
        for ring in (first_stages, long_stages, stages, first_stages, first_stages, long_stages):
            advance(ring)
        advance(stages)
        for _ in first_stages:
            pass
        kept = wire.fetch(refs.w_qkv, refs.gqkv)
        out_copies = []
        for k, ref in enumerate((refs.all_out, refs.all_out_two)):
            into = refs.w_out.at[(core,) + (EVERY,) * 5 + (side_columns(HALF, k),)]
            out_copies += [wire.swap(ref.at[yours], into), wire.fetch(ref.at[mine], into)]
        for s in range(8):
            tile = jnp.zeros((16, 128), F32)
            for x_hi in range(2):
                for z in range(4):
                    tile = tile + widen(refs.all_small[s // 2, s % 2, x_hi, z])
            refs.vecs[:, 128 * s : 128 * s + 128] = tile[:8]
            for j in range(4):
                low = HALF * s + 128 * j
                refs.b_in[:, low : low + 128] = tile[8 + j : 9 + j]
        refs.keep(refs.vecs, refs.b_in)
        refs.attend_local = semaphores[5]
        pending = project_rows(
            refs, wire, lambda k: refs.w_qkv[k].reshape(D, HALF), entry_copy, lambda: advance(long_stages)
        )
        for copy in pending[: 2 * CHIPS]:
            copy.wait()

        def values_ready():
            for copy in pending[2 * CHIPS :]:
                copy.wait()
            refs.keep(refs.qkv)
            advance(stages)

        def between(slot):
            if slot == 0:
                advance(long_stages)
            elif slot == 2:
                advance(stages)
            elif slot == 3:
                advance(long_stages)

        attend_steps(refs, Mail(here, *semaphores[3:5]), values_ready, between)

        def out_ready():
            for copy in out_copies:
                copy.wait()
            refs.keep(refs.w_out)

        def in_ready():
            advance(stages)
            for _ in long_stages:
                pass
            for copy in taken:
                copy.wait()

        def back_ready():
            for _ in stages:
                pass
            for copy in passed:
                copy.wait()
            refs.keep(refs.w_back)

        mixed_copy = wire.fetch(refs.mixed_t, refs.mixed_t_one)
        weights = Arriving(refs, {OUT: out_ready, IN: in_ready, BACK: back_ready})
        refs.mixed_t_in = refs.mixed_t
        refs.hidden = refs.tokens
        value = part_post(refs, wire, weights)
        refs.result[...] = value
        refs.keep(refs.result)
        second = types.SimpleNamespace(**vars(refs))
        second.attend_local = semaphores[-1]
        for name in [*LAYER_SAVED, *MIXED_T, CHANCES_NAME]:
            setattr(second, name, getattr(refs, name + SECOND))
        pending = part_project(second, wire, weights, value)
        for copy in pending[: 2 * CHIPS]:
            copy.wait()

        def second_ready():
            for copy in pending[2 * CHIPS :]:
                copy.wait()
            refs.keep(second.qkv)

        attend_steps(second, Mail(here, *semaphores[6:8]), second_ready, lambda slot: None)
        kept.wait()
        mixed_copy.wait()

    cube_16 = (CUBE + (16, HALF // 2), BF)
    scratch = dict(
        ATTEND_SCRATCH, pack=((2, 96, HALF), BF), small=((16, 128), BF), theirs=((96, HALF), BF),
        small_theirs=((16, 128), BF), own_qkv=((3, 16, HALF), BF), own_out=((16, HALF), BF),
        own_one=((64, HALF), BF), own_two=((64, HALF // 2), BF), own_three=((64, HALF // 2), BF),
        own_small=((16, 128), BF), w_qkv=((3,) + CUBE + (16, HALF), BF), all_out=cube_16, all_out_two=cube_16,
        all_small=(CUBE + (16, 128), BF), qkv_rows=((3, CHIP_ROWS, HALF), BF),
        qkv_stage=((3,) + STAGE, BF), outgoing=((2, ROWS, D), BF), incoming=((2, ROWS, D), BF),
        kept=ROW_F32, first=ROW_F32, mixed=HEADS_BF, mixed_t=MIXED_T[MIXED_NAME],
    )
    scratch.update(WEIGHT_SHAPES[IN])
    saved = dict(LAYER_SAVED, vecs=((8, D), F32), b_in=((1, FF), F32), result=ROW_F32)
    saved.update(WEIGHT_SHAPES[OUT])
    saved.update(WEIGHT_SHAPES[BACK])
    saved.update(PARTS[POST][1])
    saved.update({name + SECOND: spec for name, spec in LAYER_SAVED.items()})
    narrow = (CUBE + (64, HALF // 2), BF)
    copies = 3 + 9 * GATHER_COPIES + 10 + 2 * 21 + 4
    result = call(
        body, "opening", number, {}, dict(shards, vectors=vectors, tokens=tokens), {},
        {MIXED_NAME + SECOND: MIXED_T[MIXED_NAME]}, saved,
        dict(
            chances=CHANCES, chances_second=CHANCES, gqkv=((3,) + CUBE + (16, HALF), BF),
            rest_one=(CUBE + (64, HALF), BF), rest_two=narrow, rest_three=narrow,
            mixed_t_one=MIXED_T[MIXED_NAME],
        ),
        scratch,
        [dma(copies), dma(copies), dma(46)] + (MAIL_SEMS + [dma(SLOTS + 1)]) * 2,
        dict(lengths=lengths, pads=pads),
    )
    result.gout, result.gback = result.w_out, result.w_back
    return result


MIXED_NAME, CHANCES_NAME = "mixed_t", "chances"


def closing(near, loaded, sources, number):
    rest_slots = [scatter_slots(order, *REST[k], True) for k, order in enumerate(SCATTER_ORDERS[:3])]

    def body(refs, semaphores):
        send, recv, local, send_q, recv_q, send_kv, recv_kv, refs.attend_local = semaphores
        here = place()
        wire = Wire(here, send, recv, local)
        core = wire.core
        refs.round = 0
        mine, yours = pl.ds(2 * core, 2), pl.ds(2 * (1 - core), 2)
        blocks, inner, copies = (EVERY,) * 3, [], []
        for side, ref in enumerate((refs.rest_two, refs.rest_three)):
            low = pl.multiple_of(core * HALF + side * (HALF // 2), HALF // 2)
            here_columns = CUBE_ALL + (EVERY, pl.ds(low, HALF // 2))
            come_columns = CUBE_ALL + (EVERY, side_columns(HALF, side))
            for rows, gradient, come in (
                (pl.ds(0, 64), refs.g_back, refs.come_back),
                (pl.ds(64, 16), refs.g_out, refs.come_out),
            ):
                copies.append(
                    wire.fetch(gradient.at[here_columns], ref.at[(mine,) + blocks + (rows,)])
                )
                copies.append(
                    wire.fetch(come.at[come_columns], ref.at[(yours,) + blocks + (rows,)])
                )
        for k in range(4):
            source = refs.g_in.at[CUBE_ALL + (EVERY, pl.ds(k * HALF, HALF))]
            inner.append(wire.fetch(source, refs.rest_one.at[CUBE_ALL + (pl.ds(16 * k, 16),)]))
        greet(neighbours(here, (1, -1, 2)) + group(here))
        refs.arrive()

        def keep_rest(part):
            def store(value):
                (refs.sums_one, refs.sums_two, refs.sums_six)[part][...] = value

            return store

        rest_arrivals = [
            [getattr(refs, "rest_%d_%d" % (part, k)) for k in range(4)] for part in range(3)
        ]
        rest = [
            (ref, (), SCATTER_ORDERS[part], REST[part][1], rest_arrivals[part], keep_rest(part))
            for part, ref in enumerate((refs.rest_one, refs.rest_two, refs.rest_three))
        ]
        long_stages = ring_scatter(wire, rest[:1], (0, 1, 2))
        rest_stages = ring_scatter(wire, rest[1:], (0, 1, 2))
        for copy in inner:
            copy.wait()
        advance(long_stages)
        fetch_chances(refs)
        weights = Weights(refs, wire, (QKV,))

        def keep(part):
            def store(value):
                if part == 3:
                    refs.tiny[...] = value
                else:
                    refs.final[part] = value

            return store

        arrivals = [
            [getattr(refs, "slot_%d_%d" % (part, k)) for k in range(4)] for part in range(4)
        ]
        parts = [
            (refs.gradients, (part,), SCATTER_ORDERS[part], HALF, arrivals[part], keep(part))
            for part in range(3)
        ]
        parts.append((refs.small_sums, (), SCATTER_ORDERS[3], 0, arrivals[3], keep(3)))
        early_stages = ring_scatter(wire, parts[1:3], (0, 1, 2))
        stages = ring_scatter(wire, parts[:1] + parts[3:], (0, 1, 2))

        def add_gradient(k):
            total = dot(refs.entry_t[...], refs.d_qkv[k]).reshape(CUBE + (16, HALF))
            refs.gradients[k] = bfloat(widen(refs.gradients[k]) + total)

        def between(slot):
            if slot == -1:
                for copy in copies:
                    copy.wait()
                advance(rest_stages)
                turned = refs.entry_later[...].T
                for k in range(3):
                    total = dot(turned, refs.d_qkv_later[k])
                    refs.gradients[k] = bfloat(total).reshape(CUBE + (16, HALF))
                refs.entry_t[...] = refs.entry[...].T
                refs.sums[...] = refs.sums_three[...] + refs.sums_four[...]
                refs.sums_in[...] = refs.in_three[...] + refs.in_four[...]
            elif slot == 0:
                advance(rest_stages)
            elif slot == 1:
                advance(long_stages)
            elif slot == SLOTS:
                advance(long_stages)
            elif slot == SLOTS + 1:
                turn_keys_values(refs)
                add_gradient(1)
                add_gradient(2)
                advance(early_stages)
                advance(rest_stages)

        attend_back_steps(
            refs, Mail(here, send_q, recv_q), Mail(here, send_kv, recv_kv), between
        )
        turn_queries(refs)
        add_half(refs, wire, B_QUERY, row_sum(refs.d_qkv[0]))
        add_half(refs, wire, B_VALUE, row_sum(refs.d_qkv[2]))
        swaps = [wire.swap(refs.sums, refs.sums_come), wire.swap(refs.sums_in, refs.in_come)]
        add_gradient(0)
        for copy in swaps:
            copy.wait()
        both = refs.sums[...] + refs.sums_come[...]
        both_in = refs.sums_in[...] + refs.in_come[...]
        for s in range(8):
            pieces = [both[:, 128 * s : 128 * s + 128]]
            for j in range(4):
                low = HALF * s + 128 * j
                pieces.append(both_in[:, low : low + 128])
            pieces.append(jnp.zeros((4, 128), F32))
            tile = bfloat(jnp.concatenate(pieces, axis=0))
            for x_hi in range(2):
                for z in range(4):
                    refs.small_sums[s // 2, s % 2, x_hi, z] = tile
        advance(stages)
        advance(rest_stages)
        advance(long_stages)
        advance(early_stages)
        advance(stages)
        refs.d_tokens[...] = bfloat(part_back_project(refs, wire, weights))
        for _ in range(3):
            advance(early_stages)
            advance(stages)
        for ring in (rest_stages, long_stages, early_stages, stages):
            for _ in ring:
                pass

        def finish(own):
            def both(low, count):
                span = slice(low, low + count)
                return jnp.concatenate([refs.sums_two[span, :], refs.sums_six[span, :]], axis=1)

            rows = [refs.final[k, 8 * own : 8 * own + 8, :] for k in range(3)]
            rows.append(both(64 + 8 * own, 8))
            for k in range(4):
                rows.append(refs.sums_one[16 * k + 8 * own : 16 * k + 8 * own + 8, :])
            rows.append(both(32 * own, 32))
            return jnp.concatenate(rows, axis=0)

        @pl.when(core == 0)
        def _():
            refs.leaving[...] = finish(1)
            refs.landed[0] = finish(0)

        @pl.when(core == 1)
        def _():
            refs.leaving[...] = finish(0)
            refs.landed[1] = finish(1)

        wire.swap(refs.leaving, refs.landed.at[core]).wait()
    few = ((8, D), F32)
    scratch = dict(
        BACK_SCRATCH, **BACK_OUTPUTS, outgoing=((1, ROWS, D), BF), incoming=((1, ROWS, D), BF),
        kept=ROW_F32, entry_t=((D, CHIP_ROWS), BF), d_qkv=((3, CHIP_ROWS, HALF), BF), sums=few, sums_in=((1, FF), F32), sums_come=few,
        in_come=((1, FF), F32), gradients=((3,) + CUBE + (16, HALF), BF),
        small_sums=(CUBE + (16, 128), BF), final=((3, 16, HALF), F32),
        leaving=((96, HALF), F32), sums_one=(REST[0], F32), sums_two=(REST[1], F32),
        sums_six=(REST[2], F32), rest_one=(CUBE + REST[0], BF), rest_two=(CUBE + REST[1], BF),
        rest_three=(CUBE + REST[2], BF),
    )
    scratch.update(WEIGHT_SHAPES[QKV])
    for part in range(4):
        slots = scatter_slots(SCATTER_ORDERS[part], 16, HALF if part < 3 else 128, part < 3)
        for k in range(4):
            scratch["slot_%d_%d" % (part, k)] = slots[k]
    for part in range(3):
        for k in range(4):
            scratch["rest_%d_%d" % (part, k)] = rest_slots[part][k]
    copies = 7 * sum(SCATTER_COPIES) + 8
    return call(
        body, "closing", number, near, loaded, sources,
        dict(
            d_tokens=((ROWS, D), BF), landed=((2, 96, HALF), F32), tiny=((16, 128), F32),
        ),
        {}, {}, scratch,
        [dma(copies), dma(copies), dma(13)] + MAIL_SEMS + MAIL_SEMS + [dma(SLOTS)],
    )


def unpack_kernel(
    result, d_tokens, landed, tiny, o_result, o_tokens, o_query, o_key, o_value, o_out, o_in, o_back,
    o_vectors,
):
    o_result[...] = result[...]
    o_tokens[...] = d_tokens[...]
    for column in (0, 1):
        span = columns(column)
        for piece, ref in enumerate((o_query, o_key, o_value, o_out)):
            ref[:, span] = landed[column, 8 * piece : 8 * piece + 8, :]
        for chunk in range(4):
            o_in[:, columns(4 * column + chunk)] = landed[
                column, 32 + 8 * chunk : 40 + 8 * chunk, :
            ]
        o_back[:, span] = landed[column, 64:96, :]
    tok = lax.axis_index("tok")
    o_vectors[0:8, :] = pltpu.roll(tiny[0:8, :], lax.rem(128 - tok * 8, 128), 1)
    wide = tiny[8:9, :]
    for k in range(1, 4):
        wide = jnp.where(lax.div(tok, 4) == k, tiny[8 + k : 9 + k, :], wide)
    wide = pltpu.roll(wide, lax.rem(128 - lax.rem(tok, 4) * 32, 128), 1)
    o_vectors[8:16, :] = jnp.broadcast_to(wide, (8, 128))


def unpack(result, d_tokens, landed, tiny):
    vmem = pl.BlockSpec(memory_space=pltpu.VMEM)
    few = ((8, D), F32)
    specs = (
        ((ROWS, D), BF), ((ROWS, D), BF), few, few, few, few, ((8, FF), F32), ((32, D), F32),
        ((16, 128), F32),
    )
    return pl.pallas_call(
        unpack_kernel,
        out_shape=tuple(jax.ShapeDtypeStruct(*spec) for spec in specs),
        in_specs=[vmem] * 4,
        out_specs=(vmem,) * len(specs),
        name="unpack",
        compiler_params=pltpu.CompilerParams(vmem_limit_bytes=58 * 2**20),
    )(result, d_tokens, landed, tiny)


def on_device(
    tokens, cotangent, doc_lengths, pad_counts, w_query, b_query, w_key, w_value, b_value, w_out,
    b_out, gain_attn, shift_attn, w_in, b_in, w_back, b_back, gain_ffn, shift_ffn,
):
    vectors = jnp.concatenate(
        [
            b_query, b_value, b_out, gain_attn, shift_attn, b_back, gain_ffn, shift_ffn, b_in,
            jnp.zeros((32,), BF),
        ]
    )
    one = opening(
        doc_lengths, pad_counts,
        dict(
            s_query=w_query, s_key=w_key, s_value=w_value, s_out=w_out, s_in=w_in, s_back=w_back
        ),
        widen(vectors)[None], tokens, 0,
    )
    three = dense(
        (POST, BACK_DENSE, GRADIENTS, ATTEND_BACK), 4, one,
        dict(mixed_t_in=one.mixed_t_second, hidden=one.result, cotangent=cotangent),
        dict(
            qkv=one.qkv_second, mixed_head=one.mixed_head_second, inverse=one.inverse_second,
        ),
        dict(result=((ROWS, D), BF)),
        (
            "normed_one", "factor_one", "entry_two", "active", "slope", "normed_two",
            "factor_two", "d_branch", "d_before", "d_attn", "d_mixed",
        ),
        dict(chances=one.chances_second),
    )
    four = dense(
        (BACK_PROJECT, BACK_DENSE, GRADIENTS), 6, one,
        dict(
            d_q_t=three.d_q_t, d_kv_t=three.d_kv_t, d_inner=three.d_inner_out,
            normed_one=one.normed_one, factor_one=one.factor_one, normed_two=one.normed_two,
            factor_two=one.factor_two, slope=one.slope,
        ),
        dict(entry_two=one.entry_two, active=one.active, mixed_t_in=one.mixed_t_one),
        {}, ("d_branch", "d_before", "d_attn"),
        added=dict(g_in=three.g_in, g_back=three.g_back, g_out=three.g_out),
    )
    last = closing(
        {},
        dict(
            d_mixed=four.d_mixed,
            qkv=one.qkv, mixed_head=one.mixed_head, inverse=one.inverse, d_inner=four.d_inner_out,
            entry=one.entry, entry_later=one.entry_second, d_qkv_later=four.d_qkv, sums_three=three.sums,
            sums_four=four.sums, in_three=three.sums_in, in_four=four.sums_in,
        ),
        dict(
            chances=one.chances, gqkv=one.gqkv, g_in=four.g_in, g_back=four.g_back, g_out=four.g_out,
            come_back=four.come_back, come_out=four.come_out,
        ),
        8,
    )
    result, d_tokens, g_query, g_key, g_value, g_out, g_in, g_back, lines = unpack(
        three.result, last.d_tokens, last.landed, last.tiny
    )
    (
        g_b_query, g_b_value, g_b_out, g_gain_attn, g_shift_attn, g_b_back, g_gain_ffn, g_shift_ffn,
    ) = [lines[k, :8] for k in range(8)]
    return (
        result, d_tokens, g_query, g_b_query, g_key, g_value, g_b_value, g_out, g_b_out, g_gain_attn,
        g_shift_attn, g_in, lines[8, :32], g_back, g_b_back, g_gain_ffn, g_shift_ffn,
    )


def solution(mesh):
    both = ("seq", "tok")
    rows, vector = P(both, None), P(both)
    ins = (
        rows, rows, P("seq", None), P("seq"), rows, vector, rows, rows, vector, rows, vector, vector,
        vector, rows, vector, rows, vector, vector, vector,
    )
    outs = (
        rows, rows, rows, vector, rows, rows, vector, rows, vector, vector, vector, rows, vector,
        rows, vector, vector, vector,
    )
    return jax.shard_map(on_device, mesh=mesh, in_specs=ins, out_specs=outs, check_vma=False)
```

```python
import math
import types

import jax
import jax.numpy as jnp
from jax import lax
from jax.experimental import pallas as pl
from jax.experimental.pallas import tpu as pltpu
from jax.sharding import PartitionSpec as P

HEADS = 16
WINDOW = 1024
D = 1024
FF = 4096
HEAD = 64
CHIPS = 8
ROWS = 192
CHIP_ROWS = 2 * ROWS
LENGTH = CHIP_ROWS * CHIPS
HALF = 512
EPSILON = 1e-05
MASKED = -1e30
SCALE = 1.0 / math.sqrt(HEAD)
LOG2E = 1.4426950408889634
MESH = pl.DeviceIdType.MESH
BF = jnp.bfloat16
F32 = jnp.float32
CUBE = (4, 2, 2, 4)
X, Y, Z, CORE = range(4)


def bfloat(tensor):
    return tensor.astype(BF)


def widen(tensor):
    return tensor.astype(F32)


def place():
    seq, tok = lax.axis_index("seq"), lax.axis_index("tok")
    x = (tok // 8) * 2 + seq % 2
    return {X: x, Y: seq // 2, Z: (tok // 2) % 4, CORE: tok % 2}


def device(x, y, z, core):
    return (y * 2 + x % 2, (x // 2) * 8 + z * 2 + core)


def moved(here, axis, steps):
    there = dict(here)
    there[axis] = lax.rem(here[axis] + steps + 4, 4)
    return device(there[X], there[Y], there[Z], there[CORE])


def partner(here):
    return device(here[X], here[Y], here[Z], 1 - here[CORE])


def cube_index(here, whole, axis, value):
    index = []
    for name in (Y, X, Z):
        if name in whole:
            index += [slice(None)] * (2 if name == X else 1)
        else:
            at = value if name == axis else here[name]
            index += [at % 2, at // 2] if name == X else [at]
    return tuple(index)


def greet(targets):
    barrier = pltpu.get_barrier_semaphore()
    for target in targets:
        pl.semaphore_signal(barrier, inc=1, device_id=target, device_id_type=MESH)
    pl.semaphore_wait(barrier, len(targets))


def neighbours(here, steps):
    return [moved(here, axis, step) for axis in (X, Y, Z) for step in steps] + [partner(here)]


def group_device(here, number):
    seq = lax.axis_index("seq")
    return (seq, (number // 4) * 8 + (number % 4) * 2 + here[CORE])


def group_number(here):
    return (here[X] // 2) * 4 + here[Z]


def group(here):
    me = group_number(here)
    return [group_device(here, lax.rem(me + k, CHIPS)) for k in range(1, CHIPS)]


class Wire:
    def __init__(self, here, send, recv, local):
        self.send, self.recv, self.local = send, recv, local
        self.here, self.number, self.locals = here, 0, 0
        self.core, self.me = here[CORE], group_number(here)
        self.own = pl.ds(pl.multiple_of(self.core * ROWS, ROWS), ROWS)
        self.other = pl.ds(pl.multiple_of((1 - self.core) * ROWS, ROWS), ROWS)

    def to(self, source, target, device_id):
        copy = pltpu.make_async_remote_copy(
            src_ref=source,
            dst_ref=target,
            send_sem=self.send.at[self.number],
            recv_sem=self.recv.at[self.number],
            device_id=device_id,
            device_id_type=MESH,
        )
        self.number += 1
        copy.start()
        return copy

    def swap(self, source, target):
        return self.to(source, target, partner(self.here))

    def fetch(self, source, target):
        copy = pltpu.make_async_copy(source, target, self.local.at[self.locals])
        self.locals += 1
        copy.start()
        return copy

    def spread(self, stage, target):
        span = chunk_span(self.me)
        copies = []
        for k in range(1, CHIPS):
            to = lax.rem(self.me + k, CHIPS)
            copies.append(self.to(stage.at[to], target.at[:, span], group_device(self.here, to)))
        copies.append(self.fetch(stage.at[self.me], target.at[:, span]))
        return copies


def chunk_span(number):
    return pl.ds(pl.multiple_of(number * CHIP_ROWS, CHIP_ROWS), CHIP_ROWS)


EVERY = slice(None)
CUBE_ALL = (EVERY,) * 4


def side_columns(width, side):
    return pl.ds(side * (width // 2), width // 2)


SIZES = {Y: (4,), X: (2, 2), Z: (4,)}
GATHER_ORDERS = ((X, Z, Y), (Y, X, Z), (Z, Y, X), (X, Z, Y))
SCATTER_ORDERS = ((Y, Z, X), (Z, X, Y), (X, Y, Z), (Y, Z, X))


def ring_gather(wire, parts):
    here = wire.here
    sent, kept = [], []
    for buffer, prefix, order, own, _, _ in parts:
        kept.append(wire.fetch(own, buffer.at[prefix + cube_index(here, (), None, None)]))
    for phase in range(2):
        copies = []
        for step in (1, -1, 2):
            for buffer, prefix, order, own, _, _ in parts:
                axis = order[phase]
                block = buffer.at[prefix + cube_index(here, order[:phase], axis, here[axis])]
                source = own if phase == 0 else block
                copies.append(wire.to(source, block, moved(here, axis, step)))
        yield
        for copy in copies:
            copy.wait_recv()
        sent += copies
        if phase == 0:
            for copy in kept:
                copy.wait()
    first, second, onward = [], [], []

    def block_at(part, value, side):
        buffer, prefix, order, _, cut, _ = part
        index = prefix + cube_index(here, order[:2], order[2], value)
        return buffer.at[index + ((EVERY, side_columns(cut, side)) if cut else ())]

    for turn, copies in enumerate((first, second)):
        for part in parts:
            axis, cut = part[2][2], part[4]
            if cut or turn == 0:
                for side, step in enumerate((1, -1)):
                    block = block_at(part, here[axis], (side + turn) % 2)
                    copies.append(wire.to(block, block, moved(here, axis, step)))
    for _, _, order, _, _, complete in parts:
        complete(here[order[2]])
    yield
    pending = list(first)
    for part in parts:
        axis, cut = part[2][2], part[4]
        for side, step in enumerate((1, -1)):
            pending.pop(0).wait_recv()
            if cut or side == 0:
                block = block_at(part, lax.rem(here[axis] - step + 4, 4), side)
                onward.append(wire.to(block, block, moved(here, axis, step)))
    yield
    for copy in second:
        copy.wait_recv()
    for _, _, order, _, _, complete in parts:
        for step in (1, 3):
            complete(lax.rem(here[order[2]] + step, 4))
    yield
    for copy in onward:
        copy.wait_recv()
    for _, _, order, _, _, complete in parts:
        complete(lax.rem(here[order[2]] + 2, 4))
    for copy in sent + first + second + onward:
        copy.wait_send()


GATHER_COPIES = 3 + 3 + 6


def lengths_of(full):
    return tuple(n for name in (Y, X, Z) if name in full for n in SIZES[name])


def digits_of(i, lengths):
    digits = []
    for length in reversed(lengths):
        digits.append(lax.rem(i, length))
        i = lax.div(i, length)
    return tuple(digits[::-1])


def one_chip(here, full, axis, value, digits):
    digits, index = list(digits), []
    for name in (Y, X, Z):
        if name in full:
            index += [digits.pop(0) for _ in SIZES[name]]
        else:
            at = value if name == axis else here[name]
            index += [at % 2, at // 2] if name == X else [at]
    return tuple(index)


SCATTER_COPIES = (6, 3, 3)


def scatter_slots(order, rows, wide, cut):
    dims = lengths_of(order[1:])
    slots = [
        pltpu.VMEM((2,) + dims + (rows, wide // 2 if cut else wide), BF),
        pltpu.VMEM((2,) + dims + (rows, wide), BF),
    ]
    return slots + [
        pltpu.VMEM((3,) + lengths_of(order[phase + 1 :]) + (rows, wide), BF) for phase in (1, 2)
    ]


def ring_scatter(wire, parts, phases):
    here = wire.here
    sent = []
    for phase in phases:
        ahead, arriving, early = [], [], []
        for buffer, prefix, order, cut, slots, _ in parts:
            axis, full = order[phase], order[phase + 1 :]
            row = []
            if phase == 0:
                far = prefix + cube_index(here, full, axis, lax.rem(here[axis] + 2, 4))
                for side, step in enumerate((1, -1)):
                    if cut or side == 0:
                        block = buffer.at[far + ((EVERY, side_columns(cut, side)) if cut else ())]
                        row.append(wire.to(block, slots[0].at[side], moved(here, axis, step)))
                ahead.append(row)
                if cut:
                    for side, step in enumerate((1, -1)):
                        near = cube_index(here, full, axis, lax.rem(here[axis] + step + 4, 4))
                        ready = (EVERY, side_columns(cut, 1 - side))
                        early.append(
                            wire.to(
                                buffer.at[prefix + near + ready],
                                slots[1].at[(side,) + (EVERY,) * len(lengths_of(full)) + ready],
                                moved(here, axis, step),
                            )
                        )
            else:
                for k, step in enumerate((1, -1, 2)):
                    value = lax.rem(here[axis] + step + 4, 4)
                    block = buffer.at[prefix + cube_index(here, full, axis, value)]
                    row.append(
                        wire.to(block, slots[1 + phase].at[k], moved(here, axis, step))
                    )
                arriving.append(row)
            sent += row
        yield
        if phase == 0:
            for (buffer, prefix, order, cut, slots, _), row in zip(parts, ahead):
                axis, full = order[phase], order[phase + 1 :]
                pair = []
                for side, step in enumerate((1, -1)):
                    value = lax.rem(here[axis] + step + 4, 4)
                    if side < len(row):
                        row[side].wait_recv()
                        half = slots[0]
                        columns_ = side_columns(cut, side) if cut else EVERY

                        def add(
                            i, _, buffer=buffer, prefix=prefix, axis=axis, full=full, value=value,
                            half=half, side=side, columns_=columns_,
                        ):
                            digits = digits_of(i, lengths_of(full))
                            at = prefix + one_chip(here, full, axis, value, digits)
                            at += (EVERY, columns_)
                            buffer[at] = bfloat(widen(buffer[at]) + widen(half[(side,) + digits]))
                            return 0

                        lax.fori_loop(0, math.prod(lengths_of(full)), add, 0)
                    summed = (EVERY, columns_) if cut else ()
                    block = buffer.at[prefix + cube_index(here, full, axis, value) + summed]
                    target = slots[1].at[(side,) + (EVERY,) * len(lengths_of(full)) + summed]
                    pair.append(wire.to(block, target, moved(here, axis, step)))
                arriving.append(pair)
                sent += pair
            yield
        for copy in early:
            copy.wait_recv()
        sent += early
        for (buffer, prefix, order, _, slots, final), row in zip(parts, arriving):
            axis, full = order[phase], order[phase + 1 :]
            come = slots[1 + phase]
            for copy in row:
                copy.wait_recv()

            def total(
                i, _, buffer=buffer, prefix=prefix, axis=axis, full=full, come=come, final=final,
                count=len(row),
            ):
                digits = digits_of(i, lengths_of(full))
                at = prefix + one_chip(here, full, axis, here[axis], digits)
                value = widen(buffer[at])
                for k in range(count):
                    value = value + widen(come[(k,) + digits])
                if phase < 2:
                    buffer[at] = bfloat(value)
                else:
                    final(value)
                return 0

            lax.fori_loop(0, math.prod(lengths_of(full)), total, 0)
    for copy in sent:
        copy.wait_send()


def advance(stages, count=1):
    for _ in range(count):
        next(stages, None)


class Mail:
    def __init__(self, here, send, recv):
        self.here, self.me, self.send, self.recv = here, group_number(here), send, recv
        self.count = 0
        self.sent = []

    def to(self, number, source, target):
        copy = pltpu.make_async_remote_copy(
            src_ref=source,
            dst_ref=target,
            send_sem=self.send.at[self.count],
            recv_sem=self.recv.at[self.me],
            device_id=group_device(self.here, number),
            device_id_type=MESH,
        )
        self.count += 1
        copy.start()
        self.sent.append(copy)

    def finish(self, source, target):
        for k in range(1, CHIPS):
            sender = lax.rem(self.me + k, CHIPS)
            pltpu.make_async_remote_copy(
                src_ref=source,
                dst_ref=target,
                send_sem=self.send.at[0],
                recv_sem=self.recv.at[sender],
                device_id=group_device(self.here, sender),
                device_id_type=MESH,
            ).wait_recv()
        for copy in self.sent:
            copy.wait_send()


BLOCK = 256
SPAN = 1280
STEPS = LENGTH // BLOCK
SLOTS = 4
LAST_START = LENGTH - SPAN


def limits(bounds, first, count):
    places = first + lax.broadcasted_iota(jnp.int32, (1, count), 1)
    low = jnp.maximum(places - (WINDOW // 2 - 1), 0)
    high = jnp.minimum(places + WINDOW // 2, LENGTH)
    for bound in bounds:
        low = jnp.maximum(low, jnp.where(bound <= places, bound, 0))
        high = jnp.minimum(high, jnp.where(bound > places, bound, LENGTH))
    return low, high


def dot(former, latter):
    return jnp.dot(former, latter, preferred_element_type=F32)


def attend_steps(refs, mail, values_ready, between):
    qkv, mixed_t, mixed, inverse = refs.qkv, refs.mixed_t, refs.mixed_head, refs.inverse
    live, end, bounds = LENGTH - refs.pads[0], 0, []
    for k in range(4):
        end = end + refs.lengths[0, k]
        bounds.append(jnp.minimum(end, live))
    keys_rows, ones_v, chances, stage = refs.keys_rows, refs.ones_v, refs.held, refs.mixed_stage
    local = refs.attend_local
    me = mail.me
    keys_rows[...] = qkv[1].T
    ones_v[0:HEAD, :] = jnp.ones((HEAD, LENGTH), BF)
    kept = []

    def weigh(i):
        first = pl.multiple_of(i * BLOCK, BLOCK)
        start = pl.multiple_of(jnp.clip(first - 512, 0, LAST_START), BLOCK)
        scores = dot(keys_rows[pl.ds(start, SPAN), :], qkv[0, :, pl.ds(first, BLOCK)])
        low, high = limits(bounds, first, BLOCK)
        base = lax.broadcasted_iota(jnp.int32, (8, BLOCK), 0) + (start - low)
        steps = 8 * lax.broadcasted_iota(jnp.int32, (SPAN // 8, 8, BLOCK), 0)
        inside = (base[None] + steps).astype(jnp.uint32) < (high - low).astype(jnp.uint32)[None]
        scores = jnp.where(inside, scores.reshape(SPAN // 8, 8, BLOCK), MASKED)
        scores = scores.reshape(SPAN, BLOCK)
        highest = jnp.max(scores, axis=0, keepdims=True)
        chances[i] = bfloat(jnp.exp2((scores - highest) * (SCALE * LOG2E)))

    def mix(i):
        first = pl.multiple_of(i * BLOCK, BLOCK)
        start = pl.multiple_of(jnp.clip(first - 512, 0, LAST_START), BLOCK)
        out = dot(ones_v[:, pl.ds(start, SPAN)], chances[i])
        back = 1.0 / out[0:1]
        result = out[HEAD:] * back
        mixed[:, pl.ds(first, BLOCK)] = result
        stage[:, pl.ds(first, BLOCK)] = bfloat(result)
        inverse[:, pl.ds(first, BLOCK)] = back

    def each(action, slot):
        pair = lax.rem(me // 2 + 1 + slot, SLOTS)

        for t in range(3):
            action(pair * 3 + t)
        return pair

    for slot in range(SLOTS):
        if slot == 0:
            each(weigh, 0)
            each(weigh, 1)
            values_ready()
            ones_v[HEAD:, :] = qkv[2]
        elif slot < SLOTS - 1:
            each(weigh, slot + 1)
        pair = each(mix, slot)
        blocks = pl.ds(pair * 3, 3)
        copy = pltpu.make_async_copy(chances.at[blocks], refs.chances.at[blocks], local.at[slot])
        copy.start()
        kept.append(copy)
        if slot < SLOTS - 1:
            for number in (2 * pair, 2 * pair + 1):
                mail.to(number, stage.at[:, chunk_span(number)], mixed_t.at[me])
        else:
            number = me + 1 - 2 * (me % 2)
            mail.to(number, stage.at[:, chunk_span(number)], mixed_t.at[me])
            copy = pltpu.make_async_copy(
                stage.at[:, chunk_span(me)], mixed_t.at[me], local.at[SLOTS]
            )
            copy.start()
            kept.append(copy)
        between(slot)
    refs.keep(mixed, inverse)
    for copy in kept:
        copy.wait()
    mail.finish(stage.at[:, chunk_span(me)], mixed_t.at[me])


MIXED_T = dict(mixed_t=((CHIPS, HEAD, CHIP_ROWS), BF))
ATTEND_SAVED = dict(mixed_head=((HEAD, LENGTH), F32), inverse=((1, LENGTH), F32))
CHANCES = ((STEPS, SPAN, BLOCK), BF)
ATTEND_SCRATCH = dict(
    keys_rows=((LENGTH, HEAD), BF), ones_v=((2 * HEAD, LENGTH), BF), held=CHANCES,
    mixed_stage=((HEAD, LENGTH), BF),
)
MAIL_SEMS = [pltpu.SemaphoreType.DMA((CHIPS - 1,)), pltpu.SemaphoreType.DMA((CHIPS,))]


def call(
    body, name, number, near, loaded, sources, outputs, saved, far, scratch, semaphores, scalars={}
):
    vmem, hbm = pl.BlockSpec(memory_space=pltpu.VMEM), pl.BlockSpec(memory_space=pltpu.HBM)
    smem = pl.BlockSpec(memory_space=pltpu.SMEM)
    scratch = dict(scratch)
    for key, value in loaded.items():
        scratch[key] = (value.shape, value.dtype)
    scratch.update(saved)
    specs = [*outputs.values(), *saved.values(), *far.values()]

    def size(shape, dtype):
        rows, lanes = (1,) * (2 - len(shape[-2:])) + tuple(shape[-2:])
        rows, lanes = -(-rows // 8) * 8, -(-lanes // 128) * 128
        return math.prod(shape[:-2]) * rows * lanes * jnp.dtype(dtype).itemsize

    held = [(value.shape, value.dtype) for value in near.values()] + list(outputs.values())
    held += [s if isinstance(s, tuple) else (s.shape, s.dtype) for s in scratch.values()]
    limit = sum(size(*spec) for spec in held) + 10 * 2**20

    def kernel(*values):
        values = list(values)

        def take(names):
            return {key: values.pop(0) for key in names}

        refs = types.SimpleNamespace(**take(scalars), **take(near))
        heres = take(loaded)
        for key, ref in take(sources).items():
            setattr(refs, key, ref)
        for key, ref in take(outputs).items():
            setattr(refs, key, ref)
        outs = take(saved)
        for names in (far, scratch):
            for key, ref in take(names).items():
                setattr(refs, key, ref)
        copies = values.pop(0)
        pending = [
            pltpu.make_async_copy(ref, getattr(refs, key), copies.at[k])
            for k, (key, ref) in enumerate(heres.items())
        ]
        for copy in pending:
            copy.start()
        kept = []

        def arrive():
            for copy in pending:
                copy.wait()

        def keep(*arrays):
            for k, (key, out) in enumerate(outs.items()):
                if any(getattr(refs, key) is array for array in arrays):
                    copy = pltpu.make_async_copy(
                        getattr(refs, key), out, copies.at[len(heres) + k]
                    )
                    copy.start()
                    kept.append(copy)

        refs.arrive, refs.keep = arrive, keep
        body(refs, values)
        for copy in kept:
            copy.wait()

    results = pl.pallas_call(
        kernel,
        out_shape=tuple(jax.ShapeDtypeStruct(*spec) for spec in specs),
        in_specs=[smem] * len(scalars)
        + [vmem] * len(near)
        + [hbm] * (len(loaded) + len(sources)),
        out_specs=(vmem,) * len(outputs) + (hbm,) * (len(saved) + len(far)),
        scratch_shapes=[
            pltpu.VMEM(*spec) if isinstance(spec, tuple) else spec for spec in scratch.values()
        ]
        + [dma(max(1, len(loaded) + len(saved)))]
        + list(semaphores),
        name=name,
        compiler_params=pltpu.CompilerParams(
            collective_id=number, has_side_effects=True, vmem_limit_bytes=max(limit, 58 * 2**20)
        ),
    )(*scalars.values(), *near.values(), *loaded.values(), *sources.values())
    return types.SimpleNamespace(**dict(zip([*outputs, *saved, *far], results)))


def dma(count):
    return pltpu.SemaphoreType.DMA((count,))


PAD = 2 * BLOCK
PADDED = LENGTH + 2 * PAD


def fetch_chances(refs):
    copies = []
    for slot in range(SLOTS):
        blocks = pl.ds(slot * 3, 3)
        copy = pltpu.make_async_copy(
            refs.chances.at[blocks], refs.held.at[blocks], refs.attend_local.at[slot]
        )
        copy.start()
        copies.append(copy)
    refs.early = copies


def prepare_back(refs):
    qkv, turned_d, rows_q, rows_d, shift = refs.qkv, refs.turned_d, refs.rows_q, refs.rows_d, refs.shift
    refs.kv[...] = jnp.concatenate([qkv[1], qkv[2]], axis=0).T
    for edge in (0, PAD + LENGTH):
        shift[:, edge : edge + PAD] = jnp.zeros((1, PAD), F32)
        turned_d[:, edge : edge + PAD] = jnp.zeros((2 * HEAD, PAD), BF)
        rows_q[edge : edge + PAD, :] = jnp.zeros((PAD, 2 * HEAD), BF)
        rows_d[edge : edge + PAD, :] = jnp.zeros((PAD, 2 * HEAD), BF)
    middle = slice(PAD, PAD + LENGTH)
    turned_d[0:HEAD, middle] = jnp.zeros((HEAD, LENGTH), BF)
    none = jnp.zeros((HEAD, LENGTH), BF)
    rows_q[middle, :] = jnp.concatenate([qkv[0], none], axis=0).T
    refs.total_q[...] = jnp.zeros((HEAD, PADDED), F32)


def attend_back_steps(refs, mail_q, mail_kv, between):
    qkv, mixed, inverse, d_mixed = refs.qkv, refs.mixed_head, refs.inverse, refs.d_mixed
    d_q_t, d_kv_t, chances, kv = refs.d_q_t, refs.d_kv_t, refs.held, refs.kv
    rows_q, rows_d, turned_d, shift = refs.rows_q, refs.rows_d, refs.turned_d, refs.shift
    total_q, stage_q, stage_kv = refs.total_q, refs.stage_q, refs.stage_kv
    me = mail_q.me
    scaled = bfloat(widen(d_mixed[...]) * inverse[...])
    middle = slice(PAD, PAD + LENGTH)
    shift[:, middle] = jnp.sum(widen(scaled) * mixed[...], axis=0, keepdims=True)
    turned_d[HEAD:, middle] = scaled
    rows_d[middle, :] = turned_d[:, middle].T
    for copy in refs.early:
        copy.wait()
    between(-1)

    def step(i):
        first = pl.multiple_of(i * BLOCK, BLOCK)
        keys = pl.ds(first, BLOCK)
        span = pl.ds(first, SPAN)
        tiles = []
        for t in range(5):
            block = jnp.clip(i - 2 + t, 0, STEPS - 1)
            start = jnp.clip(block * BLOCK - 512, 0, LAST_START)
            offset = pl.multiple_of(jnp.clip(first - start, 0, SPAN - BLOCK), BLOCK)
            tiles.append(chances[block, pl.ds(offset, BLOCK), :])
        weights = jnp.concatenate(tiles, axis=1)
        grad_weights = dot(kv[keys, :], turned_d[:, span])
        grad_scores = bfloat(widen(weights) * (grad_weights - shift[:, span]))
        total = dot(weights, rows_d[span, :]) + dot(grad_scores, rows_q[span, :])
        total_q[:, span] += dot(qkv[1, :, keys], grad_scores)
        turned = total.T
        stage_kv[0:HEAD, keys] = bfloat(turned[:HEAD] * SCALE)
        stage_kv[HEAD:, keys] = bfloat(turned[HEAD:])

    def send_queries(number):
        span = pl.ds(pl.multiple_of(number * CHIP_ROWS + PAD, 128), CHIP_ROWS)
        stage_q[number] = bfloat(total_q[:, span] * SCALE)
        mail_q.to(number, stage_q.at[number], d_q_t.at[me])

    near = me + 1 - 2 * (me % 2)
    for slot in range(SLOTS):
        pair = lax.rem(me // 2 + 1 + slot, SLOTS)

        for t in range(3):
            step(pair * 3 + t)
        if slot < SLOTS - 1:
            for number in (2 * pair, 2 * pair + 1):
                mail_kv.to(number, stage_kv.at[:, chunk_span(number)], d_kv_t.at[me])
        else:
            mail_kv.to(near, stage_kv.at[:, chunk_span(near)], d_kv_t.at[me])
        if slot == 2:
            complete = lax.rem(me // 2 + 2, SLOTS)
            send_queries(2 * complete)
            send_queries(2 * complete + 1)
        between(slot)
    for rest in (1, 3):
        pair = lax.rem(me // 2 + rest, SLOTS)
        send_queries(2 * pair)
        send_queries(2 * pair + 1)
    send_queries(near)
    between(SLOTS)
    span = pl.ds(pl.multiple_of(me * CHIP_ROWS + PAD, 128), CHIP_ROWS)
    d_q_t[me] = bfloat(total_q[:, span] * SCALE)
    d_kv_t[me] = stage_kv[:, chunk_span(me)]
    mail_kv.finish(stage_kv.at[:, chunk_span(me)], d_kv_t.at[me])
    between(SLOTS + 1)
    mail_q.finish(stage_q.at[me], d_q_t.at[me])


BACK_SCRATCH = dict(
    held=CHANCES, kv=((LENGTH, 2 * HEAD), BF), rows_q=((PADDED, 2 * HEAD), BF),
    rows_d=((PADDED, 2 * HEAD), BF), turned_d=((2 * HEAD, PADDED), BF), shift=((1, PADDED), F32),
    total_q=((HEAD, PADDED), F32), stage_q=((CHIPS, HEAD, CHIP_ROWS), BF),
    stage_kv=((2 * HEAD, LENGTH), BF),
)
BACK_OUTPUTS = dict(
    d_q_t=((CHIPS, HEAD, CHIP_ROWS), BF), d_kv_t=((CHIPS, 2 * HEAD, CHIP_ROWS), BF)
)


REST = ((64, HALF), (80, HALF // 2), (80, HALF // 2))


def dot_nt(former, latter):
    return lax.dot_general(former, latter, (((1,), (1,)), ((), ())), preferred_element_type=F32)


QKV, OUT, IN, BACK = range(4)


class Weights:
    def __init__(self, refs, wire, names):
        self.refs, self.pending = refs, {}
        for name in names:
            if name == QKV:
                pairs = [(refs.gqkv, refs.w_qkv)]
            elif name == IN:
                pairs = [
                    (refs.rest_one.at[CUBE_ALL + (pl.ds(16 * k, 16),)], refs.w_in.at[k])
                    for k in range(4)
                ]
            elif name == OUT:
                pairs = [(refs.gout, refs.w_out)]
            else:
                pairs = [(refs.gback, refs.w_back)]
            self.pending[name] = [wire.fetch(*pair) for pair in pairs]

    def ready(self, name):
        for copy in self.pending.pop(name, []):
            copy.wait()

    def qkv(self, k):
        self.ready(QKV)
        return self.refs.w_qkv[k].reshape(D, HALF)

    def out(self, half):
        self.ready(OUT)
        return self.refs.w_out[half].reshape(HALF, HALF)

    def into(self, chunk):
        self.ready(IN)
        return self.refs.w_in[chunk].reshape(D, HALF)

    def back(self, half, chunk):
        self.ready(BACK)
        return self.refs.w_back[half, chunk // 2, chunk % 2].reshape(HALF, HALF)


def columns(k):
    return slice(k * HALF, k * HALF + HALF)


def vector(refs, k):
    return refs.vecs[k : k + 1, :]


def half_vector(refs, core, k):
    return refs.vecs[k : k + 1, pl.ds(pl.multiple_of(core * HALF, HALF), HALF)]


B_QUERY, B_VALUE, B_OUT, GAIN_ATTN, SHIFT_ATTN, B_BACK, GAIN_FFN, SHIFT_FFN = range(8)


def normalized(tensor):
    centred = tensor - jnp.mean(tensor, axis=-1, keepdims=True)
    factor = lax.rsqrt(jnp.mean(centred * centred, axis=-1, keepdims=True) + EPSILON)
    return centred * factor, factor


def normalize_back(grad_out, normed, factor, gain):
    grad_normed = grad_out * gain
    grad_input = factor * (
        grad_normed
        - jnp.mean(grad_normed, axis=-1, keepdims=True)
        - normed * jnp.mean(grad_normed * normed, axis=-1, keepdims=True)
    )
    return (
        grad_input,
        jnp.sum(grad_out * normed, axis=0, keepdims=True),
        jnp.sum(grad_out, axis=0, keepdims=True),
    )


def row_sum(tensor):
    return jnp.sum(widen(tensor), axis=0, keepdims=True)


def gelu_pair(v):
    root = math.sqrt(2.0 / math.pi)
    squared = v * v
    scaled = root * v
    half = 0.5 + 0.5 * jnp.tanh(scaled * (1.0 + 0.044715 * squared))
    slope = half + half * (1.0 - half) * scaled * (2.0 + (6 * 0.044715) * squared)
    return v * half, slope


def summed_over_cores(refs, wire, fill):
    send, come, kept = refs.outgoing.at[refs.round], refs.incoming.at[refs.round], refs.kept
    refs.round += 1
    fill(wire.other, send)
    copy = wire.swap(send, come)
    fill(wire.own, kept)
    copy.wait()
    return kept[...] + widen(come[...])


def project_rows(refs, wire, weight, copy, between):
    entry, rows_of, stage = refs.entry, refs.qkv_rows, refs.qkv_stage
    biases = (half_vector(refs, wire.core, B_QUERY), None, half_vector(refs, wire.core, B_VALUE))

    def project(rows, k):
        result = dot(entry[rows, :], weight(k))
        if biases[k] is not None:
            result = result + biases[k]
        rows_of[k, rows, :] = bfloat(result)

    for k in range(3):
        project(wire.own, k)
    copy.wait()
    refs.keep(entry)
    between()
    copies = []
    for k in range(3):
        project(wire.other, k)
        stage[k] = rows_of[k].T.reshape(CHIPS, HEAD, CHIP_ROWS)
        copies += wire.spread(stage.at[k], refs.qkv.at[k])
    return copies


def part_project(refs, wire, weights, hidden):
    entry = refs.entry
    entry[wire.own, :] = bfloat(hidden)
    copy = wire.swap(entry.at[wire.own], entry.at[wire.own])
    return project_rows(refs, wire, weights.qkv, copy, lambda: None)


def part_post(refs, wire, weights):
    mixed = refs.mixed
    mixed[...] = refs.mixed_t_in[...].reshape(HALF, CHIP_ROWS).T

    def leave(rows, target):
        for half in range(2):
            target[:, columns(half)] = dot(mixed[rows, :], weights.out(half)).astype(target.dtype)

    branch = summed_over_cores(refs, wire, leave)
    normed, factor = normalized(widen(refs.hidden[...]) + branch + vector(refs, B_OUT))
    refs.normed_one[...] = normed
    refs.factor_one[...] = factor
    refs.keep(refs.normed_one, refs.factor_one)
    first = normed * vector(refs, GAIN_ATTN) + vector(refs, SHIFT_ATTN)
    refs.first[...] = first
    entry_two, active, slope = refs.entry_two, refs.active, refs.slope
    entry_two[wire.own, :] = bfloat(first)
    copy = wire.swap(entry_two.at[wire.own], entry_two.at[wire.own])

    def inner(rows):
        for chunk in range(4):
            start = pl.multiple_of(wire.core * 2048 + chunk * HALF, HALF)
            before = dot(entry_two[rows, :], weights.into(chunk)) + refs.b_in[:, pl.ds(start, HALF)]
            value, steep = gelu_pair(before)
            active[rows, columns(chunk)] = bfloat(value)
            slope[rows, columns(chunk)] = bfloat(steep)

    inner(wire.own)
    copy.wait()
    refs.keep(entry_two)
    inner(wire.other)
    refs.keep(active, slope)

    def leave_two(rows, target):
        for half in range(2):
            total = dot(active[rows, columns(0)], weights.back(half, 0))
            for chunk in range(1, 4):
                total = total + dot(active[rows, columns(chunk)], weights.back(half, chunk))
            target[:, columns(half)] = total.astype(target.dtype)

    second = summed_over_cores(refs, wire, leave_two)
    normed, factor = normalized(refs.first[...] + second + vector(refs, B_BACK))
    refs.normed_two[...] = normed
    refs.factor_two[...] = factor
    refs.keep(refs.normed_two, refs.factor_two)
    return normed * vector(refs, GAIN_FFN) + vector(refs, SHIFT_FFN)


def part_back_dense(refs, wire, weights, grad_out):
    d_branch, d_before, d_attn = refs.d_branch, refs.d_before, refs.d_attn
    sums = refs.sums
    d_second, g_gain, g_shift = normalize_back(
        grad_out, refs.normed_two[...], refs.factor_two[...], vector(refs, GAIN_FFN)
    )
    refs.d_second[...] = d_second
    d_branch[wire.own, :] = bfloat(d_second)
    copy = wire.swap(d_branch.at[wire.own], d_branch.at[wire.own])
    sums[GAIN_FFN : GAIN_FFN + 1, :] = g_gain
    sums[SHIFT_FFN : SHIFT_FFN + 1, :] = g_shift
    sums[B_BACK : B_BACK + 1, :] = row_sum(d_branch[wire.own, :])

    def inner(rows):
        for chunk in range(4):
            d_active = dot_nt(d_branch[rows, columns(0)], weights.back(0, chunk)) + dot_nt(
                d_branch[rows, columns(1)], weights.back(1, chunk)
            )
            d_before[rows, columns(chunk)] = bfloat(
                d_active * widen(refs.slope[rows, columns(chunk)])
            )

    inner(wire.own)
    copy.wait()
    refs.keep(d_branch)
    inner(wire.other)
    refs.keep(d_before)
    for chunk in range(4):
        start = pl.multiple_of(wire.core * 2048 + chunk * HALF, HALF)
        refs.sums_in[:, pl.ds(start, HALF)] = row_sum(d_before[:, columns(chunk)])

    def leave(rows, target):
        total = dot_nt(d_before[rows, columns(0)], weights.into(0))
        for chunk in range(1, 4):
            total = total + dot_nt(d_before[rows, columns(chunk)], weights.into(chunk))
        target[...] = total.astype(target.dtype)

    d_first = refs.d_second[...] + summed_over_cores(refs, wire, leave)
    d_inner, g_gain, g_shift = normalize_back(
        d_first, refs.normed_one[...], refs.factor_one[...], vector(refs, GAIN_ATTN)
    )
    refs.d_inner_out[...] = d_inner
    refs.keep(refs.d_inner_out)
    d_attn[wire.own, :] = bfloat(d_inner)
    copy = wire.swap(d_attn.at[wire.own], d_attn.at[wire.own])
    sums[GAIN_ATTN : GAIN_ATTN + 1, :] = g_gain
    sums[SHIFT_ATTN : SHIFT_ATTN + 1, :] = g_shift
    sums[B_OUT : B_OUT + 1, :] = row_sum(d_attn[wire.own, :])
    rows_of, stage = refs.d_mixed_rows, refs.d_mixed_stage

    def enter(rows):
        rows_of[rows, :] = bfloat(
            dot_nt(d_attn[rows, columns(0)], weights.out(0))
            + dot_nt(d_attn[rows, columns(1)], weights.out(1))
        )

    enter(wire.own)
    copy.wait()
    refs.keep(d_attn, refs.sums, refs.sums_in)
    enter(wire.other)
    stage[...] = rows_of[...].T.reshape(CHIPS, HEAD, CHIP_ROWS)
    return wire.spread(stage, refs.d_mixed)


def turn_queries(refs):
    refs.d_qkv[0] = refs.d_q_t[...].reshape(HALF, CHIP_ROWS).T


def turn_keys_values(refs):
    rows_of = refs.d_qkv
    rows_of[1] = refs.d_kv_t[:, :HEAD, :].reshape(HALF, CHIP_ROWS).T
    rows_of[2] = refs.d_kv_t[:, HEAD:, :].reshape(HALF, CHIP_ROWS).T


def add_half(refs, wire, k, value):
    half = pl.ds(pl.multiple_of(wire.core * HALF, HALF), HALF)
    refs.sums[k : k + 1, half] = refs.sums[k : k + 1, half] + value


def part_back_project(refs, wire, weights):
    rows_of = refs.d_qkv

    def leave(rows, target):
        total = dot_nt(rows_of[0, rows, :], weights.qkv(0))
        for k in range(1, 3):
            total = total + dot_nt(rows_of[k, rows, :], weights.qkv(k))
        target[...] = total.astype(target.dtype)

    return refs.d_inner[...] + summed_over_cores(refs, wire, leave)


ROW_F32 = ((ROWS, D), F32)
COLUMN_F32 = ((ROWS, 1), F32)
CHIP_BF = ((CHIP_ROWS, D), BF)
WIDE_BF = ((CHIP_ROWS, 2048), BF)
HEADS_BF = ((CHIP_ROWS, HALF), BF)
STAGE = (CHIPS, HEAD, CHIP_ROWS)
POST, BACK_DENSE, BACK_PROJECT, ATTEND_BACK, GRADIENTS = range(5)
WHOLE_GRADIENTS = dict(
    g_in=(CUBE + (16, 2048), BF), g_back=((2, 2, 2, 4, 64, D), BF), g_out=((2, 2, 2, 4, 16, D), BF)
)
PARTS = (
    (
        (OUT, IN, BACK),
        dict(
            normed_one=ROW_F32, factor_one=COLUMN_F32, entry_two=CHIP_BF,
            active=WIDE_BF, slope=WIDE_BF, normed_two=ROW_F32, factor_two=COLUMN_F32,
        ),
        {},
        dict(first=ROW_F32, mixed=HEADS_BF),
        4,
        0,
    ),
    (
        (BACK, IN, OUT),
        dict(
            d_branch=CHIP_BF, d_before=WIDE_BF, d_attn=CHIP_BF, d_inner_out=ROW_F32,
            sums=((8, D), F32), sums_in=((1, FF), F32),
        ),
        dict(d_mixed=((HEAD, LENGTH), BF)),
        dict(d_second=ROW_F32, d_mixed_rows=HEADS_BF, d_mixed_stage=(STAGE, BF)),
        3 + 7,
        1,
    ),
    (
        (QKV,),
        dict(d_qkv=((3, CHIP_ROWS, HALF), BF)),
        {},
        {},
        1,
        0,
    ),
    ((), {}, BACK_OUTPUTS, BACK_SCRATCH, 0, 0),
    ((), WHOLE_GRADIENTS, {}, {}, 0, 0),
)
WEIGHT_SHAPES = (
    dict(w_qkv=((3,) + CUBE + (16, HALF), BF)),
    dict(w_out=((2, 2, 2, 2, 4, 16, HALF), BF)),
    dict(w_in=((4,) + CUBE + (16, HALF), BF)),
    dict(w_back=((2, 2, 2, 2, 4, 64, HALF), BF)),
)


WEIGHT_COPIES = (1, 1, 4, 1)


def weight_gradients(refs, mixed_t, add, ready):
    def store(ref, at, value):
        value = value.reshape(ref[at].shape)
        ref[at] = bfloat(value + widen(ref[at])) if add else bfloat(value)

    for chunk in range(4):
        value = dot(refs.active[:, columns(chunk)].T, refs.d_branch[...])
        store(refs.g_back, (chunk // 2, chunk % 2), value)
    refs.keep(refs.g_back)
    store(refs.g_out, CUBE_ALL, dot(mixed_t.reshape(HALF, CHIP_ROWS), refs.d_attn[...]))
    refs.keep(refs.g_out)
    ready()
    turned = refs.entry_two[...].T
    for chunk in range(4):
        value = dot(turned, refs.d_before[:, columns(chunk)])
        store(refs.g_in, CUBE_ALL + (EVERY, columns(chunk)), value)
    refs.keep(refs.g_in)


def dense(
    parts, number, gathered, loaded, late, extra, dropped=(), sources={}, added={}
):
    outputs, saved, weight_names, sems = {}, dict(extra), [], []
    rounds = 2 * (POST in parts) + (BACK_DENSE in parts) + (BACK_PROJECT in parts)
    sums = ((rounds, ROWS, D), BF)
    scratch = dict(outgoing=sums, incoming=sums, kept=ROW_F32)
    copies = locals_ = 0
    for part in parts:
        its_weights, its_saved, its_outputs, its_scratch, its_copies, its_locals = PARTS[part]
        weight_names += [name for name in its_weights if name not in weight_names]
        outputs.update(its_outputs)
        saved.update(its_saved)
        scratch.update(its_scratch)
        copies += its_copies
        locals_ += its_locals
    for name, value in late.items():
        scratch[name] = (value.shape, value.dtype)
    for name in dropped:
        scratch[name] = {**saved, **outputs}[name]
        saved.pop(name, None)
        outputs.pop(name, None)
    for name in weight_names:
        scratch.update(WEIGHT_SHAPES[name])
        locals_ += WEIGHT_COPIES[name]
    far = {}
    if added:
        far = dict(come_back=((2, 2, 2, 4, 64, HALF), BF), come_out=((2, 2, 2, 4, 16, HALF), BF))
    if ATTEND_BACK in parts:
        sems = MAIL_SEMS + MAIL_SEMS + [dma(SLOTS)]

    def body(refs, semaphores):
        here = place()
        wire = Wire(here, *semaphores[:3])
        refs.round = 0
        weights = Weights(refs, wire, weight_names)
        after_first = []
        if BACK_DENSE in parts:
            refs.sums[...] = jnp.zeros((8, D), F32)
            refs.sums_in[...] = jnp.zeros((1, FF), F32)
        if ATTEND_BACK in parts:
            refs.attend_local = semaphores[-1]
        greet([partner(here)] + group(here))
        refs.arrive()
        pending = []
        value = None
        for step, part in enumerate(parts):
            if step == 1:
                for key in (*late, *added):
                    after_first.append(wire.fetch(getattr(refs, key + LATER), getattr(refs, key)))
                if ATTEND_BACK in parts:
                    fetch_chances(refs)
            if part == POST:
                value = part_post(refs, wire, weights)
                refs.result[...] = value.astype(refs.result.dtype)
                refs.keep(refs.result)
            elif part == BACK_DENSE:
                if POST in parts:
                    value = widen(refs.cotangent[...])
                pending += part_back_dense(refs, wire, weights, value)
            elif part == BACK_PROJECT:
                turn_queries(refs)
                turn_keys_values(refs)
                refs.keep(refs.d_qkv)
                add_half(refs, wire, B_QUERY, row_sum(refs.d_qkv[0]))
                add_half(refs, wire, B_VALUE, row_sum(refs.d_qkv[2]))
                value = part_back_project(refs, wire, weights)
            elif part == GRADIENTS:
                for copy in after_first:
                    copy.wait()

                def ready():
                    if added:
                        low = pl.multiple_of((1 - wire.core) * HALF, HALF)
                        span = CUBE_ALL + (EVERY, pl.ds(low, HALF))
                        pending.append(wire.swap(refs.g_back.at[span], refs.come_back))
                        pending.append(wire.swap(refs.g_out.at[span], refs.come_out))

                weight_gradients(refs, refs.mixed_t_in[...], bool(added), ready)
            else:
                prepare_back(refs)
                for copy in pending:
                    copy.wait()
                pending = []
                send, recv, send_two, recv_two, _ = semaphores[3:]
                attend_back_steps(
                    refs, Mail(here, send, recv), Mail(here, send_two, recv_two), lambda slot: None
                )
        for copy in pending:
            copy.wait()

    return call(
        body, "dense_%d" % number, number, {},
        dict(loaded, vecs=gathered.vecs, b_in=gathered.b_in),
        dict(
            sources, gqkv=gathered.gqkv, gout=gathered.gout, gback=gathered.gback,
            rest_one=gathered.rest_one,
            **{key + LATER: value for key, value in (*late.items(), *added.items())},
        ),
        outputs, saved, far, scratch, [dma(copies + 2), dma(copies + 2), dma(locals_ + 6)] + sems,
    )


LATER = "_later"


class Arriving(Weights):
    def __init__(self, refs, pending):
        self.refs, self.pending = refs, pending

    def ready(self, name):
        self.pending.pop(name, lambda: None)()


LAYER_SAVED = dict(
    mixed_head=((HEAD, LENGTH), F32), inverse=((1, LENGTH), F32), entry=CHIP_BF,
    qkv=((3, HEAD, LENGTH), BF),
)
SECOND = "_second"


def opening(lengths, pads, shards, vectors, tokens, number):
    def body(refs, semaphores):
        send, recv, local = semaphores[:3]
        here = place()
        wire = Wire(here, send, recv, local)
        core = wire.core
        refs.round = 0
        greet(neighbours(here, (1, -1, 2)) + group(here))
        refs.arrive()
        tok = lax.axis_index("tok")
        lanes = lax.broadcasted_iota(jnp.int32, (1, 128), 1)
        line = widen(refs.vectors[...])
        rows = []
        for k in range(8):
            turned = pltpu.roll(line, lax.rem(tok * 8 - 8 * k + 128, 128), 1)
            rows.append(jnp.where(lanes // 8 == tok, turned, 0.0))
        turned = pltpu.roll(line, lax.rem(lax.rem(tok, 4) * 32 + 64, 128), 1)
        turned = jnp.where(lanes // 32 == lax.rem(tok, 4), turned, 0.0)
        for k in range(4):
            rows.append(jnp.where(lax.div(tok, 4) == k, turned, jnp.zeros_like(turned)))
        rows.append(jnp.zeros((4, 128), F32))
        refs.small[...] = bfloat(jnp.concatenate(rows, axis=0))
        thin = [widen(ref[...]) for ref in (refs.s_query, refs.s_key, refs.s_value, refs.s_out)]
        wide, back = widen(refs.s_in[...]), refs.s_back[...]
        for half in range(2):
            span = columns(half)
            spread = [wide[:, columns(4 * half + k)] for k in range(4)]
            pieces = [thin[k][:, span] for k in range(3)] + spread[:3]
            refs.pack[half, 0:48, :] = bfloat(jnp.concatenate(pieces, axis=0))
            refs.pack[half, 48:80, :] = back[:, span]
            refs.pack[half, 80:96, :] = bfloat(
                jnp.concatenate([spread[3], thin[3][:, span]], axis=0)
            )
        swaps = [
            wire.swap(refs.pack.at[1 - core], refs.theirs),
            wire.swap(refs.small, refs.small_theirs),
        ]
        entry = refs.entry
        entry[wire.own, :] = refs.tokens[...]
        entry_copy = wire.swap(refs.tokens, entry.at[wire.own])
        for copy in swaps:
            copy.wait()

        def build(low, high):
            low, high = widen(low), widen(high)

            def both(row):
                return bfloat(jnp.concatenate([low[row : row + 8], high[row : row + 8]], axis=0))

            for k in range(3):
                refs.own_qkv[k] = both(8 * k)
                refs.own_one[16 * k : 16 * k + 16, :] = both(24 + 8 * k)
            refs.own_one[48:64, :] = both(80)
            back = bfloat(jnp.concatenate([low[48:80], high[48:80]], axis=0))
            refs.own_out[...] = both(88)
            refs.own_two[...] = back[:, 0:256]
            refs.own_three[...] = back[:, 256:512]

        @pl.when(core == 0)
        def _():
            build(refs.pack[0], refs.theirs[...])

        @pl.when(core == 1)
        def _():
            build(refs.theirs[...], refs.pack[1])

        refs.own_small[...] = refs.small[...] + refs.small_theirs[...]

        def nothing(value):
            pass

        parts = [
            (refs.w_qkv, (k,), GATHER_ORDERS[k], refs.own_qkv.at[k], HALF, nothing)
            for k in range(3)
        ]
        for k, ref in enumerate((refs.all_out, refs.all_out_two)):
            own = refs.own_out.at[:, side_columns(HALF, k)]
            parts.append((ref, (), GATHER_ORDERS[1 + k], own, HALF // 2, nothing))
        parts.append((refs.all_small, (), GATHER_ORDERS[3], refs.own_small, 0, nothing))
        first_stages = ring_gather(wire, parts)
        mine, yours = pl.ds(2 * core, 2), pl.ds(2 * (1 - core), 2)
        taken, passed = [], []

        def take_one(value):
            for k in range(4):
                taken.append(
                    wire.fetch(
                        refs.rest_one.at[value, :, :, :, pl.ds(16 * k, 16)], refs.w_in.at[k, value]
                    )
                )

        def pass_part(ref, side, place_of):
            def take(value):
                target = refs.w_back.at[
                    (core, EVERY) + place_of(value) + (EVERY, side_columns(HALF, side))
                ]
                passed.append(wire.swap(ref.at[(yours,) + place_of(value)], target))
                passed.append(wire.fetch(ref.at[(mine,) + place_of(value)], target))

            return take

        pass_two = pass_part(refs.rest_two, 0, lambda z: (EVERY, EVERY, z))
        pass_three = pass_part(refs.rest_three, 1, lambda x: (x % 2, x // 2, EVERY))

        long_stages = ring_gather(
            wire, [(refs.rest_one, (), GATHER_ORDERS[0], refs.own_one, HALF, take_one)]
        )
        stages = ring_gather(
            wire,
            [
                (refs.rest_two, (), GATHER_ORDERS[1], refs.own_two, HALF // 2, pass_two),
                (refs.rest_three, (), GATHER_ORDERS[2], refs.own_three, HALF // 2, pass_three),
            ],
        )
        for ring in (first_stages, long_stages, stages, first_stages, first_stages, long_stages):
            advance(ring)
        advance(stages)
        for _ in first_stages:
            pass
        kept = wire.fetch(refs.w_qkv, refs.gqkv)
        out_copies = []
        for k, ref in enumerate((refs.all_out, refs.all_out_two)):
            into = refs.w_out.at[(core,) + (EVERY,) * 5 + (side_columns(HALF, k),)]
            out_copies += [wire.swap(ref.at[yours], into), wire.fetch(ref.at[mine], into)]
        for s in range(8):
            tile = jnp.zeros((16, 128), F32)
            for x_hi in range(2):
                for z in range(4):
                    tile = tile + widen(refs.all_small[s // 2, s % 2, x_hi, z])
            refs.vecs[:, 128 * s : 128 * s + 128] = tile[:8]
            for j in range(4):
                low = HALF * s + 128 * j
                refs.b_in[:, low : low + 128] = tile[8 + j : 9 + j]
        refs.keep(refs.vecs, refs.b_in)
        refs.attend_local = semaphores[5]
        pending = project_rows(
            refs, wire, lambda k: refs.w_qkv[k].reshape(D, HALF), entry_copy, lambda: advance(long_stages)
        )
        for copy in pending[: 2 * CHIPS]:
            copy.wait()

        def values_ready():
            for copy in pending[2 * CHIPS :]:
                copy.wait()
            refs.keep(refs.qkv)
            advance(stages)

        def between(slot):
            if slot == 0:
                advance(long_stages)
            elif slot == 2:
                advance(stages)
            elif slot == 3:
                advance(long_stages)

        attend_steps(refs, Mail(here, *semaphores[3:5]), values_ready, between)

        def out_ready():
            for copy in out_copies:
                copy.wait()
            refs.keep(refs.w_out)

        def in_ready():
            advance(stages)
            for _ in long_stages:
                pass
            for copy in taken:
                copy.wait()

        def back_ready():
            for _ in stages:
                pass
            for copy in passed:
                copy.wait()
            refs.keep(refs.w_back)

        mixed_copy = wire.fetch(refs.mixed_t, refs.mixed_t_one)
        weights = Arriving(refs, {OUT: out_ready, IN: in_ready, BACK: back_ready})
        refs.mixed_t_in = refs.mixed_t
        refs.hidden = refs.tokens
        value = part_post(refs, wire, weights)
        refs.result[...] = value
        refs.keep(refs.result)
        second = types.SimpleNamespace(**vars(refs))
        second.attend_local = semaphores[-1]
        for name in [*LAYER_SAVED, *MIXED_T, CHANCES_NAME]:
            setattr(second, name, getattr(refs, name + SECOND))
        pending = part_project(second, wire, weights, value)
        for copy in pending[: 2 * CHIPS]:
            copy.wait()

        def second_ready():
            for copy in pending[2 * CHIPS :]:
                copy.wait()
            refs.keep(second.qkv)

        attend_steps(second, Mail(here, *semaphores[6:8]), second_ready, lambda slot: None)
        kept.wait()
        mixed_copy.wait()

    cube_16 = (CUBE + (16, HALF // 2), BF)
    scratch = dict(
        ATTEND_SCRATCH, pack=((2, 96, HALF), BF), small=((16, 128), BF), theirs=((96, HALF), BF),
        small_theirs=((16, 128), BF), own_qkv=((3, 16, HALF), BF), own_out=((16, HALF), BF),
        own_one=((64, HALF), BF), own_two=((64, HALF // 2), BF), own_three=((64, HALF // 2), BF),
        own_small=((16, 128), BF), w_qkv=((3,) + CUBE + (16, HALF), BF), all_out=cube_16, all_out_two=cube_16,
        all_small=(CUBE + (16, 128), BF), qkv_rows=((3, CHIP_ROWS, HALF), BF),
        qkv_stage=((3,) + STAGE, BF), outgoing=((2, ROWS, D), BF), incoming=((2, ROWS, D), BF),
        kept=ROW_F32, first=ROW_F32, mixed=HEADS_BF, mixed_t=MIXED_T[MIXED_NAME],
    )
    scratch.update(WEIGHT_SHAPES[IN])
    saved = dict(LAYER_SAVED, vecs=((8, D), F32), b_in=((1, FF), F32), result=ROW_F32)
    saved.update(WEIGHT_SHAPES[OUT])
    saved.update(WEIGHT_SHAPES[BACK])
    saved.update(PARTS[POST][1])
    saved.update({name + SECOND: spec for name, spec in LAYER_SAVED.items()})
    narrow = (CUBE + (64, HALF // 2), BF)
    copies = 3 + 9 * GATHER_COPIES + 10 + 2 * 21 + 4
    result = call(
        body, "opening", number, {}, dict(shards, vectors=vectors, tokens=tokens), {},
        {MIXED_NAME + SECOND: MIXED_T[MIXED_NAME]}, saved,
        dict(
            chances=CHANCES, chances_second=CHANCES, gqkv=((3,) + CUBE + (16, HALF), BF),
            rest_one=(CUBE + (64, HALF), BF), rest_two=narrow, rest_three=narrow,
            mixed_t_one=MIXED_T[MIXED_NAME],
        ),
        scratch,
        [dma(copies), dma(copies), dma(46)] + (MAIL_SEMS + [dma(SLOTS + 1)]) * 2,
        dict(lengths=lengths, pads=pads),
    )
    result.gout, result.gback = result.w_out, result.w_back
    return result


MIXED_NAME, CHANCES_NAME = "mixed_t", "chances"


def closing(near, loaded, sources, number):
    rest_slots = [scatter_slots(order, *REST[k], True) for k, order in enumerate(SCATTER_ORDERS[:3])]

    def body(refs, semaphores):
        send, recv, local, send_q, recv_q, send_kv, recv_kv, refs.attend_local = semaphores
        here = place()
        wire = Wire(here, send, recv, local)
        core = wire.core
        refs.round = 0
        mine, yours = pl.ds(2 * core, 2), pl.ds(2 * (1 - core), 2)
        blocks, inner, copies = (EVERY,) * 3, [], []
        for side, ref in enumerate((refs.rest_two, refs.rest_three)):
            low = pl.multiple_of(core * HALF + side * (HALF // 2), HALF // 2)
            here_columns = CUBE_ALL + (EVERY, pl.ds(low, HALF // 2))
            come_columns = CUBE_ALL + (EVERY, side_columns(HALF, side))
            for rows, gradient, come in (
                (pl.ds(0, 64), refs.g_back, refs.come_back),
                (pl.ds(64, 16), refs.g_out, refs.come_out),
            ):
                copies.append(
                    wire.fetch(gradient.at[here_columns], ref.at[(mine,) + blocks + (rows,)])
                )
                copies.append(
                    wire.fetch(come.at[come_columns], ref.at[(yours,) + blocks + (rows,)])
                )
        for k in range(4):
            source = refs.g_in.at[CUBE_ALL + (EVERY, pl.ds(k * HALF, HALF))]
            inner.append(wire.fetch(source, refs.rest_one.at[CUBE_ALL + (pl.ds(16 * k, 16),)]))
        greet(neighbours(here, (1, -1, 2)) + group(here))
        refs.arrive()

        def keep_rest(part):
            def store(value):
                (refs.sums_one, refs.sums_two, refs.sums_six)[part][...] = value

            return store

        rest_arrivals = [
            [getattr(refs, "rest_%d_%d" % (part, k)) for k in range(4)] for part in range(3)
        ]
        rest = [
            (ref, (), SCATTER_ORDERS[part], REST[part][1], rest_arrivals[part], keep_rest(part))
            for part, ref in enumerate((refs.rest_one, refs.rest_two, refs.rest_three))
        ]
        long_stages = ring_scatter(wire, rest[:1], (0, 1, 2))
        rest_stages = ring_scatter(wire, rest[1:], (0, 1, 2))
        for copy in inner:
            copy.wait()
        advance(long_stages)
        fetch_chances(refs)
        weights = Weights(refs, wire, (QKV,))

        def keep(part):
            def store(value):
                if part == 3:
                    refs.tiny[...] = value
                else:
                    refs.final[part] = value

            return store

        arrivals = [
            [getattr(refs, "slot_%d_%d" % (part, k)) for k in range(4)] for part in range(4)
        ]
        parts = [
            (refs.gradients, (part,), SCATTER_ORDERS[part], HALF, arrivals[part], keep(part))
            for part in range(3)
        ]
        parts.append((refs.small_sums, (), SCATTER_ORDERS[3], 0, arrivals[3], keep(3)))
        early_stages = ring_scatter(wire, parts[1:3], (0, 1, 2))
        stages = ring_scatter(wire, parts[:1] + parts[3:], (0, 1, 2))

        def add_gradient(k):
            total = dot(refs.entry_t[...], refs.d_qkv[k]).reshape(CUBE + (16, HALF))
            refs.gradients[k] = bfloat(widen(refs.gradients[k]) + total)

        def between(slot):
            if slot == -1:
                for copy in copies:
                    copy.wait()
                advance(rest_stages)
                turned = refs.entry_later[...].T
                for k in range(3):
                    total = dot(turned, refs.d_qkv_later[k])
                    refs.gradients[k] = bfloat(total).reshape(CUBE + (16, HALF))
                refs.entry_t[...] = refs.entry[...].T
                refs.sums[...] = refs.sums_three[...] + refs.sums_four[...]
                refs.sums_in[...] = refs.in_three[...] + refs.in_four[...]
            elif slot == 0:
                advance(rest_stages)
            elif slot == 1:
                advance(long_stages)
            elif slot == SLOTS:
                advance(long_stages)
            elif slot == SLOTS + 1:
                turn_keys_values(refs)
                add_gradient(1)
                add_gradient(2)
                advance(early_stages)
                advance(rest_stages)

        prepare_back(refs)
        attend_back_steps(
            refs, Mail(here, send_q, recv_q), Mail(here, send_kv, recv_kv), between
        )
        turn_queries(refs)
        add_half(refs, wire, B_QUERY, row_sum(refs.d_qkv[0]))
        add_half(refs, wire, B_VALUE, row_sum(refs.d_qkv[2]))
        swaps = [wire.swap(refs.sums, refs.sums_come), wire.swap(refs.sums_in, refs.in_come)]
        add_gradient(0)
        for copy in swaps:
            copy.wait()
        both = refs.sums[...] + refs.sums_come[...]
        both_in = refs.sums_in[...] + refs.in_come[...]
        for s in range(8):
            pieces = [both[:, 128 * s : 128 * s + 128]]
            for j in range(4):
                low = HALF * s + 128 * j
                pieces.append(both_in[:, low : low + 128])
            pieces.append(jnp.zeros((4, 128), F32))
            tile = bfloat(jnp.concatenate(pieces, axis=0))
            for x_hi in range(2):
                for z in range(4):
                    refs.small_sums[s // 2, s % 2, x_hi, z] = tile
        advance(stages)
        advance(early_stages)
        advance(stages)
        refs.d_tokens[...] = bfloat(part_back_project(refs, wire, weights))
        for ring in (early_stages, stages, rest_stages, long_stages, early_stages, stages):
            advance(ring)
        for ring in (rest_stages, long_stages, early_stages, stages):
            for _ in ring:
                pass

        def finish(own):
            def both(low, count):
                span = slice(low, low + count)
                return jnp.concatenate([refs.sums_two[span, :], refs.sums_six[span, :]], axis=1)

            rows = [refs.final[k, 8 * own : 8 * own + 8, :] for k in range(3)]
            rows.append(both(64 + 8 * own, 8))
            for k in range(4):
                rows.append(refs.sums_one[16 * k + 8 * own : 16 * k + 8 * own + 8, :])
            rows.append(both(32 * own, 32))
            return jnp.concatenate(rows, axis=0)

        @pl.when(core == 0)
        def _():
            refs.leaving[...] = finish(1)
            refs.landed[0] = finish(0)

        @pl.when(core == 1)
        def _():
            refs.leaving[...] = finish(0)
            refs.landed[1] = finish(1)

        wire.swap(refs.leaving, refs.landed.at[core]).wait()
    few = ((8, D), F32)
    scratch = dict(
        BACK_SCRATCH, **BACK_OUTPUTS, outgoing=((1, ROWS, D), BF), incoming=((1, ROWS, D), BF),
        kept=ROW_F32, entry_t=((D, CHIP_ROWS), BF), d_qkv=((3, CHIP_ROWS, HALF), BF), sums=few, sums_in=((1, FF), F32), sums_come=few,
        in_come=((1, FF), F32), gradients=((3,) + CUBE + (16, HALF), BF),
        small_sums=(CUBE + (16, 128), BF), final=((3, 16, HALF), F32),
        leaving=((96, HALF), F32), sums_one=(REST[0], F32), sums_two=(REST[1], F32),
        sums_six=(REST[2], F32), rest_one=(CUBE + REST[0], BF), rest_two=(CUBE + REST[1], BF),
        rest_three=(CUBE + REST[2], BF),
    )
    scratch.update(WEIGHT_SHAPES[QKV])
    for part in range(4):
        slots = scatter_slots(SCATTER_ORDERS[part], 16, HALF if part < 3 else 128, part < 3)
        for k in range(4):
            scratch["slot_%d_%d" % (part, k)] = slots[k]
    for part in range(3):
        for k in range(4):
            scratch["rest_%d_%d" % (part, k)] = rest_slots[part][k]
    copies = 7 * sum(SCATTER_COPIES) + 8
    return call(
        body, "closing", number, near, loaded, sources,
        dict(
            d_tokens=((ROWS, D), BF), landed=((2, 96, HALF), F32), tiny=((16, 128), F32),
        ),
        {}, {}, scratch,
        [dma(copies), dma(copies), dma(13)] + MAIL_SEMS + MAIL_SEMS + [dma(SLOTS)],
    )


def unpack_kernel(
    result, d_tokens, landed, tiny, o_result, o_tokens, o_query, o_key, o_value, o_out, o_in, o_back,
    *o_vectors,
):
    o_result[...] = result[...]
    o_tokens[...] = d_tokens[...]
    for column in (0, 1):
        span = columns(column)
        for piece, ref in enumerate((o_query, o_key, o_value, o_out)):
            ref[:, span] = landed[column, 8 * piece : 8 * piece + 8, :]
        for chunk in range(4):
            o_in[:, columns(4 * column + chunk)] = landed[
                column, 32 + 8 * chunk : 40 + 8 * chunk, :
            ]
        o_back[:, span] = landed[column, 64:96, :]
    tok = lax.axis_index("tok")
    eight = pltpu.roll(tiny[0:8, :], lax.rem(128 - tok * 8, 128), 1)
    for k in range(8):
        o_vectors[k][...] = eight[k : k + 1, 0:8]
    wide = tiny[8:9, :]
    for k in range(1, 4):
        wide = jnp.where(lax.div(tok, 4) == k, tiny[8 + k : 9 + k, :], wide)
    wide = pltpu.roll(wide, lax.rem(128 - lax.rem(tok, 4) * 32, 128), 1)
    o_vectors[8][...] = wide[:, 0:32]


def unpack(result, d_tokens, landed, tiny):
    vmem = pl.BlockSpec(memory_space=pltpu.VMEM)
    few = ((8, D), F32)
    specs = (
        ((ROWS, D), BF), ((ROWS, D), BF), few, few, few, few, ((8, FF), F32), ((32, D), F32),
    ) + (((1, 8), F32),) * 8 + (((1, 32), F32),)
    return pl.pallas_call(
        unpack_kernel,
        out_shape=tuple(jax.ShapeDtypeStruct(*spec) for spec in specs),
        in_specs=[vmem] * 4,
        out_specs=(vmem,) * len(specs),
        name="unpack",
        compiler_params=pltpu.CompilerParams(vmem_limit_bytes=58 * 2**20),
    )(result, d_tokens, landed, tiny)


def on_device(
    tokens, cotangent, doc_lengths, pad_counts, w_query, b_query, w_key, w_value, b_value, w_out,
    b_out, gain_attn, shift_attn, w_in, b_in, w_back, b_back, gain_ffn, shift_ffn,
):
    vectors = jnp.concatenate(
        [
            b_query, b_value, b_out, gain_attn, shift_attn, b_back, gain_ffn, shift_ffn, b_in,
            jnp.zeros((32,), BF),
        ]
    )
    one = opening(
        doc_lengths, pad_counts,
        dict(
            s_query=w_query, s_key=w_key, s_value=w_value, s_out=w_out, s_in=w_in, s_back=w_back
        ),
        widen(vectors)[None], tokens, 0,
    )
    three = dense(
        (POST, BACK_DENSE, GRADIENTS, ATTEND_BACK), 4, one,
        dict(mixed_t_in=one.mixed_t_second, hidden=one.result, cotangent=cotangent),
        dict(
            qkv=one.qkv_second, mixed_head=one.mixed_head_second, inverse=one.inverse_second,
        ),
        dict(result=((ROWS, D), BF)),
        (
            "normed_one", "factor_one", "entry_two", "active", "slope", "normed_two",
            "factor_two", "d_branch", "d_before", "d_attn", "d_mixed",
        ),
        dict(chances=one.chances_second),
    )
    four = dense(
        (BACK_PROJECT, BACK_DENSE, GRADIENTS), 6, one,
        dict(
            d_q_t=three.d_q_t, d_kv_t=three.d_kv_t, d_inner=three.d_inner_out,
            normed_one=one.normed_one, factor_one=one.factor_one, normed_two=one.normed_two,
            factor_two=one.factor_two, slope=one.slope,
        ),
        dict(entry_two=one.entry_two, active=one.active, mixed_t_in=one.mixed_t_one),
        {}, ("d_branch", "d_before", "d_attn"),
        added=dict(g_in=three.g_in, g_back=three.g_back, g_out=three.g_out),
    )
    last = closing(
        {},
        dict(
            d_mixed=four.d_mixed,
            qkv=one.qkv, mixed_head=one.mixed_head, inverse=one.inverse, d_inner=four.d_inner_out,
            entry=one.entry, entry_later=one.entry_second, d_qkv_later=four.d_qkv, sums_three=three.sums,
            sums_four=four.sums, in_three=three.sums_in, in_four=four.sums_in,
        ),
        dict(
            chances=one.chances, gqkv=one.gqkv, g_in=four.g_in, g_back=four.g_back, g_out=four.g_out,
            come_back=four.come_back, come_out=four.come_out,
        ),
        8,
    )
    result, d_tokens, g_query, g_key, g_value, g_out, g_in, g_back, *lines = unpack(
        three.result, last.d_tokens, last.landed, last.tiny
    )
    (
        g_b_query, g_b_value, g_b_out, g_gain_attn, g_shift_attn, g_b_back, g_gain_ffn, g_shift_ffn,
    ) = [lines[k].reshape(8) for k in range(8)]
    return (
        result, d_tokens, g_query, g_b_query, g_key, g_value, g_b_value, g_out, g_b_out, g_gain_attn,
        g_shift_attn, g_in, lines[8].reshape(32), g_back, g_b_back, g_gain_ffn, g_shift_ffn,
    )


def solution(mesh):
    both = ("seq", "tok")
    rows, vector = P(both, None), P(both)
    ins = (
        rows, rows, P("seq", None), P("seq"), rows, vector, rows, rows, vector, rows, vector, vector,
        vector, rows, vector, rows, vector, vector, vector,
    )
    outs = (
        rows, rows, rows, vector, rows, rows, vector, rows, vector, vector, vector, rows, vector,
        rows, vector, vector, vector,
    )
    return jax.shard_map(on_device, mesh=mesh, in_specs=ins, out_specs=outs, check_vma=False)
```

```python
import math
import types

import jax
import jax.numpy as jnp
from jax import lax
from jax.experimental import pallas as pl
from jax.experimental.pallas import tpu as pltpu
from jax.sharding import PartitionSpec as P

HEADS = 16
WINDOW = 1024
D = 1024
FF = 4096
HEAD = 64
CHIPS = 8
ROWS = 192
CHIP_ROWS = 2 * ROWS
LENGTH = CHIP_ROWS * CHIPS
HALF = 512
EPSILON = 1e-05
MASKED = -1e30
SCALE = 1.0 / math.sqrt(HEAD)
LOG2E = 1.4426950408889634
MESH = pl.DeviceIdType.MESH
BF = jnp.bfloat16
F32 = jnp.float32
CUBE = (4, 2, 2, 4)
X, Y, Z, CORE = range(4)


def bfloat(tensor):
    return tensor.astype(BF)


def widen(tensor):
    return tensor.astype(F32)


def place():
    seq, tok = lax.axis_index("seq"), lax.axis_index("tok")
    x = (tok // 8) * 2 + seq % 2
    return {X: x, Y: seq // 2, Z: (tok // 2) % 4, CORE: tok % 2}


def device(x, y, z, core):
    return (y * 2 + x % 2, (x // 2) * 8 + z * 2 + core)


def moved(here, axis, steps):
    there = dict(here)
    there[axis] = lax.rem(here[axis] + steps + 4, 4)
    return device(there[X], there[Y], there[Z], there[CORE])


def partner(here):
    return device(here[X], here[Y], here[Z], 1 - here[CORE])


def cube_index(here, whole, axis, value):
    index = []
    for name in (Y, X, Z):
        if name in whole:
            index += [slice(None)] * (2 if name == X else 1)
        else:
            at = value if name == axis else here[name]
            index += [at % 2, at // 2] if name == X else [at]
    return tuple(index)


def greet(targets):
    barrier = pltpu.get_barrier_semaphore()
    for target in targets:
        pl.semaphore_signal(barrier, inc=1, device_id=target, device_id_type=MESH)
    pl.semaphore_wait(barrier, len(targets))


def neighbours(here, steps):
    return [moved(here, axis, step) for axis in (X, Y, Z) for step in steps] + [partner(here)]


def group_device(here, number):
    seq = lax.axis_index("seq")
    return (seq, (number // 4) * 8 + (number % 4) * 2 + here[CORE])


def group_number(here):
    return (here[X] // 2) * 4 + here[Z]


def group(here):
    me = group_number(here)
    return [group_device(here, lax.rem(me + k, CHIPS)) for k in range(1, CHIPS)]


class Wire:
    def __init__(self, here, send, recv, local):
        self.send, self.recv, self.local = send, recv, local
        self.here, self.number, self.locals = here, 0, 0
        self.core, self.me = here[CORE], group_number(here)
        self.own = pl.ds(pl.multiple_of(self.core * ROWS, ROWS), ROWS)
        self.other = pl.ds(pl.multiple_of((1 - self.core) * ROWS, ROWS), ROWS)

    def to(self, source, target, device_id):
        copy = pltpu.make_async_remote_copy(
            src_ref=source,
            dst_ref=target,
            send_sem=self.send.at[self.number],
            recv_sem=self.recv.at[self.number],
            device_id=device_id,
            device_id_type=MESH,
        )
        self.number += 1
        copy.start()
        return copy

    def swap(self, source, target):
        return self.to(source, target, partner(self.here))

    def fetch(self, source, target):
        copy = pltpu.make_async_copy(source, target, self.local.at[self.locals])
        self.locals += 1
        copy.start()
        return copy

    def spread(self, stage, target):
        span = chunk_span(self.me)
        copies = []
        for k in range(1, CHIPS):
            to = lax.rem(self.me + k, CHIPS)
            copies.append(self.to(stage.at[to], target.at[:, span], group_device(self.here, to)))
        copies.append(self.fetch(stage.at[self.me], target.at[:, span]))
        return copies


def chunk_span(number):
    return pl.ds(pl.multiple_of(number * CHIP_ROWS, CHIP_ROWS), CHIP_ROWS)


EVERY = slice(None)
CUBE_ALL = (EVERY,) * 4


def side_columns(width, side):
    return pl.ds(side * (width // 2), width // 2)


SIZES = {Y: (4,), X: (2, 2), Z: (4,)}
GATHER_ORDERS = ((X, Z, Y), (Y, X, Z), (Z, Y, X), (X, Z, Y))
LAST_ORDERS = ((Z, X, Y), (Y, Z, X), (X, Y, Z))
SCATTER_ORDERS = ((Y, Z, X), (Z, X, Y), (X, Y, Z), (Y, Z, X))


def ring_gather(wire, parts):
    here = wire.here
    sent, kept = [], []
    for buffer, prefix, order, own, _, _ in parts:
        kept.append(wire.fetch(own, buffer.at[prefix + cube_index(here, (), None, None)]))
    for phase in range(2):
        copies = []
        for step in (1, -1, 2):
            for buffer, prefix, order, own, _, _ in parts:
                axis = order[phase]
                block = buffer.at[prefix + cube_index(here, order[:phase], axis, here[axis])]
                source = own if phase == 0 else block
                copies.append(wire.to(source, block, moved(here, axis, step)))
        yield
        for copy in copies:
            copy.wait_recv()
        sent += copies
        if phase == 0:
            for copy in kept:
                copy.wait()
    first, second, onward = [], [], []

    def block_at(part, value, side):
        buffer, prefix, order, _, cut, _ = part
        index = prefix + cube_index(here, order[:2], order[2], value)
        return buffer.at[index + ((EVERY, side_columns(cut, side)) if cut else ())]

    for turn, copies in enumerate((first, second)):
        for part in parts:
            axis, cut = part[2][2], part[4]
            if cut or turn == 0:
                for side, step in enumerate((1, -1)):
                    block = block_at(part, here[axis], (side + turn) % 2)
                    copies.append(wire.to(block, block, moved(here, axis, step)))
    for _, _, order, _, _, complete in parts:
        complete(here[order[2]])
    yield
    pending = list(first)
    for part in parts:
        axis, cut = part[2][2], part[4]
        for side, step in enumerate((1, -1)):
            pending.pop(0).wait_recv()
            if cut or side == 0:
                block = block_at(part, lax.rem(here[axis] - step + 4, 4), side)
                onward.append(wire.to(block, block, moved(here, axis, step)))
    yield
    for copy in second:
        copy.wait_recv()
    for _, _, order, _, _, complete in parts:
        for step in (1, 3):
            complete(lax.rem(here[order[2]] + step, 4))
    yield
    for copy in onward:
        copy.wait_recv()
    for _, _, order, _, _, complete in parts:
        complete(lax.rem(here[order[2]] + 2, 4))
    for copy in sent + first + second + onward:
        copy.wait_send()


GATHER_COPIES = 3 + 3 + 6


def lengths_of(full):
    return tuple(n for name in (Y, X, Z) if name in full for n in SIZES[name])


def digits_of(i, lengths):
    digits = []
    for length in reversed(lengths):
        digits.append(lax.rem(i, length))
        i = lax.div(i, length)
    return tuple(digits[::-1])


def one_chip(here, full, axis, value, digits):
    digits, index = list(digits), []
    for name in (Y, X, Z):
        if name in full:
            index += [digits.pop(0) for _ in SIZES[name]]
        else:
            at = value if name == axis else here[name]
            index += [at % 2, at // 2] if name == X else [at]
    return tuple(index)


SCATTER_COPIES = (6, 3, 3)


def scatter_slots(order, rows, wide, cut, double=(0,)):
    slots = []
    for phase in range(3):
        dims = lengths_of(order[phase + 1 :])
        if phase in double:
            slots.append(pltpu.VMEM((2,) + dims + (rows, wide // 2 if cut else wide), BF))
            slots.append(pltpu.VMEM((2,) + dims + (rows, wide), BF))
        else:
            slots.append(pltpu.VMEM((3,) + dims + (rows, wide), BF))
    return slots


def ring_scatter(wire, parts, double=(0,)):
    here = wire.here
    sent, low = [], 0
    for phase in range(3):
        ahead, arriving, early = [], [], []
        slot, last = low, low + (phase in double)
        low = last + 1
        for buffer, prefix, order, cut, slots, _ in parts:
            axis, full = order[phase], order[phase + 1 :]
            row = []
            if phase in double:
                far = prefix + cube_index(here, full, axis, lax.rem(here[axis] + 2, 4))
                for side, step in enumerate((1, -1)):
                    if cut or side == 0:
                        block = buffer.at[far + ((EVERY, side_columns(cut, side)) if cut else ())]
                        row.append(wire.to(block, slots[slot].at[side], moved(here, axis, step)))
                ahead.append(row)
                if cut:
                    for side, step in enumerate((1, -1)):
                        near = cube_index(here, full, axis, lax.rem(here[axis] + step + 4, 4))
                        ready = (EVERY, side_columns(cut, 1 - side))
                        early.append(
                            wire.to(
                                buffer.at[prefix + near + ready],
                                slots[last].at[(side,) + (EVERY,) * len(lengths_of(full)) + ready],
                                moved(here, axis, step),
                            )
                        )
            else:
                for k, step in enumerate((1, -1, 2)):
                    value = lax.rem(here[axis] + step + 4, 4)
                    block = buffer.at[prefix + cube_index(here, full, axis, value)]
                    row.append(
                        wire.to(block, slots[last].at[k], moved(here, axis, step))
                    )
                arriving.append(row)
            sent += row
        yield
        if phase in double:
            for (buffer, prefix, order, cut, slots, _), row in zip(parts, ahead):
                axis, full = order[phase], order[phase + 1 :]
                pair = []
                for side, step in enumerate((1, -1)):
                    value = lax.rem(here[axis] + step + 4, 4)
                    if side < len(row):
                        row[side].wait_recv()
                        half = slots[slot]
                        columns_ = side_columns(cut, side) if cut else EVERY

                        def add(
                            i, _, buffer=buffer, prefix=prefix, axis=axis, full=full, value=value,
                            half=half, side=side, columns_=columns_,
                        ):
                            digits = digits_of(i, lengths_of(full))
                            at = prefix + one_chip(here, full, axis, value, digits)
                            at += (EVERY, columns_)
                            buffer[at] = bfloat(widen(buffer[at]) + widen(half[(side,) + digits]))
                            return 0

                        lax.fori_loop(0, math.prod(lengths_of(full)), add, 0)
                    summed = (EVERY, columns_) if cut else ()
                    block = buffer.at[prefix + cube_index(here, full, axis, value) + summed]
                    target = slots[last].at[(side,) + (EVERY,) * len(lengths_of(full)) + summed]
                    pair.append(wire.to(block, target, moved(here, axis, step)))
                arriving.append(pair)
                sent += pair
            yield
        for copy in early:
            copy.wait_recv()
        sent += early
        for (buffer, prefix, order, _, slots, final), row in zip(parts, arriving):
            axis, full = order[phase], order[phase + 1 :]
            come = slots[last]
            for copy in row:
                copy.wait_recv()

            def total(
                i, _, buffer=buffer, prefix=prefix, axis=axis, full=full, come=come, final=final,
                count=len(row),
            ):
                digits = digits_of(i, lengths_of(full))
                at = prefix + one_chip(here, full, axis, here[axis], digits)
                value = widen(buffer[at])
                for k in range(count):
                    value = value + widen(come[(k,) + digits])
                if phase < 2:
                    buffer[at] = bfloat(value)
                else:
                    final(value)
                return 0

            lax.fori_loop(0, math.prod(lengths_of(full)), total, 0)
    for copy in sent:
        copy.wait_send()


def advance(stages, count=1):
    for _ in range(count):
        next(stages, None)


class Mail:
    def __init__(self, here, send, recv):
        self.here, self.me, self.send, self.recv = here, group_number(here), send, recv
        self.count = 0
        self.sent = []

    def to(self, number, source, target):
        copy = pltpu.make_async_remote_copy(
            src_ref=source,
            dst_ref=target,
            send_sem=self.send.at[self.count],
            recv_sem=self.recv.at[self.me],
            device_id=group_device(self.here, number),
            device_id_type=MESH,
        )
        self.count += 1
        copy.start()
        self.sent.append(copy)

    def finish(self, source, target):
        for k in range(1, CHIPS):
            sender = lax.rem(self.me + k, CHIPS)
            pltpu.make_async_remote_copy(
                src_ref=source,
                dst_ref=target,
                send_sem=self.send.at[0],
                recv_sem=self.recv.at[sender],
                device_id=group_device(self.here, sender),
                device_id_type=MESH,
            ).wait_recv()
        for copy in self.sent:
            copy.wait_send()


BLOCK = 256
SPAN = 1280
STEPS = LENGTH // BLOCK
SLOTS = 4
LAST_START = LENGTH - SPAN


def limits(bounds, first, count):
    places = first + lax.broadcasted_iota(jnp.int32, (1, count), 1)
    low = jnp.maximum(places - (WINDOW // 2 - 1), 0)
    high = jnp.minimum(places + WINDOW // 2, LENGTH)
    for bound in bounds:
        low = jnp.maximum(low, jnp.where(bound <= places, bound, 0))
        high = jnp.minimum(high, jnp.where(bound > places, bound, LENGTH))
    return low, high


def dot(former, latter):
    return jnp.dot(former, latter, preferred_element_type=F32)


def attend_steps(refs, mail, values_ready, between):
    qkv, mixed_t, mixed, inverse = refs.qkv, refs.mixed_t, refs.mixed_head, refs.inverse
    live, end, bounds = LENGTH - refs.pads[0], 0, []
    for k in range(4):
        end = end + refs.lengths[0, k]
        bounds.append(jnp.minimum(end, live))
    keys_rows, ones_v, chances, stage = refs.keys_rows, refs.ones_v, refs.held, refs.mixed_stage
    local = refs.attend_local
    me = mail.me
    keys_rows[...] = qkv[1].T
    ones_v[0:HEAD, :] = jnp.ones((HEAD, LENGTH), BF)
    kept = []

    def weigh(i):
        first = pl.multiple_of(i * BLOCK, BLOCK)
        start = pl.multiple_of(jnp.clip(first - 512, 0, LAST_START), BLOCK)
        scores = dot(keys_rows[pl.ds(start, SPAN), :], qkv[0, :, pl.ds(first, BLOCK)])
        low, high = limits(bounds, first, BLOCK)
        base = lax.broadcasted_iota(jnp.int32, (8, BLOCK), 0) + (start - low)
        steps = 8 * lax.broadcasted_iota(jnp.int32, (SPAN // 8, 8, BLOCK), 0)
        inside = (base[None] + steps).astype(jnp.uint32) < (high - low).astype(jnp.uint32)[None]
        scores = jnp.where(inside, scores.reshape(SPAN // 8, 8, BLOCK), MASKED)
        scores = scores.reshape(SPAN, BLOCK)
        highest = jnp.max(scores, axis=0, keepdims=True)
        chances[i] = bfloat(jnp.exp2((scores - highest) * (SCALE * LOG2E)))

    def mix(i):
        first = pl.multiple_of(i * BLOCK, BLOCK)
        start = pl.multiple_of(jnp.clip(first - 512, 0, LAST_START), BLOCK)
        out = dot(ones_v[:, pl.ds(start, SPAN)], chances[i])
        back = 1.0 / out[0:1]
        result = out[HEAD:] * back
        mixed[:, pl.ds(first, BLOCK)] = result
        stage[:, pl.ds(first, BLOCK)] = bfloat(result)
        inverse[:, pl.ds(first, BLOCK)] = back

    def each(action, slot):
        pair = lax.rem(me // 2 + 1 + slot, SLOTS)

        for t in range(3):
            action(pair * 3 + t)
        return pair

    for slot in range(SLOTS):
        if slot == 0:
            each(weigh, 0)
            each(weigh, 1)
            values_ready()
            ones_v[HEAD:, :] = qkv[2]
        elif slot < SLOTS - 1:
            each(weigh, slot + 1)
        pair = each(mix, slot)
        blocks = pl.ds(pair * 3, 3)
        copy = pltpu.make_async_copy(chances.at[blocks], refs.chances.at[blocks], local.at[slot])
        copy.start()
        kept.append(copy)
        if slot < SLOTS - 1:
            for number in (2 * pair, 2 * pair + 1):
                mail.to(number, stage.at[:, chunk_span(number)], mixed_t.at[me])
        else:
            number = me + 1 - 2 * (me % 2)
            mail.to(number, stage.at[:, chunk_span(number)], mixed_t.at[me])
            copy = pltpu.make_async_copy(
                stage.at[:, chunk_span(me)], mixed_t.at[me], local.at[SLOTS]
            )
            copy.start()
            kept.append(copy)
        between(slot)
    refs.keep(mixed, inverse)
    for copy in kept:
        copy.wait()
    mail.finish(stage.at[:, chunk_span(me)], mixed_t.at[me])


MIXED_T = dict(mixed_t=((CHIPS, HEAD, CHIP_ROWS), BF))
ATTEND_SAVED = dict(mixed_head=((HEAD, LENGTH), F32), inverse=((1, LENGTH), F32))
CHANCES = ((STEPS, SPAN, BLOCK), BF)
ATTEND_SCRATCH = dict(
    keys_rows=((LENGTH, HEAD), BF), ones_v=((2 * HEAD, LENGTH), BF), held=CHANCES,
    mixed_stage=((HEAD, LENGTH), BF),
)
MAIL_SEMS = [pltpu.SemaphoreType.DMA((CHIPS - 1,)), pltpu.SemaphoreType.DMA((CHIPS,))]


def call(
    body, name, number, near, loaded, sources, outputs, saved, far, scratch, semaphores, scalars={}
):
    vmem, hbm = pl.BlockSpec(memory_space=pltpu.VMEM), pl.BlockSpec(memory_space=pltpu.HBM)
    smem = pl.BlockSpec(memory_space=pltpu.SMEM)
    scratch = dict(scratch)
    for key, value in loaded.items():
        scratch[key] = (value.shape, value.dtype)
    scratch.update(saved)
    specs = [*outputs.values(), *saved.values(), *far.values()]

    def size(shape, dtype):
        rows, lanes = (1,) * (2 - len(shape[-2:])) + tuple(shape[-2:])
        rows, lanes = -(-rows // 8) * 8, -(-lanes // 128) * 128
        return math.prod(shape[:-2]) * rows * lanes * jnp.dtype(dtype).itemsize

    held = [(value.shape, value.dtype) for value in near.values()] + list(outputs.values())
    held += [s if isinstance(s, tuple) else (s.shape, s.dtype) for s in scratch.values()]
    limit = sum(size(*spec) for spec in held) + 10 * 2**20

    def kernel(*values):
        values = list(values)

        def take(names):
            return {key: values.pop(0) for key in names}

        refs = types.SimpleNamespace(**take(scalars), **take(near))
        heres = take(loaded)
        for key, ref in take(sources).items():
            setattr(refs, key, ref)
        for key, ref in take(outputs).items():
            setattr(refs, key, ref)
        outs = take(saved)
        for names in (far, scratch):
            for key, ref in take(names).items():
                setattr(refs, key, ref)
        copies = values.pop(0)
        pending = [
            pltpu.make_async_copy(ref, getattr(refs, key), copies.at[k])
            for k, (key, ref) in enumerate(heres.items())
        ]
        for copy in pending:
            copy.start()
        kept = []

        def arrive():
            for copy in pending:
                copy.wait()

        def keep(*arrays):
            for k, (key, out) in enumerate(outs.items()):
                if any(getattr(refs, key) is array for array in arrays):
                    copy = pltpu.make_async_copy(
                        getattr(refs, key), out, copies.at[len(heres) + k]
                    )
                    copy.start()
                    kept.append(copy)

        refs.arrive, refs.keep = arrive, keep
        body(refs, values)
        for copy in kept:
            copy.wait()

    results = pl.pallas_call(
        kernel,
        out_shape=tuple(jax.ShapeDtypeStruct(*spec) for spec in specs),
        in_specs=[smem] * len(scalars)
        + [vmem] * len(near)
        + [hbm] * (len(loaded) + len(sources)),
        out_specs=(vmem,) * len(outputs) + (hbm,) * (len(saved) + len(far)),
        scratch_shapes=[
            pltpu.VMEM(*spec) if isinstance(spec, tuple) else spec for spec in scratch.values()
        ]
        + [dma(max(1, len(loaded) + len(saved)))]
        + list(semaphores),
        name=name,
        compiler_params=pltpu.CompilerParams(
            collective_id=number, has_side_effects=True, vmem_limit_bytes=max(limit, 58 * 2**20)
        ),
    )(*scalars.values(), *near.values(), *loaded.values(), *sources.values())
    return types.SimpleNamespace(**dict(zip([*outputs, *saved, *far], results)))


def dma(count):
    return pltpu.SemaphoreType.DMA((count,))


PAD = 2 * BLOCK
PADDED = LENGTH + 2 * PAD


def fetch_chances(refs):
    copies = []
    for slot in range(SLOTS):
        blocks = pl.ds(slot * 3, 3)
        copy = pltpu.make_async_copy(
            refs.chances.at[blocks], refs.held.at[blocks], refs.attend_local.at[slot]
        )
        copy.start()
        copies.append(copy)
    refs.early = copies


def prepare_back(refs):
    qkv, turned_d, rows_q, rows_d, shift = refs.qkv, refs.turned_d, refs.rows_q, refs.rows_d, refs.shift
    refs.kv[...] = jnp.concatenate([qkv[1], qkv[2]], axis=0).T
    for edge in (0, PAD + LENGTH):
        shift[:, edge : edge + PAD] = jnp.zeros((1, PAD), F32)
        turned_d[:, edge : edge + PAD] = jnp.zeros((2 * HEAD, PAD), BF)
        rows_q[edge : edge + PAD, :] = jnp.zeros((PAD, 2 * HEAD), BF)
        rows_d[edge : edge + PAD, :] = jnp.zeros((PAD, 2 * HEAD), BF)
    middle = slice(PAD, PAD + LENGTH)
    turned_d[0:HEAD, middle] = jnp.zeros((HEAD, LENGTH), BF)
    none = jnp.zeros((HEAD, LENGTH), BF)
    rows_q[middle, :] = jnp.concatenate([qkv[0], none], axis=0).T
    refs.total_q[...] = jnp.zeros((HEAD, PADDED), F32)


def attend_back_steps(refs, mail_q, mail_kv, between):
    qkv, mixed, inverse, d_mixed = refs.qkv, refs.mixed_head, refs.inverse, refs.d_mixed
    d_q_t, d_kv_t, chances, kv = refs.d_q_t, refs.d_kv_t, refs.held, refs.kv
    rows_q, rows_d, turned_d, shift = refs.rows_q, refs.rows_d, refs.turned_d, refs.shift
    total_q, stage_q, stage_kv = refs.total_q, refs.stage_q, refs.stage_kv
    me = mail_q.me
    scaled = bfloat(widen(d_mixed[...]) * inverse[...])
    middle = slice(PAD, PAD + LENGTH)
    shift[:, middle] = jnp.sum(widen(scaled) * mixed[...], axis=0, keepdims=True)
    turned_d[HEAD:, middle] = scaled
    rows_d[middle, :] = turned_d[:, middle].T
    for copy in refs.early:
        copy.wait()
    between(-1)

    def step(i):
        first = pl.multiple_of(i * BLOCK, BLOCK)
        keys = pl.ds(first, BLOCK)
        span = pl.ds(first, SPAN)
        tiles = []
        for t in range(5):
            block = jnp.clip(i - 2 + t, 0, STEPS - 1)
            start = jnp.clip(block * BLOCK - 512, 0, LAST_START)
            offset = pl.multiple_of(jnp.clip(first - start, 0, SPAN - BLOCK), BLOCK)
            tiles.append(chances[block, pl.ds(offset, BLOCK), :])
        weights = jnp.concatenate(tiles, axis=1)
        grad_weights = dot(kv[keys, :], turned_d[:, span])
        grad_scores = bfloat(widen(weights) * (grad_weights - shift[:, span]))
        total = dot(weights, rows_d[span, :]) + dot(grad_scores, rows_q[span, :])
        total_q[:, span] += dot(qkv[1, :, keys], grad_scores)
        turned = total.T
        stage_kv[0:HEAD, keys] = bfloat(turned[:HEAD] * SCALE)
        stage_kv[HEAD:, keys] = bfloat(turned[HEAD:])

    def send_queries(number):
        span = pl.ds(pl.multiple_of(number * CHIP_ROWS + PAD, 128), CHIP_ROWS)
        stage_q[number] = bfloat(total_q[:, span] * SCALE)
        mail_q.to(number, stage_q.at[number], d_q_t.at[me])

    near = me + 1 - 2 * (me % 2)
    for slot in range(SLOTS):
        pair = lax.rem(me // 2 + 1 + slot, SLOTS)

        for t in range(3):
            step(pair * 3 + t)
        if slot < SLOTS - 1:
            for number in (2 * pair, 2 * pair + 1):
                mail_kv.to(number, stage_kv.at[:, chunk_span(number)], d_kv_t.at[me])
        else:
            mail_kv.to(near, stage_kv.at[:, chunk_span(near)], d_kv_t.at[me])
        if slot == 2:
            complete = lax.rem(me // 2 + 2, SLOTS)
            send_queries(2 * complete)
            send_queries(2 * complete + 1)
        between(slot)
    for rest in (1, 3):
        pair = lax.rem(me // 2 + rest, SLOTS)
        send_queries(2 * pair)
        send_queries(2 * pair + 1)
    send_queries(near)
    between(SLOTS)
    span = pl.ds(pl.multiple_of(me * CHIP_ROWS + PAD, 128), CHIP_ROWS)
    d_q_t[me] = bfloat(total_q[:, span] * SCALE)
    d_kv_t[me] = stage_kv[:, chunk_span(me)]
    mail_kv.finish(stage_kv.at[:, chunk_span(me)], d_kv_t.at[me])
    between(SLOTS + 1)
    mail_q.finish(stage_q.at[me], d_q_t.at[me])


BACK_SCRATCH = dict(
    held=CHANCES, kv=((LENGTH, 2 * HEAD), BF), rows_q=((PADDED, 2 * HEAD), BF),
    rows_d=((PADDED, 2 * HEAD), BF), turned_d=((2 * HEAD, PADDED), BF), shift=((1, PADDED), F32),
    total_q=((HEAD, PADDED), F32), stage_q=((CHIPS, HEAD, CHIP_ROWS), BF),
    stage_kv=((2 * HEAD, LENGTH), BF),
)
BACK_OUTPUTS = dict(
    d_q_t=((CHIPS, HEAD, CHIP_ROWS), BF), d_kv_t=((CHIPS, 2 * HEAD, CHIP_ROWS), BF)
)


REST_DOUBLE = (0, 1)
REST = ((64, HALF), (80, HALF // 2), (80, HALF // 2))


def dot_nt(former, latter):
    return lax.dot_general(former, latter, (((1,), (1,)), ((), ())), preferred_element_type=F32)


QKV, OUT, IN, BACK = range(4)


class Weights:
    def __init__(self, refs, wire, names):
        self.refs, self.pending = refs, {}
        for name in names:
            if name == QKV:
                pairs = [(refs.gqkv, refs.w_qkv)]
            elif name == IN:
                pairs = [
                    (refs.rest_one.at[CUBE_ALL + (pl.ds(16 * k, 16),)], refs.w_in.at[k])
                    for k in range(4)
                ]
            elif name == OUT:
                pairs = [(refs.gout, refs.w_out)]
            else:
                pairs = [(refs.gback, refs.w_back)]
            self.pending[name] = [wire.fetch(*pair) for pair in pairs]

    def ready(self, name):
        for copy in self.pending.pop(name, []):
            copy.wait()

    def qkv(self, k):
        self.ready(QKV)
        return self.refs.w_qkv[k].reshape(D, HALF)

    def out(self, half):
        self.ready(OUT)
        return self.refs.w_out[half].reshape(HALF, HALF)

    def into(self, chunk):
        self.ready(IN)
        return self.refs.w_in[chunk].reshape(D, HALF)

    def back(self, half, chunk):
        self.ready(BACK)
        return self.refs.w_back[half, chunk // 2, chunk % 2].reshape(HALF, HALF)


def columns(k):
    return slice(k * HALF, k * HALF + HALF)


def vector(refs, k):
    return refs.vecs[k : k + 1, :]


def half_vector(refs, core, k):
    return refs.vecs[k : k + 1, pl.ds(pl.multiple_of(core * HALF, HALF), HALF)]


B_QUERY, B_VALUE, B_OUT, GAIN_ATTN, SHIFT_ATTN, B_BACK, GAIN_FFN, SHIFT_FFN = range(8)


def normalized(tensor):
    centred = tensor - jnp.mean(tensor, axis=-1, keepdims=True)
    factor = lax.rsqrt(jnp.mean(centred * centred, axis=-1, keepdims=True) + EPSILON)
    return centred * factor, factor


def normalize_back(grad_out, normed, factor, gain):
    grad_normed = grad_out * gain
    grad_input = factor * (
        grad_normed
        - jnp.mean(grad_normed, axis=-1, keepdims=True)
        - normed * jnp.mean(grad_normed * normed, axis=-1, keepdims=True)
    )
    return (
        grad_input,
        jnp.sum(grad_out * normed, axis=0, keepdims=True),
        jnp.sum(grad_out, axis=0, keepdims=True),
    )


def row_sum(tensor):
    return jnp.sum(widen(tensor), axis=0, keepdims=True)


def gelu_pair(v):
    root = math.sqrt(2.0 / math.pi)
    squared = v * v
    scaled = root * v
    half = 0.5 + 0.5 * jnp.tanh(scaled * (1.0 + 0.044715 * squared))
    slope = half + half * (1.0 - half) * scaled * (2.0 + (6 * 0.044715) * squared)
    return v * half, slope


def summed_over_cores(refs, wire, fill):
    send, come, kept = refs.outgoing.at[refs.round], refs.incoming.at[refs.round], refs.kept
    refs.round += 1
    fill(wire.other, send)
    copy = wire.swap(send, come)
    fill(wire.own, kept)
    copy.wait()
    return kept[...] + widen(come[...])


def project_rows(refs, wire, weight, copy, between):
    entry, rows_of, stage = refs.entry, refs.qkv_rows, refs.qkv_stage
    biases = (half_vector(refs, wire.core, B_QUERY), None, half_vector(refs, wire.core, B_VALUE))

    def project(rows, k):
        result = dot(entry[rows, :], weight(k))
        if biases[k] is not None:
            result = result + biases[k]
        rows_of[k, rows, :] = bfloat(result)

    for k in range(3):
        project(wire.own, k)
    copy.wait()
    refs.keep(entry)
    between()
    copies = []
    for k in range(3):
        project(wire.other, k)
        stage[k] = rows_of[k].T.reshape(CHIPS, HEAD, CHIP_ROWS)
        copies += wire.spread(stage.at[k], refs.qkv.at[k])
    return copies


def part_project(refs, wire, weights, hidden):
    entry = refs.entry
    entry[wire.own, :] = bfloat(hidden)
    copy = wire.swap(entry.at[wire.own], entry.at[wire.own])
    return project_rows(refs, wire, weights.qkv, copy, lambda: None)


def part_post(refs, wire, weights):
    mixed = refs.mixed
    mixed[...] = refs.mixed_t_in[...].reshape(HALF, CHIP_ROWS).T

    def leave(rows, target):
        for half in range(2):
            target[:, columns(half)] = dot(mixed[rows, :], weights.out(half)).astype(target.dtype)

    branch = summed_over_cores(refs, wire, leave)
    normed, factor = normalized(widen(refs.hidden[...]) + branch + vector(refs, B_OUT))
    refs.normed_one[...] = normed
    refs.factor_one[...] = factor
    refs.keep(refs.normed_one, refs.factor_one)
    first = normed * vector(refs, GAIN_ATTN) + vector(refs, SHIFT_ATTN)
    refs.first[...] = first
    entry_two, active, slope = refs.entry_two, refs.active, refs.slope
    entry_two[wire.own, :] = bfloat(first)
    copy = wire.swap(entry_two.at[wire.own], entry_two.at[wire.own])

    def inner(rows):
        for chunk in range(4):
            start = pl.multiple_of(wire.core * 2048 + chunk * HALF, HALF)
            before = dot(entry_two[rows, :], weights.into(chunk)) + refs.b_in[:, pl.ds(start, HALF)]
            value, steep = gelu_pair(before)
            active[rows, columns(chunk)] = bfloat(value)
            slope[rows, columns(chunk)] = bfloat(steep)

    inner(wire.own)
    copy.wait()
    refs.keep(entry_two)
    inner(wire.other)
    refs.keep(active, slope)

    def leave_two(rows, target):
        for half in range(2):
            total = dot(active[rows, columns(0)], weights.back(half, 0))
            for chunk in range(1, 4):
                total = total + dot(active[rows, columns(chunk)], weights.back(half, chunk))
            target[:, columns(half)] = total.astype(target.dtype)

    second = summed_over_cores(refs, wire, leave_two)
    normed, factor = normalized(refs.first[...] + second + vector(refs, B_BACK))
    refs.normed_two[...] = normed
    refs.factor_two[...] = factor
    refs.keep(refs.normed_two, refs.factor_two)
    return normed * vector(refs, GAIN_FFN) + vector(refs, SHIFT_FFN)


def part_back_dense(refs, wire, weights, grad_out):
    d_branch, d_before, d_attn = refs.d_branch, refs.d_before, refs.d_attn
    sums = refs.sums
    d_second, g_gain, g_shift = normalize_back(
        grad_out, refs.normed_two[...], refs.factor_two[...], vector(refs, GAIN_FFN)
    )
    refs.d_second[...] = d_second
    d_branch[wire.own, :] = bfloat(d_second)
    copy = wire.swap(d_branch.at[wire.own], d_branch.at[wire.own])
    sums[GAIN_FFN : GAIN_FFN + 1, :] = g_gain
    sums[SHIFT_FFN : SHIFT_FFN + 1, :] = g_shift
    sums[B_BACK : B_BACK + 1, :] = row_sum(d_branch[wire.own, :])

    def inner(rows):
        for chunk in range(4):
            d_active = dot_nt(d_branch[rows, columns(0)], weights.back(0, chunk)) + dot_nt(
                d_branch[rows, columns(1)], weights.back(1, chunk)
            )
            d_before[rows, columns(chunk)] = bfloat(
                d_active * widen(refs.slope[rows, columns(chunk)])
            )

    inner(wire.own)
    copy.wait()
    refs.keep(d_branch)
    inner(wire.other)
    refs.keep(d_before)
    for chunk in range(4):
        start = pl.multiple_of(wire.core * 2048 + chunk * HALF, HALF)
        refs.sums_in[:, pl.ds(start, HALF)] = row_sum(d_before[:, columns(chunk)])

    def leave(rows, target):
        total = dot_nt(d_before[rows, columns(0)], weights.into(0))
        for chunk in range(1, 4):
            total = total + dot_nt(d_before[rows, columns(chunk)], weights.into(chunk))
        target[...] = total.astype(target.dtype)

    d_first = refs.d_second[...] + summed_over_cores(refs, wire, leave)
    d_inner, g_gain, g_shift = normalize_back(
        d_first, refs.normed_one[...], refs.factor_one[...], vector(refs, GAIN_ATTN)
    )
    refs.d_inner_out[...] = d_inner
    refs.keep(refs.d_inner_out)
    d_attn[wire.own, :] = bfloat(d_inner)
    copy = wire.swap(d_attn.at[wire.own], d_attn.at[wire.own])
    sums[GAIN_ATTN : GAIN_ATTN + 1, :] = g_gain
    sums[SHIFT_ATTN : SHIFT_ATTN + 1, :] = g_shift
    sums[B_OUT : B_OUT + 1, :] = row_sum(d_attn[wire.own, :])
    rows_of, stage = refs.d_mixed_rows, refs.d_mixed_stage

    def enter(rows):
        rows_of[rows, :] = bfloat(
            dot_nt(d_attn[rows, columns(0)], weights.out(0))
            + dot_nt(d_attn[rows, columns(1)], weights.out(1))
        )

    enter(wire.own)
    copy.wait()
    refs.keep(d_attn, refs.sums, refs.sums_in)
    enter(wire.other)
    stage[...] = rows_of[...].T.reshape(CHIPS, HEAD, CHIP_ROWS)
    return wire.spread(stage, refs.d_mixed)


def turn_queries(refs):
    refs.d_qkv[0] = refs.d_q_t[...].reshape(HALF, CHIP_ROWS).T


def turn_keys_values(refs):
    rows_of = refs.d_qkv
    rows_of[1] = refs.d_kv_t[:, :HEAD, :].reshape(HALF, CHIP_ROWS).T
    rows_of[2] = refs.d_kv_t[:, HEAD:, :].reshape(HALF, CHIP_ROWS).T


def add_half(refs, wire, k, value):
    half = pl.ds(pl.multiple_of(wire.core * HALF, HALF), HALF)
    refs.sums[k : k + 1, half] = refs.sums[k : k + 1, half] + value


def part_back_project(refs, wire, weights):
    rows_of = refs.d_qkv

    def leave(rows, target):
        total = dot_nt(rows_of[0, rows, :], weights.qkv(0))
        for k in range(1, 3):
            total = total + dot_nt(rows_of[k, rows, :], weights.qkv(k))
        target[...] = total.astype(target.dtype)

    return refs.d_inner[...] + summed_over_cores(refs, wire, leave)


ROW_F32 = ((ROWS, D), F32)
COLUMN_F32 = ((ROWS, 1), F32)
CHIP_BF = ((CHIP_ROWS, D), BF)
WIDE_BF = ((CHIP_ROWS, 2048), BF)
HEADS_BF = ((CHIP_ROWS, HALF), BF)
STAGE = (CHIPS, HEAD, CHIP_ROWS)
POST, BACK_DENSE, BACK_PROJECT, ATTEND_BACK, GRADIENTS = range(5)
WHOLE_GRADIENTS = dict(
    g_in=(CUBE + (16, 2048), BF), g_back=((2, 2, 2, 4, 64, D), BF), g_out=((2, 2, 2, 4, 16, D), BF)
)
PARTS = (
    (
        (OUT, IN, BACK),
        dict(
            normed_one=ROW_F32, factor_one=COLUMN_F32, entry_two=CHIP_BF,
            active=WIDE_BF, slope=WIDE_BF, normed_two=ROW_F32, factor_two=COLUMN_F32,
        ),
        {},
        dict(first=ROW_F32, mixed=HEADS_BF),
        4,
        0,
    ),
    (
        (BACK, IN, OUT),
        dict(
            d_branch=CHIP_BF, d_before=WIDE_BF, d_attn=CHIP_BF, d_inner_out=ROW_F32,
            sums=((8, D), F32), sums_in=((1, FF), F32),
        ),
        dict(d_mixed=((HEAD, LENGTH), BF)),
        dict(d_second=ROW_F32, d_mixed_rows=HEADS_BF, d_mixed_stage=(STAGE, BF)),
        3 + 7,
        1,
    ),
    (
        (QKV,),
        dict(d_qkv=((3, CHIP_ROWS, HALF), BF)),
        {},
        {},
        1,
        0,
    ),
    ((), {}, BACK_OUTPUTS, BACK_SCRATCH, 0, 0),
    ((), WHOLE_GRADIENTS, {}, {}, 0, 0),
)
WEIGHT_SHAPES = (
    dict(w_qkv=((3,) + CUBE + (16, HALF), BF)),
    dict(w_out=((2, 2, 2, 2, 4, 16, HALF), BF)),
    dict(w_in=((4,) + CUBE + (16, HALF), BF)),
    dict(w_back=((2, 2, 2, 2, 4, 64, HALF), BF)),
)


WEIGHT_COPIES = (1, 1, 4, 1)


def weight_gradients(refs, mixed_t, add, ready):
    def store(ref, at, value):
        value = value.reshape(ref[at].shape)
        ref[at] = bfloat(value + widen(ref[at])) if add else bfloat(value)

    for chunk in range(4):
        value = dot(refs.active[:, columns(chunk)].T, refs.d_branch[...])
        store(refs.g_back, (chunk // 2, chunk % 2), value)
    refs.keep(refs.g_back)
    store(refs.g_out, CUBE_ALL, dot(mixed_t.reshape(HALF, CHIP_ROWS), refs.d_attn[...]))
    refs.keep(refs.g_out)
    ready()
    turned = refs.entry_two[...].T
    for chunk in range(4):
        value = dot(turned, refs.d_before[:, columns(chunk)])
        store(refs.g_in, CUBE_ALL + (EVERY, columns(chunk)), value)
    refs.keep(refs.g_in)


def dense(
    parts, number, gathered, loaded, late, extra, dropped=(), sources={}, added={}
):
    outputs, saved, weight_names, sems = {}, dict(extra), [], []
    rounds = 2 * (POST in parts) + (BACK_DENSE in parts) + (BACK_PROJECT in parts)
    sums = ((rounds, ROWS, D), BF)
    scratch = dict(outgoing=sums, incoming=sums, kept=ROW_F32)
    copies = locals_ = 0
    for part in parts:
        its_weights, its_saved, its_outputs, its_scratch, its_copies, its_locals = PARTS[part]
        weight_names += [name for name in its_weights if name not in weight_names]
        outputs.update(its_outputs)
        saved.update(its_saved)
        scratch.update(its_scratch)
        copies += its_copies
        locals_ += its_locals
    for name, value in late.items():
        scratch[name] = (value.shape, value.dtype)
    for name in dropped:
        scratch[name] = {**saved, **outputs}[name]
        saved.pop(name, None)
        outputs.pop(name, None)
    for name in weight_names:
        scratch.update(WEIGHT_SHAPES[name])
        locals_ += WEIGHT_COPIES[name]
    far = {}
    if added:
        far = dict(come_back=((2, 2, 2, 4, 64, HALF), BF), come_out=((2, 2, 2, 4, 16, HALF), BF))
    if ATTEND_BACK in parts:
        sems = MAIL_SEMS + MAIL_SEMS + [dma(SLOTS)]

    def body(refs, semaphores):
        here = place()
        wire = Wire(here, *semaphores[:3])
        refs.round = 0
        weights = Weights(refs, wire, weight_names)
        after_first = []
        if BACK_DENSE in parts:
            refs.sums[...] = jnp.zeros((8, D), F32)
            refs.sums_in[...] = jnp.zeros((1, FF), F32)
        if ATTEND_BACK in parts:
            refs.attend_local = semaphores[-1]
        greet([partner(here)] + group(here))
        refs.arrive()
        pending = []
        value = None
        for step, part in enumerate(parts):
            if step == 1:
                for key in (*late, *added):
                    after_first.append(wire.fetch(getattr(refs, key + LATER), getattr(refs, key)))
                if ATTEND_BACK in parts:
                    fetch_chances(refs)
            if part == POST:
                value = part_post(refs, wire, weights)
                refs.result[...] = value.astype(refs.result.dtype)
                refs.keep(refs.result)
            elif part == BACK_DENSE:
                if POST in parts:
                    value = widen(refs.cotangent[...])
                pending += part_back_dense(refs, wire, weights, value)
            elif part == BACK_PROJECT:
                turn_queries(refs)
                turn_keys_values(refs)
                refs.keep(refs.d_qkv)
                add_half(refs, wire, B_QUERY, row_sum(refs.d_qkv[0]))
                add_half(refs, wire, B_VALUE, row_sum(refs.d_qkv[2]))
                value = part_back_project(refs, wire, weights)
            elif part == GRADIENTS:
                for copy in after_first:
                    copy.wait()

                def ready():
                    if added:
                        low = pl.multiple_of((1 - wire.core) * HALF, HALF)
                        span = CUBE_ALL + (EVERY, pl.ds(low, HALF))
                        pending.append(wire.swap(refs.g_back.at[span], refs.come_back))
                        pending.append(wire.swap(refs.g_out.at[span], refs.come_out))

                weight_gradients(refs, refs.mixed_t_in[...], bool(added), ready)
            else:
                prepare_back(refs)
                for copy in pending:
                    copy.wait()
                pending = []
                send, recv, send_two, recv_two, _ = semaphores[3:]
                attend_back_steps(
                    refs, Mail(here, send, recv), Mail(here, send_two, recv_two), lambda slot: None
                )
        for copy in pending:
            copy.wait()

    return call(
        body, "dense_%d" % number, number, {},
        dict(loaded, vecs=gathered.vecs, b_in=gathered.b_in),
        dict(
            sources, gqkv=gathered.gqkv, gout=gathered.gout, gback=gathered.gback,
            rest_one=gathered.rest_one,
            **{key + LATER: value for key, value in (*late.items(), *added.items())},
        ),
        outputs, saved, far, scratch, [dma(copies + 2), dma(copies + 2), dma(locals_ + 6)] + sems,
    )


LATER = "_later"


class Arriving(Weights):
    def __init__(self, refs, pending):
        self.refs, self.pending = refs, pending

    def ready(self, name):
        self.pending.pop(name, lambda: None)()


LAYER_SAVED = dict(
    mixed_head=((HEAD, LENGTH), F32), inverse=((1, LENGTH), F32), entry=CHIP_BF,
    qkv=((3, HEAD, LENGTH), BF),
)
SECOND = "_second"


def opening(lengths, pads, shards, vectors, tokens, number):
    def body(refs, semaphores):
        send, recv, local = semaphores[:3]
        here = place()
        wire = Wire(here, send, recv, local)
        core = wire.core
        refs.round = 0
        greet(neighbours(here, (1, -1, 2)) + group(here))
        refs.arrive()
        tok = lax.axis_index("tok")
        lanes = lax.broadcasted_iota(jnp.int32, (1, 128), 1)
        line = widen(refs.vectors[...])
        rows = []
        for k in range(8):
            turned = pltpu.roll(line, lax.rem(tok * 8 - 8 * k + 128, 128), 1)
            rows.append(jnp.where(lanes // 8 == tok, turned, 0.0))
        turned = pltpu.roll(line, lax.rem(lax.rem(tok, 4) * 32 + 64, 128), 1)
        turned = jnp.where(lanes // 32 == lax.rem(tok, 4), turned, 0.0)
        for k in range(4):
            rows.append(jnp.where(lax.div(tok, 4) == k, turned, jnp.zeros_like(turned)))
        rows.append(jnp.zeros((4, 128), F32))
        refs.small[...] = bfloat(jnp.concatenate(rows, axis=0))
        thin = [widen(ref[...]) for ref in (refs.s_query, refs.s_key, refs.s_value, refs.s_out)]
        wide, back = widen(refs.s_in[...]), refs.s_back[...]
        for half in range(2):
            span = columns(half)
            spread = [wide[:, columns(4 * half + k)] for k in range(4)]
            pieces = [thin[k][:, span] for k in range(3)] + spread[:3]
            refs.pack[half, 0:48, :] = bfloat(jnp.concatenate(pieces, axis=0))
            refs.pack[half, 48:80, :] = back[:, span]
            refs.pack[half, 80:96, :] = bfloat(
                jnp.concatenate([spread[3], thin[3][:, span]], axis=0)
            )
        swaps = [
            wire.swap(refs.pack.at[1 - core], refs.theirs),
            wire.swap(refs.small, refs.small_theirs),
        ]
        entry = refs.entry
        entry[wire.own, :] = refs.tokens[...]
        entry_copy = wire.swap(refs.tokens, entry.at[wire.own])
        for copy in swaps:
            copy.wait()

        def build(low, high):
            low, high = widen(low), widen(high)

            def both(row):
                return bfloat(jnp.concatenate([low[row : row + 8], high[row : row + 8]], axis=0))

            for k in range(3):
                refs.own_qkv[k] = both(8 * k)
                refs.own_one[16 * k : 16 * k + 16, :] = both(24 + 8 * k)
            refs.own_one[48:64, :] = both(80)
            back = bfloat(jnp.concatenate([low[48:80], high[48:80]], axis=0))
            refs.own_out[...] = both(88)
            refs.own_two[...] = back[:, 0:256]
            refs.own_three[...] = back[:, 256:512]

        @pl.when(core == 0)
        def _():
            build(refs.pack[0], refs.theirs[...])

        @pl.when(core == 1)
        def _():
            build(refs.theirs[...], refs.pack[1])

        refs.own_small[...] = refs.small[...] + refs.small_theirs[...]

        def nothing(value):
            pass

        parts = [
            (refs.w_qkv, (k,), GATHER_ORDERS[k], refs.own_qkv.at[k], HALF, nothing)
            for k in range(3)
        ]
        for k, ref in enumerate((refs.all_out, refs.all_out_two)):
            own = refs.own_out.at[:, side_columns(HALF, k)]
            parts.append((ref, (), GATHER_ORDERS[1 + k], own, HALF // 2, nothing))
        parts.append((refs.all_small, (), GATHER_ORDERS[3], refs.own_small, 0, nothing))
        first_stages = ring_gather(wire, parts)
        mine, yours = pl.ds(2 * core, 2), pl.ds(2 * (1 - core), 2)
        taken, passed = [], []

        def take_one(value):
            for k in range(4):
                taken.append(
                    wire.fetch(
                        refs.rest_one.at[value, :, :, :, pl.ds(16 * k, 16)], refs.w_in.at[k, value]
                    )
                )

        def pass_part(ref, side, place_of):
            def take(value):
                target = refs.w_back.at[
                    (core, EVERY) + place_of(value) + (EVERY, side_columns(HALF, side))
                ]
                passed.append(wire.swap(ref.at[(yours,) + place_of(value)], target))
                passed.append(wire.fetch(ref.at[(mine,) + place_of(value)], target))

            return take

        pass_two = pass_part(refs.rest_two, 0, lambda z: (EVERY, EVERY, z))
        pass_three = pass_part(refs.rest_three, 1, lambda x: (x % 2, x // 2, EVERY))

        long_stages = ring_gather(
            wire, [(refs.rest_one, (), GATHER_ORDERS[0], refs.own_one, HALF, take_one)]
        )
        stages = ring_gather(
            wire,
            [
                (refs.rest_two, (), GATHER_ORDERS[1], refs.own_two, HALF // 2, pass_two),
                (refs.rest_three, (), GATHER_ORDERS[2], refs.own_three, HALF // 2, pass_three),
            ],
        )
        for ring in (first_stages, long_stages, stages, first_stages, first_stages, long_stages):
            advance(ring)
        advance(stages)
        for _ in first_stages:
            pass
        kept = wire.fetch(refs.w_qkv, refs.gqkv)
        out_copies = []
        for k, ref in enumerate((refs.all_out, refs.all_out_two)):
            into = refs.w_out.at[(core,) + (EVERY,) * 5 + (side_columns(HALF, k),)]
            out_copies += [wire.swap(ref.at[yours], into), wire.fetch(ref.at[mine], into)]
        for s in range(8):
            tile = jnp.zeros((16, 128), F32)
            for x_hi in range(2):
                for z in range(4):
                    tile = tile + widen(refs.all_small[s // 2, s % 2, x_hi, z])
            refs.vecs[:, 128 * s : 128 * s + 128] = tile[:8]
            for j in range(4):
                low = HALF * s + 128 * j
                refs.b_in[:, low : low + 128] = tile[8 + j : 9 + j]
        refs.keep(refs.vecs, refs.b_in)
        refs.attend_local = semaphores[5]
        pending = project_rows(
            refs, wire, lambda k: refs.w_qkv[k].reshape(D, HALF), entry_copy, lambda: advance(long_stages)
        )
        for copy in pending[: 2 * CHIPS]:
            copy.wait()
        advance(stages)

        def values_ready():
            for copy in pending[2 * CHIPS :]:
                copy.wait()
            refs.keep(refs.qkv)

        def between(slot):
            if slot == 0:
                advance(long_stages)
            elif slot == 2:
                advance(stages)
            elif slot == 3:
                advance(long_stages)

        attend_steps(refs, Mail(here, *semaphores[3:5]), values_ready, between)

        def out_ready():
            for copy in out_copies:
                copy.wait()
            refs.keep(refs.w_out)

        def in_ready():
            advance(stages)
            for _ in long_stages:
                pass
            for copy in taken:
                copy.wait()

        def back_ready():
            for _ in stages:
                pass
            for copy in passed:
                copy.wait()
            refs.keep(refs.w_back)

        mixed_copy = wire.fetch(refs.mixed_t, refs.mixed_t_one)
        weights = Arriving(refs, {OUT: out_ready, IN: in_ready, BACK: back_ready})
        refs.mixed_t_in = refs.mixed_t
        refs.hidden = refs.tokens
        value = part_post(refs, wire, weights)
        refs.result[...] = value
        refs.keep(refs.result)
        second = types.SimpleNamespace(**vars(refs))
        second.attend_local = semaphores[-1]
        for name in [*LAYER_SAVED, *MIXED_T, CHANCES_NAME]:
            setattr(second, name, getattr(refs, name + SECOND))
        pending = part_project(second, wire, weights, value)
        for copy in pending[: 2 * CHIPS]:
            copy.wait()

        def second_ready():
            for copy in pending[2 * CHIPS :]:
                copy.wait()
            refs.keep(second.qkv)

        attend_steps(second, Mail(here, *semaphores[6:8]), second_ready, lambda slot: None)
        kept.wait()
        mixed_copy.wait()

    cube_16 = (CUBE + (16, HALF // 2), BF)
    scratch = dict(
        ATTEND_SCRATCH, pack=((2, 96, HALF), BF), small=((16, 128), BF), theirs=((96, HALF), BF),
        small_theirs=((16, 128), BF), own_qkv=((3, 16, HALF), BF), own_out=((16, HALF), BF),
        own_one=((64, HALF), BF), own_two=((64, HALF // 2), BF), own_three=((64, HALF // 2), BF),
        own_small=((16, 128), BF), w_qkv=((3,) + CUBE + (16, HALF), BF), all_out=cube_16, all_out_two=cube_16,
        all_small=(CUBE + (16, 128), BF), qkv_rows=((3, CHIP_ROWS, HALF), BF),
        qkv_stage=((3,) + STAGE, BF), outgoing=((2, ROWS, D), BF), incoming=((2, ROWS, D), BF),
        kept=ROW_F32, first=ROW_F32, mixed=HEADS_BF, mixed_t=MIXED_T[MIXED_NAME],
    )
    scratch.update(WEIGHT_SHAPES[IN])
    saved = dict(LAYER_SAVED, vecs=((8, D), F32), b_in=((1, FF), F32), result=ROW_F32)
    saved.update(WEIGHT_SHAPES[OUT])
    saved.update(WEIGHT_SHAPES[BACK])
    saved.update(PARTS[POST][1])
    saved.update({name + SECOND: spec for name, spec in LAYER_SAVED.items()})
    narrow = (CUBE + (64, HALF // 2), BF)
    copies = 3 + 9 * GATHER_COPIES + 10 + 2 * 21 + 4
    result = call(
        body, "opening", number, {}, dict(shards, vectors=vectors, tokens=tokens), {},
        {MIXED_NAME + SECOND: MIXED_T[MIXED_NAME]}, saved,
        dict(
            chances=CHANCES, chances_second=CHANCES, gqkv=((3,) + CUBE + (16, HALF), BF),
            rest_one=(CUBE + (64, HALF), BF), rest_two=narrow, rest_three=narrow,
            mixed_t_one=MIXED_T[MIXED_NAME],
        ),
        scratch,
        [dma(copies), dma(copies), dma(46)] + (MAIL_SEMS + [dma(SLOTS + 1)]) * 2,
        dict(lengths=lengths, pads=pads),
    )
    result.gout, result.gback = result.w_out, result.w_back
    return result


MIXED_NAME, CHANCES_NAME = "mixed_t", "chances"


def closing(near, loaded, sources, number):
    rest_slots = [
        scatter_slots(order, *REST[k], True, REST_DOUBLE) for k, order in enumerate(SCATTER_ORDERS[:3])
    ]

    def body(refs, semaphores):
        send, recv, local, send_q, recv_q, send_kv, recv_kv, refs.attend_local = semaphores
        here = place()
        wire = Wire(here, send, recv, local)
        core = wire.core
        refs.round = 0
        mine, yours = pl.ds(2 * core, 2), pl.ds(2 * (1 - core), 2)
        blocks, inner, copies = (EVERY,) * 3, [], []
        for side, ref in enumerate((refs.rest_two, refs.rest_three)):
            low = pl.multiple_of(core * HALF + side * (HALF // 2), HALF // 2)
            here_columns = CUBE_ALL + (EVERY, pl.ds(low, HALF // 2))
            come_columns = CUBE_ALL + (EVERY, side_columns(HALF, side))
            for rows, gradient, come in (
                (pl.ds(0, 64), refs.g_back, refs.come_back),
                (pl.ds(64, 16), refs.g_out, refs.come_out),
            ):
                copies.append(
                    wire.fetch(gradient.at[here_columns], ref.at[(mine,) + blocks + (rows,)])
                )
                copies.append(
                    wire.fetch(come.at[come_columns], ref.at[(yours,) + blocks + (rows,)])
                )
        for k in range(4):
            source = refs.g_in.at[CUBE_ALL + (EVERY, pl.ds(k * HALF, HALF))]
            inner.append(wire.fetch(source, refs.rest_one.at[CUBE_ALL + (pl.ds(16 * k, 16),)]))
        greet(neighbours(here, (1, -1, 2)) + group(here))
        refs.arrive()

        def keep_rest(part):
            def store(value):
                (refs.sums_one, refs.sums_two, refs.sums_six)[part][...] = value

            return store

        rest_arrivals = [
            [getattr(refs, "rest_%d_%d" % (part, k)) for k in range(5)] for part in range(3)
        ]
        rest = [
            (ref, (), SCATTER_ORDERS[part], REST[part][1], rest_arrivals[part], keep_rest(part))
            for part, ref in enumerate((refs.rest_one, refs.rest_two, refs.rest_three))
        ]
        long_stages = ring_scatter(wire, rest[:1], REST_DOUBLE)
        rest_stages = ring_scatter(wire, rest[1:], REST_DOUBLE)
        for copy in inner:
            copy.wait()
        advance(long_stages)
        fetch_chances(refs)
        weights = Weights(refs, wire, (QKV,))

        def keep(part):
            def store(value):
                if part == 3:
                    refs.tiny[...] = value
                else:
                    refs.final[part] = value

            return store

        arrivals = [
            [getattr(refs, "slot_%d_%d" % (part, k)) for k in range(4)] for part in range(4)
        ]
        parts = [
            (refs.gradients, (part,), LAST_ORDERS[part], HALF, arrivals[part], keep(part))
            for part in range(3)
        ]
        parts.append((refs.small_sums, (), SCATTER_ORDERS[3], 0, arrivals[3], keep(3)))
        early_stages = ring_scatter(wire, parts[1:3])
        stages = ring_scatter(wire, parts[:1] + parts[3:])

        def add_gradient(k):
            total = dot(refs.entry_t[...], refs.d_qkv[k]).reshape(CUBE + (16, HALF))
            refs.gradients[k] = bfloat(widen(refs.gradients[k]) + total)

        def between(slot):
            if slot == -1:
                for copy in copies:
                    copy.wait()
                advance(rest_stages)
                turned = refs.entry_later[...].T
                for k in range(3):
                    total = dot(turned, refs.d_qkv_later[k])
                    refs.gradients[k] = bfloat(total).reshape(CUBE + (16, HALF))
                refs.entry_t[...] = refs.entry[...].T
                refs.sums[...] = refs.sums_three[...] + refs.sums_four[...]
                refs.sums_in[...] = refs.in_three[...] + refs.in_four[...]
            elif slot == 0:
                advance(rest_stages)
            elif slot == 1:
                advance(long_stages)
            elif slot == SLOTS:
                advance(long_stages)
            elif slot == SLOTS + 1:
                turn_keys_values(refs)
                add_gradient(1)
                add_gradient(2)
                advance(early_stages)
                advance(rest_stages)

        prepare_back(refs)
        attend_back_steps(
            refs, Mail(here, send_q, recv_q), Mail(here, send_kv, recv_kv), between
        )
        turn_queries(refs)
        add_half(refs, wire, B_QUERY, row_sum(refs.d_qkv[0]))
        add_half(refs, wire, B_VALUE, row_sum(refs.d_qkv[2]))
        swaps = [wire.swap(refs.sums, refs.sums_come), wire.swap(refs.sums_in, refs.in_come)]
        add_gradient(0)
        for copy in swaps:
            copy.wait()
        both = refs.sums[...] + refs.sums_come[...]
        both_in = refs.sums_in[...] + refs.in_come[...]
        for s in range(8):
            pieces = [both[:, 128 * s : 128 * s + 128]]
            for j in range(4):
                low = HALF * s + 128 * j
                pieces.append(both_in[:, low : low + 128])
            pieces.append(jnp.zeros((4, 128), F32))
            tile = bfloat(jnp.concatenate(pieces, axis=0))
            for x_hi in range(2):
                for z in range(4):
                    refs.small_sums[s // 2, s % 2, x_hi, z] = tile
        for ring in (stages, early_stages, stages, long_stages, rest_stages):
            advance(ring)
        refs.d_tokens[...] = bfloat(part_back_project(refs, wire, weights))
        for ring in (early_stages, stages, rest_stages, long_stages, early_stages, stages):
            advance(ring)
        for ring in (rest_stages, long_stages):
            advance(ring)
        for ring in (rest_stages, long_stages, early_stages, stages):
            for _ in ring:
                pass

        def finish(own):
            def both(low, count):
                span = slice(low, low + count)
                return jnp.concatenate([refs.sums_two[span, :], refs.sums_six[span, :]], axis=1)

            rows = [refs.final[k, 8 * own : 8 * own + 8, :] for k in range(3)]
            rows.append(both(64 + 8 * own, 8))
            for k in range(4):
                rows.append(refs.sums_one[16 * k + 8 * own : 16 * k + 8 * own + 8, :])
            rows.append(both(32 * own, 32))
            return jnp.concatenate(rows, axis=0)

        @pl.when(core == 0)
        def _():
            refs.leaving[...] = finish(1)
            refs.landed[0] = finish(0)

        @pl.when(core == 1)
        def _():
            refs.leaving[...] = finish(0)
            refs.landed[1] = finish(1)

        wire.swap(refs.leaving, refs.landed.at[core]).wait()
    few = ((8, D), F32)
    scratch = dict(
        BACK_SCRATCH, **BACK_OUTPUTS, outgoing=((1, ROWS, D), BF), incoming=((1, ROWS, D), BF),
        kept=ROW_F32, entry_t=((D, CHIP_ROWS), BF), d_qkv=((3, CHIP_ROWS, HALF), BF), sums=few, sums_in=((1, FF), F32), sums_come=few,
        in_come=((1, FF), F32), gradients=((3,) + CUBE + (16, HALF), BF),
        small_sums=(CUBE + (16, 128), BF), final=((3, 16, HALF), F32),
        leaving=((96, HALF), F32), sums_one=(REST[0], F32), sums_two=(REST[1], F32),
        sums_six=(REST[2], F32), rest_one=(CUBE + REST[0], BF), rest_two=(CUBE + REST[1], BF),
        rest_three=(CUBE + REST[2], BF),
    )
    scratch.update(WEIGHT_SHAPES[QKV])
    for part in range(4):
        slots = scatter_slots((*LAST_ORDERS, SCATTER_ORDERS[3])[part], 16, HALF if part < 3 else 128, part < 3)
        for k in range(4):
            scratch["slot_%d_%d" % (part, k)] = slots[k]
    for part in range(3):
        for k in range(5):
            scratch["rest_%d_%d" % (part, k)] = rest_slots[part][k]
    copies = 7 * sum(SCATTER_COPIES) + 3 * 3 + 8
    return call(
        body, "closing", number, near, loaded, sources,
        dict(
            d_tokens=((ROWS, D), BF), landed=((2, 96, HALF), F32), tiny=((16, 128), F32),
        ),
        {}, {}, scratch,
        [dma(copies), dma(copies), dma(13)] + MAIL_SEMS + MAIL_SEMS + [dma(SLOTS)],
    )


def unpack_kernel(
    result, d_tokens, landed, tiny, o_result, o_tokens, o_query, o_key, o_value, o_out, o_in, o_back,
    *o_vectors,
):
    o_result[...] = result[...]
    o_tokens[...] = d_tokens[...]
    for column in (0, 1):
        span = columns(column)
        for piece, ref in enumerate((o_query, o_key, o_value, o_out)):
            ref[:, span] = landed[column, 8 * piece : 8 * piece + 8, :]
        for chunk in range(4):
            o_in[:, columns(4 * column + chunk)] = landed[
                column, 32 + 8 * chunk : 40 + 8 * chunk, :
            ]
        o_back[:, span] = landed[column, 64:96, :]
    tok = lax.axis_index("tok")
    eight = pltpu.roll(tiny[0:8, :], lax.rem(128 - tok * 8, 128), 1)
    for k in range(8):
        o_vectors[k][...] = eight[k : k + 1, 0:8]
    wide = tiny[8:9, :]
    for k in range(1, 4):
        wide = jnp.where(lax.div(tok, 4) == k, tiny[8 + k : 9 + k, :], wide)
    wide = pltpu.roll(wide, lax.rem(128 - lax.rem(tok, 4) * 32, 128), 1)
    o_vectors[8][...] = wide[:, 0:32]


def unpack(result, d_tokens, landed, tiny):
    vmem = pl.BlockSpec(memory_space=pltpu.VMEM)
    few = ((8, D), F32)
    specs = (
        ((ROWS, D), BF), ((ROWS, D), BF), few, few, few, few, ((8, FF), F32), ((32, D), F32),
    ) + (((1, 8), F32),) * 8 + (((1, 32), F32),)
    return pl.pallas_call(
        unpack_kernel,
        out_shape=tuple(jax.ShapeDtypeStruct(*spec) for spec in specs),
        in_specs=[vmem] * 4,
        out_specs=(vmem,) * len(specs),
        name="unpack",
        compiler_params=pltpu.CompilerParams(vmem_limit_bytes=58 * 2**20),
    )(result, d_tokens, landed, tiny)


def on_device(
    tokens, cotangent, doc_lengths, pad_counts, w_query, b_query, w_key, w_value, b_value, w_out,
    b_out, gain_attn, shift_attn, w_in, b_in, w_back, b_back, gain_ffn, shift_ffn,
):
    vectors = jnp.concatenate(
        [
            b_query, b_value, b_out, gain_attn, shift_attn, b_back, gain_ffn, shift_ffn, b_in,
            jnp.zeros((32,), BF),
        ]
    )
    one = opening(
        doc_lengths, pad_counts,
        dict(
            s_query=w_query, s_key=w_key, s_value=w_value, s_out=w_out, s_in=w_in, s_back=w_back
        ),
        widen(vectors)[None], tokens, 0,
    )
    three = dense(
        (POST, BACK_DENSE, GRADIENTS, ATTEND_BACK), 4, one,
        dict(mixed_t_in=one.mixed_t_second, hidden=one.result, cotangent=cotangent),
        dict(
            qkv=one.qkv_second, mixed_head=one.mixed_head_second, inverse=one.inverse_second,
        ),
        dict(result=((ROWS, D), BF)),
        (
            "normed_one", "factor_one", "entry_two", "active", "slope", "normed_two",
            "factor_two", "d_branch", "d_before", "d_attn", "d_mixed",
        ),
        dict(chances=one.chances_second),
    )
    four = dense(
        (BACK_PROJECT, BACK_DENSE, GRADIENTS), 6, one,
        dict(
            d_q_t=three.d_q_t, d_kv_t=three.d_kv_t, d_inner=three.d_inner_out,
            normed_one=one.normed_one, factor_one=one.factor_one, normed_two=one.normed_two,
            factor_two=one.factor_two, slope=one.slope,
        ),
        dict(entry_two=one.entry_two, active=one.active, mixed_t_in=one.mixed_t_one),
        {}, ("d_branch", "d_before", "d_attn"),
        added=dict(g_in=three.g_in, g_back=three.g_back, g_out=three.g_out),
    )
    last = closing(
        {},
        dict(
            d_mixed=four.d_mixed,
            qkv=one.qkv, mixed_head=one.mixed_head, inverse=one.inverse, d_inner=four.d_inner_out,
            entry=one.entry, entry_later=one.entry_second, d_qkv_later=four.d_qkv, sums_three=three.sums,
            sums_four=four.sums, in_three=three.sums_in, in_four=four.sums_in,
        ),
        dict(
            chances=one.chances, gqkv=one.gqkv, g_in=four.g_in, g_back=four.g_back, g_out=four.g_out,
            come_back=four.come_back, come_out=four.come_out,
        ),
        8,
    )
    result, d_tokens, g_query, g_key, g_value, g_out, g_in, g_back, *lines = unpack(
        three.result, last.d_tokens, last.landed, last.tiny
    )
    (
        g_b_query, g_b_value, g_b_out, g_gain_attn, g_shift_attn, g_b_back, g_gain_ffn, g_shift_ffn,
    ) = [lines[k].reshape(8) for k in range(8)]
    return (
        result, d_tokens, g_query, g_b_query, g_key, g_value, g_b_value, g_out, g_b_out, g_gain_attn,
        g_shift_attn, g_in, lines[8].reshape(32), g_back, g_b_back, g_gain_ffn, g_shift_ffn,
    )


def solution(mesh):
    both = ("seq", "tok")
    rows, vector = P(both, None), P(both)
    ins = (
        rows, rows, P("seq", None), P("seq"), rows, vector, rows, rows, vector, rows, vector, vector,
        vector, rows, vector, rows, vector, vector, vector,
    )
    outs = (
        rows, rows, rows, vector, rows, rows, vector, rows, vector, vector, vector, rows, vector,
        rows, vector, vector, vector,
    )
    return jax.shard_map(on_device, mesh=mesh, in_specs=ins, out_specs=outs, check_vma=False)
```
